128 devices in a mesh: dp: 32 (over y, x, z_lo), tensor: 4 (over z_hi, core).
Axes of the slice: x: 4, y: 4, z: 4 (z_hi: 2, z_lo: 2; z = z_hi * 2 + z_lo), core: 2. Of those that a mesh axis runs over, the one named last changes fastest.
Arguments:
- inputs: float32 [100352, 512], P(('dp', 'tensor')), may hold values from -6 to 6
- w_qkv: bfloat16 [2, 512, 3, 512], P(None, 'dp', None, 'tensor'), may hold values from -0.25 to 0.25
- w_proj: bfloat16 [2, 512, 512], P(None, ('tensor', 'dp')), may hold values from -0.75 to 0.75
- w_up: bfloat16 [2, 512, 2048], P(None, 'dp', 'tensor'), may hold values from -0.25 to 0.25
- w_down: bfloat16 [2, 2048, 512], P(None, ('tensor', 'dp')), may hold values from -0.1875 to 0.1875
- ln_gain: float32 [2, 2, 512], P(None, None, ('dp', 'tensor')), may hold values from 0.25 to 1.75
- ln_shift: float32 [2, 2, 512], P(None, None, ('dp', 'tensor')), may hold values from -1.5 to 1.5
- tables: float32 [2, 169, 16], P(None, None, 'tensor'), may hold values from -4 to 4
- region: int32 [196], replicated, may hold values from 0 to 3
- rel_index: int32 [49, 49], replicated, may hold values from 0 to 168, as said below
- cotangent: float32 [100352, 512], P(('dp', 'tensor')), may hold values from -6 to 6
Outputs:
- out: float32 [100352, 512], P(('dp', 'tensor'))
- grad_inputs: float32 [100352, 512], P(('dp', 'tensor'))
- grad_qkv: float32 [2, 512, 3, 512], P(None, 'dp', None, 'tensor')
- grad_proj: float32 [2, 512, 512], P(None, ('tensor', 'dp'))
- grad_up: float32 [2, 512, 2048], P(None, 'dp', 'tensor')
- grad_down: float32 [2, 2048, 512], P(None, ('tensor', 'dp'))
- grad_gain: float32 [2, 2, 512], P(None, None, ('dp', 'tensor'))
- grad_shift: float32 [2, 2, 512], P(None, None, ('dp', 'tensor'))
- grad_tables: float32 [2, 169, 16], P(None, None, 'tensor')
The draws below stay inside these ranges and needn't reach their ends.
Inputs may be any that keep to these rules, and one draw needn't show every extreme that they name: In blocks with shifted windows a query attends only to keys of its window whose region equals its own. `rel_index`: two query-key pairs whose offsets between their window positions are equal name the same row; different offsets name different rows.
All inputs are finite; a program needn't handle non-finite values.
Results may differ from the reference program's by a relative error of at most 0.033.
Values may be sent and summed in bfloat16 or wider, within the bound.
A program may use at most 256 MiB of HBM per device.

```python
import jax
import jax.numpy as jnp
from jax import lax

D = 512
HEADS = 16
HEAD = 32
FF = 2048
WINDOW = 7
SIDE = 14
SHIFT = 3
LAYERS = 2
IMG_DEV = 16
TABLE = 169
TOKENS = 100352


def draw_rel_index(key, part):
    key = jax.random.fold_in(key, 11)
    cells = WINDOW * WINDOW
    place = jnp.arange(cells, dtype=jnp.int32)
    row_of = place // WINDOW
    col_of = place % WINDOW
    span = 2 * WINDOW - 1
    offset = (row_of[:, None] - row_of[None, :] + WINDOW - 1) * span + (col_of[:, None] - col_of[None, :] + WINDOW - 1)
    labels = jax.random.permutation(key, span * span).astype(jnp.int32)
    return labels[offset].astype(jnp.int32)


def set_ends(entries, rng, low, top_value):
    index_at = [jax.random.randint(jax.random.fold_in(rng, axis), (), 0, length) for axis, length in enumerate(entries.shape)]
    widest = entries.shape.index(max(entries.shape))
    next_to = index_at[:widest] + [(index_at[widest] + 1) % entries.shape[widest]] + index_at[widest + 1:]
    return entries.at[tuple(index_at)].set(low).at[tuple(next_to)].set(top_value)


def block_scale(key, shape, split, low, top_value):
    def one(dim, parts):
        draws = jax.random.uniform(jax.random.fold_in(jax.random.fold_in(key, 6), dim), (parts,), jnp.float32, low / len(split), top_value / len(split))
        return jnp.repeat(jnp.exp(draws), shape[dim] // parts).reshape((-1,) + (1,) * (len(shape) - dim - 1))

    factor_of = one(*split[0])
    for cut in split[1:]:
        factor_of = factor_of * one(*cut)
    return factor_of


def gaussian(rng, shape, scale, reach, pieces=(), kind=jnp.bfloat16):
    level = block_scale(rng, shape, pieces, -0.22, 0.18) if pieces else 1.0
    drawn = jax.random.normal(rng, shape, jnp.float32) * scale * level
    return jnp.minimum(jnp.maximum(drawn, -reach), reach).astype(kind)


def setup_inputs(seed: int = 0) -> dict:
    key_list = jax.random.split(jax.random.key(seed), 12)
    inputs = gaussian(key_list[0], (TOKENS, D), 1.0, 6.0, ((0, 128),), jnp.float32)
    w_qkv = gaussian(key_list[1], (LAYERS, D, 3, D), D ** -0.5, 0.25, ((1, 32), (3, 4)))
    w_proj = gaussian(key_list[2], (LAYERS, D, D), (D // 8) ** -0.5, 0.75, ((1, 128),))
    w_up = gaussian(key_list[3], (LAYERS, D, FF), D ** -0.5, 0.25, ((1, 32), (2, 4)))
    w_down = gaussian(key_list[4], (LAYERS, FF, D), (FF // 2) ** -0.5, 0.1875, ((1, 128),))
    ln_gain = jnp.clip(1.0 + 0.15 * jax.random.normal(key_list[5], (LAYERS, 2, D), jnp.float32), 0.25, 1.75)
    ln_shift = gaussian(key_list[6], (LAYERS, 2, D), 0.3, 1.5, ((2, 128),), jnp.float32)
    tables = gaussian(key_list[7], (LAYERS, TABLE, HEADS), 1.0, 4.0, ((2, 4),), jnp.float32)
    region = set_ends(jax.random.randint(key_list[8], (SIDE * SIDE,), 0, 4), jax.random.fold_in(key_list[8], 1), 0, 3).astype(jnp.int32)
    rel_index = draw_rel_index(jax.random.fold_in(key_list[11], 71), 0)
    cotangent = gaussian(key_list[10], (TOKENS, D), 1.0, 6.0, ((0, 128),), jnp.float32)
    return {"inputs": inputs, "w_qkv": w_qkv, "w_proj": w_proj, "w_up": w_up, "w_down": w_down, "ln_gain": ln_gain, "ln_shift": ln_shift, "tables": tables, "region": region, "rel_index": rel_index, "cotangent": cotangent}


@jax.custom_vjp
def low(v):
    return lax.optimization_barrier(v.astype(jnp.bfloat16)).astype(jnp.float32)

@jax.custom_vjp
def low_back(v):
    return v

def low_keep(v):
    return (low(v), None)

def low_pass(kept, grad):
    return (grad,)

def back_keep(v):
    return (v, None)

def back_low(kept, grad):
    return (low(grad),)
low.defvjp(low_keep, low_pass)
low_back.defvjp(back_keep, back_low)

def layer_norm(values, gain, shift):
    mean = lax.optimization_barrier(jnp.mean(values, axis=-1, keepdims=True))
    centered = values - mean
    spread = lax.optimization_barrier(jnp.mean(centered * centered, axis=-1, keepdims=True))
    return centered * lax.rsqrt(spread + 1e-05) * gain + shift

def to_windows(field):
    count, side, _, width = field.shape
    per = side // WINDOW
    field = field.reshape(count, per, WINDOW, per, WINDOW, width).transpose(0, 1, 3, 2, 4, 5)
    return field.reshape(count * per * per, WINDOW * WINDOW, width)

def from_windows(blocks, count):
    per = SIDE // WINDOW
    width = blocks.shape[-1]
    blocks = blocks.reshape(count, per, per, WINDOW, WINDOW, width).transpose(0, 1, 3, 2, 4, 5)
    return blocks.reshape(count, SIDE, SIDE, width)

def window_rows(rows, shifted):
    count = rows.shape[0] // (SIDE * SIDE)
    field = rows.reshape(count, SIDE, SIDE, rows.shape[-1])
    if shifted:
        field = jnp.roll(field, (-SHIFT, -SHIFT), axis=(1, 2))
    blocks = to_windows(field)
    return blocks.reshape(blocks.shape[0], WINDOW * WINDOW, HEADS, HEAD)

def unwindow_rows(blocks, shifted):
    per = SIDE // WINDOW
    count = blocks.shape[0] // (per * per)
    field = from_windows(blocks.reshape(blocks.shape[0], WINDOW * WINDOW, -1), count)
    if shifted:
        field = jnp.roll(field, (SHIFT, SHIFT), axis=(1, 2))
    return field.reshape(count * SIDE * SIDE, -1)

def attend_group(item, bias, mask_add, shifted):
    q_win = window_rows(item[0], shifted)
    k_win = window_rows(item[1], shifted)
    v_win = window_rows(item[2], shifted)
    raw = jnp.einsum('wqhc,wkhc->whqk', q_win, k_win, precision=lax.Precision.HIGHEST) * HEAD ** (-0.5)
    raw = raw + bias[None]
    if shifted:
        count = raw.shape[0] // mask_add.shape[0]
        raw = raw + jnp.tile(mask_add, (count, 1, 1))[:, None]
    raw = low_back(raw)
    probs = jax.nn.softmax(raw, axis=-1)
    mixed = jnp.einsum('whqk,wkhc->wqhc', low(probs), v_win, precision=lax.Precision.HIGHEST)
    return unwindow_rows(mixed, shifted)

def block(x, wq, wp, wu, wd, gain, shift, table, rel_index, mask_add, shifted):
    normed = low(layer_norm(x, gain[0], shift[0]))
    qkv = jnp.einsum('td,dsc->tsc', normed, wq, precision=lax.Precision.HIGHEST)
    query = low(low_back(qkv[:, 0]))
    keys = low(low_back(qkv[:, 1]))
    values = low(low_back(qkv[:, 2]))
    bias = table[rel_index].transpose(2, 0, 1)
    group_rows = IMG_DEV * SIDE * SIDE
    stacked = jnp.stack([query, keys, values]).reshape(3, -1, group_rows, D).transpose(1, 0, 2, 3)
    attend = jax.checkpoint(lambda item: attend_group(item, bias, mask_add, shifted))
    attended = lax.map(attend, stacked).reshape(-1, D)
    attended = low(low_back(attended))
    middle = x + low_back(jnp.dot(attended, wp, precision=lax.Precision.HIGHEST))
    normed2 = low(layer_norm(middle, gain[1], shift[1]))
    hidden = low_back(jnp.dot(normed2, wu, precision=lax.Precision.HIGHEST))
    active = low(jax.nn.gelu(hidden, approximate=True))
    return middle + low_back(jnp.dot(active, wd, precision=lax.Precision.HIGHEST))

def reference(inputs, w_qkv, w_proj, w_up, w_down, ln_gain, ln_shift, tables, region, rel_index, cotangent):
    region_win = to_windows(region.reshape(1, SIDE, SIDE, 1))[..., 0]
    same = region_win[:, :, None] == region_win[:, None, :]
    mask_add = jnp.where(same, jnp.float32(0.0), jnp.float32(-1000000000.0)).astype(jnp.float32)

    def forward(x, wq, wp, wu, wd, gains, shifts, tabs):
        for layer in range(LAYERS):
            x = block(x, wq[layer], wp[layer], wu[layer], wd[layer], gains[layer], shifts[layer], tabs[layer], rel_index, mask_add, layer % 2 == 1)
        return x
    params = (inputs, w_qkv.astype(jnp.float32), w_proj.astype(jnp.float32), w_up.astype(jnp.float32), w_down.astype(jnp.float32), ln_gain, ln_shift, tables)
    out, pullback = jax.vjp(forward, *params)
    grads = pullback(cotangent)
    return (out, grads[0], grads[1], grads[2], grads[3], grads[4], grads[5], grads[6], grads[7])
```

```python
import functools
import jax
import jax.numpy as jnp
from jax import lax
from jax.experimental import pallas as pl
from jax.experimental.pallas import tpu as pltpu
from jax.sharding import PartitionSpec as P

MESH = pl.DeviceIdType.MESH
ORDERS = (("x", "y", "z"), ("y", "z", "x"), ("z", "x", "y"))


def coords():
    dp, tp = lax.axis_index("dp"), lax.axis_index("tensor")
    return {
        "y": dp // 8,
        "x": (dp // 2) % 4,
        "z": (tp // 2) * 2 + dp % 2,
        "c": tp % 2,
    }


def device(at):
    return (at["y"] * 8 + at["x"] * 2 + at["z"] % 2, (at["z"] // 2) * 2 + at["c"])


def moved(at, axis, step):
    size = 2 if axis == "c" else 4
    return device({**at, axis: (at[axis] + step) % size})


NEIGHBOURS = (("x", 1), ("x", 3), ("y", 1), ("y", 3), ("z", 1), ("z", 3), ("c", 1))


def enter(at, peers=NEIGHBOURS):
    barrier = pltpu.get_barrier_semaphore()
    for axis, step in peers:
        pl.semaphore_signal(barrier, inc=1, device_id=moved(at, axis, step), device_id_type=MESH)
    pl.semaphore_wait(barrier, len(peers))


PEERS = NEIGHBOURS + (("x", 2), ("y", 2), ("z", 2))
COPIES = 224


class Copier:
    def __init__(self, at, send, recv):
        self.at, self.send, self.recv, self.made = at, send, recv, []

    def __call__(self, src, dst, axis, step):
        slot = len(self.made)
        copy = pltpu.make_async_remote_copy(
            src_ref=src,
            dst_ref=dst,
            send_sem=self.send.at[slot],
            recv_sem=self.recv.at[slot],
            device_id=moved(self.at, axis, step),
            device_id_type=MESH,
        )
        copy.start()
        self.made.append(copy)
        return copy

    def finish(self):
        for copy in self.made:
            copy.wait_send()


def ring_gather(copy, axis, index, slot):
    left, right = (index + 3) % 4, (index + 1) % 4
    held = {}

    def first():
        held["r"] = copy(slot(index), slot(index), axis, 1)
        held["l"] = copy(slot(index), slot(index), axis, 3)

    def second():
        held["r"].wait_recv()
        held["r2"] = copy(slot(left).at[0:2], slot(left).at[0:2], axis, 1)
        held["l"].wait_recv()
        held["l2"] = copy(slot(right).at[2:4], slot(right).at[2:4], axis, 3)

    def third():
        held["r2"].wait_recv()
        held["l2"].wait_recv()

    return first, second, third


def gather_kernel(a, b, c, d, ga, gb, gc, gd, send, recv, local):
    at = coords()
    core = at["c"]
    copy = Copier(at, send, recv)
    own = []

    def place(src, dst):
        put = pltpu.make_async_copy(src, dst, local.at[len(own)])
        put.start()
        own.append(put)

    place(d, gd.at[core, at["z"], at["y"], at["x"]])
    for layer in range(2):
        for order, src, dst in zip(ORDERS, (a, b, c), (ga, gb, gc)):
            i1, i2, i3 = (at[axis] for axis in order)
            place(src.at[layer], dst.at[layer, core, i3, i2, i1])
    enter(at, PEERS)
    for put in own:
        put.wait()

    def stages(layer):
        plans = []
        for order, dst in zip(ORDERS, (ga, gb, gc)):
            i1, i2, i3 = (at[axis] for axis in order)
            whole = dst.at[layer, core]
            plans.append(
                (
                    ring_gather(copy, order[0], i1, lambda j, w=whole, p=i3, q=i2: w.at[p, q, j]),
                    ring_gather(copy, order[1], i2, lambda j, w=whole, p=i3: w.at[p, j]),
                    ring_gather(copy, order[2], i3, lambda j, w=whole: w.at[j]),
                    whole,
                    i3,
                )
            )
        across = []

        def pass_on(ref):
            across.append(copy(ref, ref, "c", 1))

        def one(phase, step):
            def run():
                for plan in plans:
                    plan[phase][step]()
                    if phase == 2:
                        whole, i3 = plan[3], plan[4]
                        if step == 0:
                            pass_on(whole.at[i3])
                        elif step == 1:
                            pass_on(whole.at[(i3 + 3) % 4])
                            pass_on(whole.at[(i3 + 1) % 4])
                        else:
                            pass_on(whole.at[(i3 + 2) % 4])

            return run

        def last():
            for sent in across:
                sent.wait_recv()

        return [one(phase, step) for phase in range(3) for step in range(3)] + [last]

    def small():
        slots = (
            ("x", lambda: gd.at[core, at["z"], at["y"], at["x"]]),
            ("y", lambda: gd.at[core, at["z"], at["y"]]),
            ("z", lambda: gd.at[core, at["z"]]),
            ("c", lambda: gd.at[core]),
        )
        out = []
        for axis, ref in slots:

            def start(axis=axis, ref=ref):
                steps = (1,) if axis == "c" else (1, 2, 3)
                out.append([copy(ref(), ref(), axis, step) for step in steps])

            def end():
                for sent in out[-1]:
                    sent.wait_recv()

            yield start
            yield end

    low, high, tiny = stages(0), stages(1), list(small())
    for step in range(12):
        if step < len(low):
            low[step]()
        if step < len(tiny):
            tiny[step]()
        if step >= 2:
            high[step - 2]()
    copy.finish()


def gather_all(a, b, c, d):
    shape = jax.ShapeDtypeStruct((2, 2, 4, 4, 4, 4, 16, 128), jnp.bfloat16)
    return pl.pallas_call(
        gather_kernel,
        out_shape=(shape, shape, shape, jax.ShapeDtypeStruct((2, 4, 4, 4, 8, 128), jnp.float32)),
        in_specs=[pl.BlockSpec(memory_space=pl.ANY)] * 4,
        out_specs=[pl.BlockSpec(memory_space=pl.ANY)] * 4,
        scratch_shapes=[
            pltpu.SemaphoreType.DMA((COPIES,)),
            pltpu.SemaphoreType.DMA((COPIES,)),
            pltpu.SemaphoreType.DMA((8,)),
        ],
        compiler_params=pltpu.CompilerParams(collective_id=0, has_side_effects=True),
        name="gather_weights",
    )(a, b, c, d)


def add_into(dst, *terms):
    lead = dst.shape[:-3]
    count = 1
    for size in lead:
        count *= size

    def body(n, carry):
        index = []
        for size in reversed(lead):
            index.append(n % size)
            n = n // size
        index = tuple(reversed(index))
        total = dst[index].astype(jnp.float32)
        for term in terms:
            total = total + term[index].astype(jnp.float32)
        dst[index] = total.astype(dst.dtype)
        return carry

    lax.fori_loop(0, count, body, 0)


def ring_scatter(copy, axis, index, slot, half_r, half_l, full_r, full_l):
    left, right, far = (index + 3) % 4, (index + 1) % 4, (index + 2) % 4
    held = {}

    def first():
        held["r"] = copy(slot(far).at[0:2], half_r, axis, 1)
        held["l"] = copy(slot(far).at[2:4], half_l, axis, 3)

    def second():
        held["r"].wait_recv()
        add_into(slot(right).at[0:2], half_r)
        held["r2"] = copy(slot(right), full_r, axis, 1)
        held["l"].wait_recv()
        add_into(slot(left).at[2:4], half_l)
        held["l2"] = copy(slot(left), full_l, axis, 3)

    def third():
        held["r2"].wait_recv()
        held["l2"].wait_recv()
        add_into(slot(index), full_r, full_l)

    return first, second, third


def scatter_kernel(ga, gb, gc, d, oa, ob, oc, od, sums, landed, h3, f3, h2, f2, h1, f1, dsum, dland, send, recv, local):
    at = coords()
    core = at["c"]
    copy = Copier(at, send, recv)
    puts = {}
    for layer in (1, 0):
        for family, src in enumerate((ga, gb, gc)):
            put = pltpu.make_async_copy(src.at[layer, core], sums.at[layer, family], local.at[layer * 3 + family])
            put.start()
            puts[layer, family] = put
    enter(at, PEERS)
    plans = {0: [], 1: []}
    for layer in (1, 0):
        for family, src in enumerate((ga, gb, gc)):
            order = ORDERS[family]
            i1, i2, i3 = (at[axis] for axis in order)
            whole = sums.at[layer, family]
            put = puts[layer, family]
            land = landed.at[layer, family]

            def core_first(src=src, land=land, layer=layer, held=None):
                return copy(src.at[layer, 1 - core], land, "c", 1)

            plans[layer].append(
                (
                    core_first,
                    put,
                    whole,
                    land,
                    ring_scatter(
                        copy, order[2], i3, lambda j, w=whole: w.at[j],
                        *(h3.at[layer, family, k] for k in range(2)), *(f3.at[layer, family, k] for k in range(2)),
                    ),
                    ring_scatter(
                        copy, order[1], i2, lambda j, w=whole, p=i3: w.at[p, j],
                        *(h2.at[layer, family, k] for k in range(2)), *(f2.at[layer, family, k] for k in range(2)),
                    ),
                    ring_scatter(
                        copy, order[0], i1, lambda j, w=whole, p=i3, q=i2: w.at[p, q, j],
                        *(h1.at[layer, family, k] for k in range(2)), *(f1.at[layer, family, k] for k in range(2)),
                    ),
                    whole.at[i3, i2, i1],
                )
            )

    def stages(layer):
        crossed = []

        def begin():
            for plan in plans[layer]:
                crossed.append(plan[0]())

        def joined():
            for plan, sent in zip(plans[layer], crossed):
                plan[1].wait()
                sent.wait_recv()
                add_into(plan[2], plan[3])

        def one(phase, step):
            def run():
                for plan in plans[layer]:
                    plan[4 + phase][step]()

            return run

        def last():
            for plan, out in zip(plans[layer], (oa, ob, oc)):
                out[layer] = plan[7][...].astype(jnp.float32)

        return [begin, joined] + [one(phase, step) for phase in range(3) for step in range(3)] + [last]

    dsum[...] = d[...]
    turns = []
    for phase, (axis, size) in enumerate((("c", 2), ("x", 4), ("y", 4), ("z", 4))):
        sent = []

        def start(axis=axis, size=size, phase=phase, sent=sent):
            mine = at[axis]
            dland[phase, mine] = dsum[...]
            for step in range(1, size):
                sent.append(copy(dland.at[phase, mine], dland.at[phase, mine], axis, step))

        def end(size=size, phase=phase, sent=sent):
            for one in sent:
                one.wait_recv()
            total = dland[phase, 0]
            for k in range(1, size):
                total = total + dland[phase, k]
            dsum[...] = total

        turns += [start, end]

    high, low = stages(1), stages(0)
    for step in range(14):
        if step < len(high):
            high[step]()
        if step < len(turns):
            turns[step]()
        if step >= 2:
            low[step - 2]()
    od[...] = dsum[...]
    copy.finish()


def scatter_all(ga, gb, gc, d):
    out = jax.ShapeDtypeStruct((2, 4, 16, 128), jnp.float32)
    bf = jnp.bfloat16
    return pl.pallas_call(
        scatter_kernel,
        out_shape=(out, out, out, jax.ShapeDtypeStruct(d.shape, jnp.float32)),
        in_specs=[pl.BlockSpec(memory_space=pl.ANY)] * 3 + [pl.BlockSpec(memory_space=pltpu.VMEM)],
        out_specs=[pl.BlockSpec(memory_space=pltpu.VMEM)] * 4,
        scratch_shapes=[
            pltpu.VMEM((2, 3, 4, 4, 4, 4, 16, 128), bf),
            pltpu.VMEM((2, 3, 4, 4, 4, 4, 16, 128), bf),
            pltpu.VMEM((2, 3, 2, 2, 4, 4, 16, 128), bf),
            pltpu.VMEM((2, 3, 2, 4, 4, 4, 16, 128), bf),
            pltpu.VMEM((2, 3, 2, 2, 4, 16, 128), bf),
            pltpu.VMEM((2, 3, 2, 4, 4, 16, 128), bf),
            pltpu.VMEM((2, 3, 2, 2, 16, 128), bf),
            pltpu.VMEM((2, 3, 2, 4, 16, 128), bf),
            pltpu.VMEM(d.shape, jnp.float32),
            pltpu.VMEM((4, 4) + d.shape, jnp.float32),
            pltpu.SemaphoreType.DMA((COPIES,)),
            pltpu.SemaphoreType.DMA((COPIES,)),
            pltpu.SemaphoreType.DMA((8,)),
        ],
        compiler_params=pltpu.CompilerParams(
            collective_id=1, has_side_effects=True, vmem_limit_bytes=48 * 2**20
        ),
        name="scatter_grads",
    )(ga, gb, gc, d)


HEAD = 32
WINDOW = 7
SIDE = 14
SHIFT = 3


EPS = 1e-05


def normalize(values, gain, shift):
    mean = jnp.mean(values, axis=-1, keepdims=True)
    centered = values - mean
    spread = jnp.mean(centered * centered, axis=-1, keepdims=True)
    return centered * lax.rsqrt(spread + EPS) * gain + shift


def gelu_tanh(values):
    return jax.nn.gelu(values, approximate=True)


def to_windows(field):
    count, side, _, width = field.shape
    per = side // WINDOW
    field = field.reshape(count, per, WINDOW, per, WINDOW, width).transpose(0, 1, 3, 2, 4, 5)
    return field.reshape(count * per * per, WINDOW * WINDOW, width)


def from_windows(blocks, count):
    per = SIDE // WINDOW
    width = blocks.shape[-1]
    blocks = blocks.reshape(count, per, per, WINDOW, WINDOW, width).transpose(0, 1, 3, 2, 4, 5)
    return blocks.reshape(count, SIDE, SIDE, width)


def window_rows(rows, shifted):
    count = rows.shape[0] // (SIDE * SIDE)
    field = rows.reshape(count, SIDE, SIDE, rows.shape[-1])
    if shifted:
        field = jnp.roll(field, (-SHIFT, -SHIFT), axis=(1, 2))
    blocks = to_windows(field)
    return blocks.reshape(blocks.shape[0], WINDOW * WINDOW, rows.shape[-1] // HEAD, HEAD)


def unwindow_rows(blocks, shifted):
    per = SIDE // WINDOW
    count = blocks.shape[0] // (per * per)
    field = from_windows(blocks.reshape(blocks.shape[0], WINDOW * WINDOW, -1), count)
    if shifted:
        field = jnp.roll(field, (SHIFT, SHIFT), axis=(1, 2))
    return field.reshape(count * SIDE * SIDE, -1)


def scores_of(q_win, k_win, bias, mask_add, shifted):
    raw = jnp.einsum(
        "wqhc,wkhc->whqk", q_win, k_win, preferred_element_type=jnp.float32
    ) * HEAD ** (-0.5)
    raw = raw + bias[None]
    if shifted:
        count = raw.shape[0] // mask_add.shape[0]
        raw = raw + jnp.tile(mask_add, (count, 1, 1))[:, None]
    return raw


def gather_rows(values):
    return values


def sum_rows(term, rows):
    return term(0, rows)


gather_grads, sum_grads = gather_rows, sum_rows


def forward_layer(state, weights, gain, shift, bias, mask_add, shifted):
    w_qkv, w_proj, w_up, w_down = weights
    rows = state.shape[0]
    normed_all = gather_rows(normalize(state, gain[0], shift[0]).astype(jnp.bfloat16))
    qkv = jnp.einsum("td,dsc->tsc", normed_all, w_qkv, preferred_element_type=jnp.float32).astype(
        jnp.bfloat16
    )
    q_win = window_rows(qkv[:, 0], shifted)
    k_win = window_rows(qkv[:, 1], shifted)
    v_win = window_rows(qkv[:, 2], shifted)
    raw = scores_of(q_win, k_win, bias, mask_add, shifted)
    top = jnp.max(raw, axis=-1, keepdims=True)
    expd = jnp.exp(raw - top)
    total = jnp.sum(expd, axis=-1, keepdims=True)
    probs = expd / total
    log_total = top[..., 0] + jnp.log(total[..., 0])
    mixed = jnp.einsum(
        "whqk,wkhc->wqhc", probs.astype(jnp.bfloat16), v_win, preferred_element_type=jnp.float32
    )
    attended = unwindow_rows(mixed, shifted).astype(jnp.bfloat16)

    def project(start, count):
        return jnp.dot(attended, w_proj, preferred_element_type=jnp.float32)

    middle = state + sum_rows(project, rows)
    normed2_all = gather_rows(normalize(middle, gain[1], shift[1]).astype(jnp.bfloat16))
    hidden = jnp.dot(normed2_all, w_up, preferred_element_type=jnp.float32)
    active = gelu_tanh(hidden).astype(jnp.bfloat16)

    def lower(start, count):
        return jnp.dot(active, w_down, preferred_element_type=jnp.float32)

    result = middle + sum_rows(lower, rows)
    saved = (
        state,
        normed_all,
        q_win,
        k_win,
        v_win,
        log_total,
        attended,
        middle,
        normed2_all,
        hidden,
        active,
    )
    return (result, saved)


def backward_layer(grad_out, saved, weights, gain, shift, bias, mask_add, shifted, onehot):
    (
        state,
        normed_all,
        q_win,
        k_win,
        v_win,
        log_total,
        attended,
        middle,
        normed2_all,
        hidden,
        active,
    ) = saved
    w_qkv, w_proj, w_up, w_down = weights
    rows = grad_out.shape[0]
    heads = q_win.shape[2]
    grad_low = gather_grads(grad_out.astype(jnp.bfloat16))
    grad_down = jnp.einsum("tf,td->fd", active, grad_low, preferred_element_type=jnp.float32)
    grad_active = jnp.einsum("td,fd->tf", grad_low, w_down, preferred_element_type=jnp.float32)
    _, gelu_back = jax.vjp(gelu_tanh, hidden)
    grad_hidden = gelu_back(grad_active)[0].astype(jnp.bfloat16)
    grad_up = jnp.einsum("td,tf->df", normed2_all, grad_hidden, preferred_element_type=jnp.float32)

    def back_up(start, count):
        return jnp.einsum("tf,df->td", grad_hidden, w_up, preferred_element_type=jnp.float32)

    grad_normed2 = sum_grads(back_up, rows)
    _, norm_back2 = jax.vjp(normalize, middle, gain[1], shift[1])
    grad_mid, grad_gain2, grad_shift2 = norm_back2(grad_normed2)
    grad_mid = grad_out + grad_mid
    grad_mid_low = gather_grads(grad_mid.astype(jnp.bfloat16))
    grad_proj = jnp.einsum("tc,td->cd", attended, grad_mid_low, preferred_element_type=jnp.float32)
    grad_att = jnp.einsum(
        "td,cd->tc", grad_mid_low, w_proj, preferred_element_type=jnp.float32
    ).astype(jnp.bfloat16)
    grad_win = window_rows(grad_att, shifted)
    raw = scores_of(q_win, k_win, bias, mask_add, shifted)
    probs = jnp.exp(raw - log_total[..., None])
    grad_probs = jnp.einsum("wqhc,wkhc->whqk", grad_win, v_win, preferred_element_type=jnp.float32)
    grad_v = jnp.einsum(
        "whqk,wqhc->wkhc", probs.astype(jnp.bfloat16), grad_win, preferred_element_type=jnp.float32
    ).astype(jnp.bfloat16)
    inner = jnp.sum(probs * grad_probs, axis=-1, keepdims=True)
    grad_raw = (probs * (grad_probs - inner)).astype(jnp.bfloat16)
    grad_q = (
        jnp.einsum("whqk,wkhc->wqhc", grad_raw, k_win, preferred_element_type=jnp.float32)
        * HEAD ** (-0.5)
    ).astype(jnp.bfloat16)
    grad_k = (
        jnp.einsum("whqk,wqhc->wkhc", grad_raw, q_win, preferred_element_type=jnp.float32)
        * HEAD ** (-0.5)
    ).astype(jnp.bfloat16)
    grad_bias = jnp.sum(grad_raw.astype(jnp.float32), axis=0)
    grad_bias = grad_bias.transpose(1, 2, 0).reshape(-1, heads)
    grad_table = jnp.einsum("pr,ph->rh", onehot, grad_bias, precision=lax.Precision.HIGHEST)
    grad_qkv_rows = jnp.stack(
        [
            unwindow_rows(grad_q, shifted),
            unwindow_rows(grad_k, shifted),
            unwindow_rows(grad_v, shifted),
        ],
        axis=1,
    )
    grad_qkv = jnp.einsum(
        "td,tsc->dsc", normed_all, grad_qkv_rows, preferred_element_type=jnp.float32
    )

    def back_qkv(start, count):
        return jnp.einsum("tsc,dsc->td", grad_qkv_rows, w_qkv, preferred_element_type=jnp.float32)

    grad_normed = sum_grads(back_qkv, rows)
    _, norm_back1 = jax.vjp(normalize, state, gain[0], shift[0])
    grad_state, grad_gain1, grad_shift1 = norm_back1(grad_normed)
    grad_in = grad_mid + grad_state
    grad_gain = jnp.stack([grad_gain1, grad_gain2])
    grad_shift = jnp.stack([grad_shift1, grad_shift2])
    return (grad_in, (grad_qkv, grad_proj, grad_up, grad_down), grad_gain, grad_shift, grad_table)


def pack_shards(w_qkv, w_proj, w_up, w_down):
    qkv = w_qkv.transpose(0, 2, 1, 3)
    proj = w_proj.reshape(2, 1, 16, 128)
    a = jnp.concatenate([qkv, proj], axis=1)
    b = w_up.reshape(2, 16, 4, 128).transpose(0, 2, 1, 3)
    c = w_down.reshape(2, 16, 4, 128).transpose(0, 2, 1, 3)
    return a, b, c


def natural(gathered, order):
    where = {axis: 4 - k for k, axis in enumerate(order)}
    moved_to = gathered.transpose(0, where["y"], where["x"], where["z"], 1, 5, 6, 7)
    moved_to = moved_to.reshape(2, 4, 4, 2, 2, 2, 4, 16, 128)
    return moved_to.transpose(0, 1, 2, 4, 3, 5, 6, 7, 8)


def unnatural(grads, order):
    back = grads.transpose(0, 1, 2, 4, 3, 5, 6, 7, 8).reshape(2, 4, 4, 4, 2, 4, 16, 128)
    place = {"y": 1, "x": 2, "z": 3}
    return back.transpose(0, 4, place[order[2]], place[order[1]], place[order[0]], 5, 6, 7)


def unpack(ga, gb, gc):
    a, b, c = (natural(g, order) for g, order in zip((ga, gb, gc), ORDERS))
    qkv = a[:, :, :, :, :, :, :3].transpose(0, 1, 2, 3, 7, 6, 4, 5, 8).reshape(2, 512, 3, 512)
    proj = a[:, :, :, :, :, :, 3].transpose(0, 4, 5, 1, 2, 3, 6, 7).reshape(2, 512, 512)
    up = b.transpose(0, 1, 2, 3, 7, 4, 5, 6, 8).reshape(2, 512, 2048)
    down = c.transpose(0, 4, 5, 1, 2, 3, 7, 6, 8).reshape(2, 2048, 512)
    return qkv, proj, up, down


def repack(qkv, proj, up, down):
    q = qkv.reshape(2, 4, 4, 2, 16, 3, 2, 2, 128).transpose(0, 1, 2, 3, 6, 7, 5, 4, 8)
    p = proj.reshape(2, 2, 2, 4, 4, 2, 1, 16, 128).transpose(0, 3, 4, 5, 1, 2, 6, 7, 8)
    a = jnp.concatenate([q, p], axis=6)
    b = up.reshape(2, 4, 4, 2, 16, 2, 2, 4, 128).transpose(0, 1, 2, 3, 5, 6, 7, 4, 8)
    c = down.reshape(2, 2, 2, 4, 4, 2, 16, 4, 128).transpose(0, 3, 4, 5, 1, 2, 7, 6, 8)
    return tuple(unnatural(g, order) for g, order in zip((a, b, c), ORDERS))


def shards(
    inputs, w_qkv, w_proj, w_up, w_down, ln_gain, ln_shift, tables, region, rel_index, cotangent
):
    dp, tp = lax.axis_index("dp"), lax.axis_index("tensor")
    a, b, c = pack_shards(w_qkv, w_proj, w_up, w_down)
    flat = jnp.pad(tables.reshape(-1), (0, 32 * 44 - 2 * 169 * 4))
    piece = lax.dynamic_slice(flat, (dp * 44,), (44,))
    small = jnp.concatenate([ln_gain.reshape(-1), ln_shift.reshape(-1), piece])
    small = jnp.pad(small, (0, 1024 - 76)).reshape(8, 128)
    ga, gb, gc, gd = gather_all(a, b, c, small)
    tiny = gd.reshape(2, 2, 2, 4, 4, 1024)[..., :76].transpose(3, 4, 2, 1, 0, 5).reshape(32, 4, 76)
    gain_all = tiny[:, :, :16].reshape(32, 4, 2, 2, 4).transpose(2, 3, 0, 1, 4).reshape(2, 2, 512)
    shift_all = tiny[:, :, 16:32].reshape(32, 4, 2, 2, 4).transpose(2, 3, 0, 1, 4).reshape(2, 2, 512)
    table_all = tiny[:, :, 32:].transpose(1, 0, 2).reshape(4, 32 * 44)[:, : 2 * 169 * 4]
    table_all = table_all.reshape(4, 2, 169, 4).transpose(1, 2, 0, 3).reshape(2, 169, 16)
    qkv, proj, up, down = unpack(ga, gb, gc)
    onehot = (
        rel_index.reshape(-1)[:, None] == jnp.arange(169, dtype=jnp.int32)[None, :]
    ).astype(jnp.float32)
    region_win = to_windows(region.reshape(1, SIDE, SIDE, 1))[..., 0]
    same = region_win[:, :, None] == region_win[:, None, :]
    mask_add = jnp.where(same, jnp.float32(0.0), jnp.float32(-1000000000.0))
    biases, saved_all, state = [], [], inputs
    for layer in range(2):
        weights = (qkv[layer], proj[layer], up[layer], down[layer])
        bias = jnp.dot(onehot, table_all[layer], precision=lax.Precision.HIGHEST)
        bias = bias.reshape(49, 49, -1).transpose(2, 0, 1)
        biases.append(bias)
        state, saved = forward_layer(
            state, weights, gain_all[layer], shift_all[layer], bias, mask_add, layer == 1
        )
        saved_all.append(saved)
    grad = cotangent
    grads, gains, shifts, tabs = [None] * 2, [None] * 2, [None] * 2, [None] * 2
    for layer in (1, 0):
        weights = (qkv[layer], proj[layer], up[layer], down[layer])
        grad, grads[layer], gains[layer], shifts[layer], tabs[layer] = backward_layer(
            grad, saved_all[layer], weights, gain_all[layer], shift_all[layer], biases[layer],
            mask_add, layer == 1, onehot,
        )
    stacked = [
        jnp.stack([grads[layer][k] for layer in range(2)]).astype(jnp.bfloat16) for k in range(4)
    ]
    ra, rb, rc = repack(*stacked)
    rest = jnp.concatenate(
        [jnp.stack(gains).reshape(-1), jnp.stack(shifts).reshape(-1), jnp.stack(tabs).reshape(-1)]
    )
    rest = jnp.pad(rest, (0, 80 * 128 - rest.shape[0])).reshape(80, 128)
    oa, ob, oc, od = scatter_all(ra, rb, rc, rest)
    od = od.reshape(-1)
    me = (dp * 4 + tp) * 4
    grad_gain = lax.dynamic_slice(od[:2048].reshape(2, 2, 512), (0, 0, me), (2, 2, 4))
    grad_shift = lax.dynamic_slice(od[2048:4096].reshape(2, 2, 512), (0, 0, me), (2, 2, 4))
    grad_tables = lax.dynamic_slice(
        od[4096 : 4096 + 2 * 169 * 16].reshape(2, 169, 16), (0, 0, tp * 4), (2, 169, 4)
    )
    return (
        state,
        grad,
        oa[:, :3].transpose(0, 2, 1, 3),
        oa[:, 3].reshape(2, 4, 512),
        ob.transpose(0, 2, 1, 3).reshape(2, 16, 512),
        oc.transpose(0, 2, 1, 3).reshape(2, 16, 512),
        grad_gain,
        grad_shift,
        grad_tables,
    )


def solution(mesh):
    return jax.shard_map(
        shards,
        mesh=mesh,
        in_specs=(
            P(("dp", "tensor"), None),
            P(None, "dp", None, "tensor"),
            P(None, ("tensor", "dp"), None),
            P(None, "dp", "tensor"),
            P(None, ("tensor", "dp"), None),
            P(None, None, ("dp", "tensor")),
            P(None, None, ("dp", "tensor")),
            P(None, None, "tensor"),
            P(),
            P(),
            P(("dp", "tensor"), None),
        ),
        out_specs=(
            P(("dp", "tensor"), None),
            P(("dp", "tensor"), None),
            P(None, "dp", None, "tensor"),
            P(None, ("tensor", "dp"), None),
            P(None, "dp", "tensor"),
            P(None, ("tensor", "dp"), None),
            P(None, None, ("dp", "tensor")),
            P(None, None, ("dp", "tensor")),
            P(None, None, "tensor"),
        ),
        check_vma=False,
    )
```

```python
import functools
import jax
import jax.numpy as jnp
import numpy as np
from jax import lax
from jax.experimental import pallas as pl
from jax.experimental.pallas import tpu as pltpu
from jax.sharding import PartitionSpec as P

MESH = pl.DeviceIdType.MESH
ORDERS = (("x", "y", "z"), ("y", "z", "x"), ("z", "x", "y"))


def coords():
    dp, tp = lax.axis_index("dp"), lax.axis_index("tensor")
    return {
        "y": dp // 8,
        "x": (dp // 2) % 4,
        "z": (tp // 2) * 2 + dp % 2,
        "c": tp % 2,
    }


def device(at):
    return (at["y"] * 8 + at["x"] * 2 + at["z"] % 2, (at["z"] // 2) * 2 + at["c"])


def moved(at, axis, step):
    size = 2 if axis == "c" else 4
    return device({**at, axis: (at[axis] + step) % size})


NEIGHBOURS = (("x", 1), ("x", 3), ("y", 1), ("y", 3), ("z", 1), ("z", 3), ("c", 1))


def enter(at, peers=NEIGHBOURS):
    barrier = pltpu.get_barrier_semaphore()
    for axis, step in peers:
        pl.semaphore_signal(barrier, inc=1, device_id=moved(at, axis, step), device_id_type=MESH)
    pl.semaphore_wait(barrier, len(peers))


PEERS = NEIGHBOURS + (("x", 2), ("y", 2), ("z", 2))
COPIES = 224


class Copier:
    def __init__(self, at, send, recv):
        self.at, self.send, self.recv, self.made = at, send, recv, []

    def __call__(self, src, dst, axis, step):
        slot = len(self.made)
        copy = pltpu.make_async_remote_copy(
            src_ref=src,
            dst_ref=dst,
            send_sem=self.send.at[slot],
            recv_sem=self.recv.at[slot],
            device_id=moved(self.at, axis, step),
            device_id_type=MESH,
        )
        copy.start()
        self.made.append(copy)
        return copy

    def finish(self):
        for copy in self.made:
            copy.wait_send()


def ring_gather(copy, axis, index, slot):
    left, right = (index + 3) % 4, (index + 1) % 4
    held = {}

    def first():
        held["r"] = copy(slot(index), slot(index), axis, 1)
        held["l"] = copy(slot(index), slot(index), axis, 3)

    def second():
        held["r"].wait_recv()
        held["r2"] = copy(slot(left).at[0:2], slot(left).at[0:2], axis, 1)
        held["l"].wait_recv()
        held["l2"] = copy(slot(right).at[2:4], slot(right).at[2:4], axis, 3)

    def third():
        held["r2"].wait_recv()
        held["l2"].wait_recv()

    return first, second, third


def gather_kernel(a, b, c, d, ga, gb, gc, gd, send, recv, local):
    at = coords()
    core = at["c"]
    copy = Copier(at, send, recv)
    own = []

    def place(src, dst):
        put = pltpu.make_async_copy(src, dst, local.at[len(own)])
        put.start()
        own.append(put)

    place(d, gd.at[core, at["z"], at["y"], at["x"]])
    for layer in range(2):
        for order, src, dst in zip(ORDERS, (a, b, c), (ga, gb, gc)):
            i1, i2, i3 = (at[axis] for axis in order)
            place(src.at[layer], dst.at[layer, core, i3, i2, i1])
    enter(at, PEERS)
    for put in own:
        put.wait()

    def stages(layer):
        plans = []
        for order, dst in zip(ORDERS, (ga, gb, gc)):
            i1, i2, i3 = (at[axis] for axis in order)
            whole = dst.at[layer, core]
            plans.append(
                (
                    ring_gather(copy, order[0], i1, lambda j, w=whole, p=i3, q=i2: w.at[p, q, j]),
                    ring_gather(copy, order[1], i2, lambda j, w=whole, p=i3: w.at[p, j]),
                    ring_gather(copy, order[2], i3, lambda j, w=whole: w.at[j]),
                    whole,
                    i3,
                )
            )
        across = []

        def pass_on(ref):
            across.append(copy(ref, ref, "c", 1))

        def one(phase, step):
            def run():
                for plan in plans:
                    plan[phase][step]()
                    if phase == 2:
                        whole, i3 = plan[3], plan[4]
                        if step == 0:
                            pass_on(whole.at[i3])
                        elif step == 1:
                            pass_on(whole.at[(i3 + 3) % 4])
                            pass_on(whole.at[(i3 + 1) % 4])
                        else:
                            pass_on(whole.at[(i3 + 2) % 4])

            return run

        def last():
            for sent in across:
                sent.wait_recv()

        return [one(phase, step) for phase in range(3) for step in range(3)] + [last]

    def small():
        slots = (
            ("x", lambda: gd.at[core, at["z"], at["y"], at["x"]]),
            ("y", lambda: gd.at[core, at["z"], at["y"]]),
            ("z", lambda: gd.at[core, at["z"]]),
            ("c", lambda: gd.at[core]),
        )
        out = []
        for axis, ref in slots:

            def start(axis=axis, ref=ref):
                steps = (1,) if axis == "c" else (1, 2, 3)
                out.append([copy(ref(), ref(), axis, step) for step in steps])

            def end():
                for sent in out[-1]:
                    sent.wait_recv()

            yield start
            yield end

    low, high, tiny = stages(0), stages(1), list(small())
    for step in range(12):
        if step < len(low):
            low[step]()
        if step < len(tiny):
            tiny[step]()
        if step >= 2:
            high[step - 2]()
    copy.finish()


def gather_all(a, b, c, d):
    shape = jax.ShapeDtypeStruct((2, 2, 4, 4, 4, 4, 16, 128), jnp.bfloat16)
    return pl.pallas_call(
        gather_kernel,
        out_shape=(shape, shape, shape, jax.ShapeDtypeStruct((2, 4, 4, 4, 8, 128), jnp.float32)),
        in_specs=[pl.BlockSpec(memory_space=pl.ANY)] * 4,
        out_specs=[pl.BlockSpec(memory_space=pl.ANY)] * 4,
        scratch_shapes=[
            pltpu.SemaphoreType.DMA((COPIES,)),
            pltpu.SemaphoreType.DMA((COPIES,)),
            pltpu.SemaphoreType.DMA((8,)),
        ],
        compiler_params=pltpu.CompilerParams(collective_id=0, has_side_effects=True),
        name="gather_weights",
    )(a, b, c, d)


def add_into(dst, *terms):
    lead = dst.shape[:-3]
    count = 1
    for size in lead:
        count *= size

    def body(n, carry):
        index = []
        for size in reversed(lead):
            index.append(n % size)
            n = n // size
        index = tuple(reversed(index))
        total = dst[index].astype(jnp.float32)
        for term in terms:
            total = total + term[index].astype(jnp.float32)
        dst[index] = total.astype(dst.dtype)
        return carry

    lax.fori_loop(0, count, body, 0)


def ring_scatter(copy, axis, index, slot, half_r, half_l, full_r, full_l):
    left, right, far = (index + 3) % 4, (index + 1) % 4, (index + 2) % 4
    held = {}

    def first():
        held["r"] = copy(slot(far).at[0:2], half_r, axis, 1)
        held["l"] = copy(slot(far).at[2:4], half_l, axis, 3)

    def second():
        held["r"].wait_recv()
        add_into(slot(right).at[0:2], half_r)
        held["r2"] = copy(slot(right), full_r, axis, 1)
        held["l"].wait_recv()
        add_into(slot(left).at[2:4], half_l)
        held["l2"] = copy(slot(left), full_l, axis, 3)

    def third():
        held["r2"].wait_recv()
        held["l2"].wait_recv()
        add_into(slot(index), full_r, full_l)

    return first, second, third


def scatter_kernel(ga, gb, gc, d, oa, ob, oc, od, sums, landed, h3, f3, h2, f2, h1, f1, dsum, dland, send, recv, local):
    at = coords()
    core = at["c"]
    copy = Copier(at, send, recv)
    puts = {}
    for layer in (1, 0):
        for family, src in enumerate((ga, gb, gc)):
            put = pltpu.make_async_copy(src.at[layer, core], sums.at[layer, family], local.at[layer * 3 + family])
            put.start()
            puts[layer, family] = put
    enter(at, PEERS)
    plans = {0: [], 1: []}
    for layer in (1, 0):
        for family, src in enumerate((ga, gb, gc)):
            order = ORDERS[family]
            i1, i2, i3 = (at[axis] for axis in order)
            whole = sums.at[layer, family]
            put = puts[layer, family]
            land = landed.at[layer, family]

            def core_first(src=src, land=land, layer=layer, held=None):
                return copy(src.at[layer, 1 - core], land, "c", 1)

            plans[layer].append(
                (
                    core_first,
                    put,
                    whole,
                    land,
                    ring_scatter(
                        copy, order[2], i3, lambda j, w=whole: w.at[j],
                        *(h3.at[layer, family, k] for k in range(2)), *(f3.at[layer, family, k] for k in range(2)),
                    ),
                    ring_scatter(
                        copy, order[1], i2, lambda j, w=whole, p=i3: w.at[p, j],
                        *(h2.at[layer, family, k] for k in range(2)), *(f2.at[layer, family, k] for k in range(2)),
                    ),
                    ring_scatter(
                        copy, order[0], i1, lambda j, w=whole, p=i3, q=i2: w.at[p, q, j],
                        *(h1.at[layer, family, k] for k in range(2)), *(f1.at[layer, family, k] for k in range(2)),
                    ),
                    whole.at[i3, i2, i1],
                )
            )

    def stages(layer):
        crossed = []

        def begin():
            for plan in plans[layer]:
                crossed.append(plan[0]())

        def joined():
            for plan, sent in zip(plans[layer], crossed):
                plan[1].wait()
                sent.wait_recv()
                add_into(plan[2], plan[3])

        def one(phase, step):
            def run():
                for plan in plans[layer]:
                    plan[4 + phase][step]()

            return run

        def last():
            for plan, out in zip(plans[layer], (oa, ob, oc)):
                out[layer] = plan[7][...].astype(jnp.float32)

        return [begin, joined] + [one(phase, step) for phase in range(3) for step in range(3)] + [last]

    dsum[...] = d[...]
    turns = []
    for phase, (axis, size) in enumerate((("c", 2), ("x", 4), ("y", 4), ("z", 4))):
        sent = []

        def start(axis=axis, size=size, phase=phase, sent=sent):
            mine = at[axis]
            dland[phase, mine] = dsum[...]
            for step in range(1, size):
                sent.append(copy(dland.at[phase, mine], dland.at[phase, mine], axis, step))

        def end(size=size, phase=phase, sent=sent):
            for one in sent:
                one.wait_recv()
            total = dland[phase, 0]
            for k in range(1, size):
                total = total + dland[phase, k]
            dsum[...] = total

        turns += [start, end]

    high, low = stages(1), stages(0)
    for step in range(14):
        if step < len(high):
            high[step]()
        if step < len(turns):
            turns[step]()
        if step >= 2:
            low[step - 2]()
    od[...] = dsum[...]
    copy.finish()


def scatter_all(ga, gb, gc, d):
    out = jax.ShapeDtypeStruct((2, 4, 16, 128), jnp.float32)
    bf = jnp.bfloat16
    return pl.pallas_call(
        scatter_kernel,
        out_shape=(out, out, out, jax.ShapeDtypeStruct(d.shape, jnp.float32)),
        in_specs=[pl.BlockSpec(memory_space=pl.ANY)] * 3 + [pl.BlockSpec(memory_space=pltpu.VMEM)],
        out_specs=[pl.BlockSpec(memory_space=pltpu.VMEM)] * 4,
        scratch_shapes=[
            pltpu.VMEM((2, 3, 4, 4, 4, 4, 16, 128), bf),
            pltpu.VMEM((2, 3, 4, 4, 4, 4, 16, 128), bf),
            pltpu.VMEM((2, 3, 2, 2, 4, 4, 16, 128), bf),
            pltpu.VMEM((2, 3, 2, 4, 4, 4, 16, 128), bf),
            pltpu.VMEM((2, 3, 2, 2, 4, 16, 128), bf),
            pltpu.VMEM((2, 3, 2, 4, 4, 16, 128), bf),
            pltpu.VMEM((2, 3, 2, 2, 16, 128), bf),
            pltpu.VMEM((2, 3, 2, 4, 16, 128), bf),
            pltpu.VMEM(d.shape, jnp.float32),
            pltpu.VMEM((4, 4) + d.shape, jnp.float32),
            pltpu.SemaphoreType.DMA((COPIES,)),
            pltpu.SemaphoreType.DMA((COPIES,)),
            pltpu.SemaphoreType.DMA((8,)),
        ],
        compiler_params=pltpu.CompilerParams(
            collective_id=1, has_side_effects=True, vmem_limit_bytes=48 * 2**20
        ),
        name="scatter_grads",
    )(ga, gb, gc, d)


WINDOW = 7
SIDE = 14
EPS = 1e-05


def to_windows(field):
    count, side, _, width = field.shape
    per = side // WINDOW
    field = field.reshape(count, per, WINDOW, per, WINDOW, width).transpose(0, 1, 3, 2, 4, 5)
    return field.reshape(count * per * per, WINDOW * WINDOW, width)


BF, F32 = jnp.bfloat16, jnp.float32
SCALE = 32.0 ** -0.5
ROWS, PADDED, WIDTH = 784, 1024, 512
NN = (((1,), (0,)), ((), ()))
NT = (((1,), (1,)), ((), ()))
TN = (((0,), (0,)), ((), ()))


def mul(a, b, dims=NN):
    return lax.dot_general(a, b, dims, preferred_element_type=F32)


def window_maps():
    maps = np.zeros((2, 2, 512, 400), np.float32)
    for layer in range(2):
        for pair in range(2):
            for image in range(2):
                for window in range(4):
                    for r in range(7):
                        for c in range(7):
                            row = 7 * (window // 2) + r
                            col = 7 * (window % 2) + c
                            if layer:
                                row, col = (row + 3) % 14, (col + 3) % 14
                            to = image * 256 + window * 64 + r * 7 + c
                            maps[layer, pair, to, image * 196 + row * 14 + col + 8 * pair] = 1
    return maps


def proj_maps():
    maps = np.zeros((4, 64, 256), np.float32)
    for q in range(4):
        for dev in range(16):
            for r in range(4):
                maps[q, dev * 4 + r, dev * 16 + r * 4 + q] = 1
    return maps


PLACES = [(y, x, zl) for y in range(4) for x in range(4) for zl in range(2)]


def rows_of(tiles):
    return jnp.concatenate(tiles, axis=0)


def up_block(wb, slot):
    return jnp.concatenate(
        [rows_of([wb[slot, x, zl, y, q] for y, x, zl in PLACES]) for q in range(4)], axis=1
    )


def down_block(wc, slot):
    return jnp.concatenate(
        [rows_of([wc[slot, y, x, zl, q] for y, x, zl in PLACES]) for q in range(4)], axis=1
    )


def qkv_block(ga, layer, s):
    return jnp.concatenate(
        [
            rows_of([ga[layer, t % 2, 2 * (t // 2) + zl, y, x, s] for y, x, zl in PLACES])
            for t in range(4)
        ],
        axis=1,
    )


def norm_parts(values):
    mean = jnp.mean(values, axis=1, keepdims=True)
    centered = values - mean
    r = lax.rsqrt(jnp.mean(centered * centered, axis=1, keepdims=True) + EPS)
    return centered * r, r


def norm_back(grad, values, gain):
    xhat, r = norm_parts(values)
    e = grad * gain
    through = r * (
        e - jnp.mean(e, axis=1, keepdims=True) - xhat * jnp.mean(e * xhat, axis=1, keepdims=True)
    )
    return (
        through,
        jnp.sum(grad * xhat, axis=0, keepdims=True),
        jnp.sum(grad, axis=0, keepdims=True),
    )


C0, C1 = 0.7978845608028654, 0.044715


def gelu(u):
    return 0.5 * u * (1.0 + jnp.tanh(C0 * u * (1.0 + C1 * (u * u))))


def gelu_both(u):
    square = u * u
    t = jnp.tanh(C0 * u * (1.0 + C1 * square))
    half = 0.5 * (1.0 + t)
    slope = half + (0.5 * C0) * u * (1.0 - t * t) * (1.0 + (3.0 * C1) * square)
    return u * half, slope


def to_windows_of(maps, layer, tokens):
    return [mul(maps[layer, pair], tokens[pair * 384 : pair * 384 + 400, :]) for pair in range(2)]


def from_windows_of(maps, layer, rows):
    first = mul(maps[layer, 0], rows[0:512, :], TN)
    second = mul(maps[layer, 1], rows[512:1024, :], TN)
    return jnp.concatenate(
        [first[:384], first[384:400] + second[:16], second[16:]], axis=0
    )


def head_masks():
    lane = lax.broadcasted_iota(jnp.int32, (1, 128), 1) // 32
    return [lane == h for h in range(4)]


def spread(v, masks):
    none = jnp.zeros((64, 128), v.dtype)
    rows = []
    for h in range(8):
        half = h // 4
        part = jnp.where(masks[h % 4], v[:, half * 128 : half * 128 + 128], jnp.zeros((), v.dtype))
        rows.append(jnp.concatenate([none, part] if half else [part, none], axis=1))
    return jnp.concatenate(rows, axis=0)


def fold(r, masks):
    halves = []
    for half in range(2):
        out = None
        for h in range(4):
            at = (half * 4 + h) * 64
            part = r[at : at + 64, half * 128 : half * 128 + 128]
            out = part if out is None else jnp.where(masks[h], part, out)
        halves.append(out)
    return jnp.concatenate(halves, axis=1)


UNROLL = 4


def columns(s, g):
    return slice(s * 512 + g * 256, s * 512 + g * 256 + 256)


def attend(layer, qkv, bias, mask, kept, out):
    masks = head_masks()

    def some(n, carry):
        items = [(n * UNROLL + u, u, g) for u in range(UNROLL) for g in range(2)]

        def rows(w):
            return pl.ds(pl.multiple_of(w * 64, 64), 64)

        scores = [
            mul(qkv[layer, rows(w), columns(1, g)], spread(qkv[layer, rows(w), columns(0, g)], masks), NT)
            for w, u, g in items
        ]
        probs = []
        for (w, u, g), s in zip(items, scores):
            s = s * SCALE + bias[layer, g]
            if layer:
                s = s + mask[u % 4]
            e = jnp.exp(s - jnp.max(s, axis=0, keepdims=True))
            p = (e * (1.0 / jnp.sum(e, axis=0, keepdims=True))).astype(BF)
            kept[layer, w * 2 + g] = p
            probs.append(p)
        for (w, u, g), p in zip(items, probs):
            r = mul(p, qkv[layer, rows(w), columns(2, g)], TN)
            out[rows(w), g * 256 : g * 256 + 256] = fold(r, masks).astype(BF)
        return carry

    lax.fori_loop(0, 16 // UNROLL, some, 0)


def attend_back(layer, qkv, kept, gout, gbias):
    masks = head_masks()

    def some(n, carry):
        items = [(n * UNROLL + u, g) for u in range(UNROLL) for g in range(2)]

        def rows(w):
            return pl.ds(pl.multiple_of(w * 64, 64), 64)

        gprobs, gvs = [], []
        for w, g in items:
            d = spread(gout[rows(w), g * 256 : g * 256 + 256], masks)
            gprobs.append(mul(qkv[layer, rows(w), columns(2, g)], d, NT))
            gvs.append(mul(kept[layer, w * 2 + g], d))
        for (w, g), gv in zip(items, gvs):
            qkv[layer, rows(w), columns(2, g)] = gv.astype(BF)
        gscores = []
        for (w, g), gp in zip(items, gprobs):
            p = kept[layer, w * 2 + g].astype(F32)
            pg = p * gp
            gscores.append(pg - p * jnp.sum(pg, axis=0, keepdims=True))
        for g in range(2):
            total = gbias[layer, g]
            for (w, h), gs in zip(items, gscores):
                if h == g:
                    total = total + gs
            gbias[layer, g] = total
        for (w, g), gs in zip(items, gscores):
            ds = gs.astype(BF)
            q = qkv[layer, rows(w), columns(0, g)]
            k = qkv[layer, rows(w), columns(1, g)]
            gk = mul(ds, spread(q, masks)) * SCALE
            gq = fold(mul(ds, k, TN), masks) * SCALE
            qkv[layer, rows(w), columns(0, g)] = gq.astype(BF)
            qkv[layer, rows(w), columns(1, g)] = gk.astype(BF)
        return carry

    lax.fori_loop(0, 16 // UNROLL, some, 0)


def forward(layer, x, result, gain, shift, ga, feed, wp, maps, bias, mask, s):
    xhat, _ = norm_parts(x[...])
    s.low[...] = (xhat * gain[layer, 0:1] + shift[layer, 0:1]).astype(BF)
    for pair, part in enumerate(to_windows_of(maps, layer, s.low)):
        s.n1w[layer, pair * 512 : pair * 512 + 512, :] = part.astype(BF)
    for k in range(3):
        s.qkv[layer, :, k * 512 : k * 512 + 512] = mul(s.n1w[layer], qkv_block(ga, layer, k)).astype(BF)
    attend(layer, s.qkv, bias, mask, s.kept, s.ow)
    s.att[layer] = from_windows_of(maps, layer, s.ow).astype(BF)
    s.mid[layer] = x[...] + mul(s.att[layer], wp[layer])
    xhat, _ = norm_parts(s.mid[layer])
    s.n2[layer] = (xhat * gain[layer, 1:2] + shift[layer, 1:2]).astype(BF)
    result[...] = s.mid[layer]

    def chunk(t, carry):
        slot = feed.take(t)
        feed.fetch(jnp.where(t == 3, 1, layer), (t + 1) % 4)
        hidden = mul(s.n2[layer], up_block(feed.wb, slot))
        s.hid[layer, t] = hidden.astype(BF)
        result[...] += mul(gelu(hidden).astype(BF), down_block(feed.wc, slot))
        return carry

    lax.fori_loop(0, 4, chunk, 0)


def backward(layer, x, g, gain, ga, feed, ra, rb, rc, wp, maps, pack, dgain, dshift, gbias, s):
    s.low[...] = g[...].astype(BF)
    s.gn[0:ROWS, :] = jnp.zeros((ROWS, WIDTH), F32)

    def chunk(t, carry):
        zh, c = t // 2, t % 2
        slot = feed.take(t)
        if layer:
            feed.fetch(jnp.where(t == 3, 0, 1), (t + 1) % 4)
        else:
            pl.when(t < 3)(lambda: feed.fetch(0, (t + 1) % 4))

        @pl.when(t >= 2)
        def _():
            s.wait_mlp(rb, rc, layer, slot)

        active, slope = gelu_both(s.hid[layer, t].astype(F32))
        gh = (mul(s.low[...], down_block(feed.wc, slot), NT) * slope).astype(BF)
        gdown = mul(active.astype(BF), s.low[...], TN).astype(BF)
        for n, (y, xx, zl) in enumerate(PLACES):
            for q in range(4):
                s.stage_c[slot, y, xx, zl, q] = gdown[n * 16 : n * 16 + 16, q * 128 : q * 128 + 128]
        gup = mul(s.n2[layer], gh, TN).astype(BF)
        for n, (y, xx, zl) in enumerate(PLACES):
            for q in range(4):
                s.stage_b[slot, xx, zl, y, q] = gup[n * 16 : n * 16 + 16, q * 128 : q * 128 + 128]
        s.send_mlp(rb, rc, layer, slot, zh, c)
        s.gn[0:ROWS, :] += mul(gh, up_block(feed.wb, slot), NT)
        return carry

    lax.fori_loop(0, 4, chunk, 0)
    for slot in range(2):
        s.wait_mlp(rb, rc, layer, slot)
    through, dg, ds = norm_back(s.gn[0:ROWS, :], s.mid[layer], gain[layer, 1:2])
    dgain[layer, 1:2] = dg
    dshift[layer, 1:2] = ds
    g[...] += through
    s.low[...] = g[...].astype(BF)
    gproj = mul(s.att[layer], s.low[...], TN).astype(BF)
    for block in range(8):
        part = gproj[block * 64 : block * 64 + 64]
        packed = mul(pack[0], part[:, 0:128], TN)
        for q in range(1, 4):
            packed = packed + mul(pack[q], part[:, q * 128 : q * 128 + 128], TN)
        packed = packed.astype(BF)
        for n in range(16):
            dev = block * 16 + n
            t, (y, xx, zl) = dev // 32, PLACES[dev % 32]
            s.stage_a[t % 2, 2 * (t // 2) + zl, y, xx, 3] = packed[n * 16 : n * 16 + 16]
    for pair, part in enumerate(to_windows_of(maps, layer, s.low)):
        s.ow[pair * 512 : pair * 512 + 512, :] = part.astype(BF)
    s.ow[...] = mul(s.ow[...], wp[layer], NT).astype(BF)
    attend_back(layer, s.qkv, s.kept, s.ow, gbias)
    s.gn[...] = jnp.zeros((PADDED, WIDTH), F32)
    for k in range(3):
        grads = s.qkv[layer, :, k * 512 : k * 512 + 512]
        gw = mul(s.n1w[layer], grads, TN).astype(BF)
        for t in range(4):
            for n, (y, xx, zl) in enumerate(PLACES):
                s.stage_a[t % 2, 2 * (t // 2) + zl, y, xx, k] = gw[n * 16 : n * 16 + 16, t * 128 : t * 128 + 128]
        s.gn[...] += mul(grads, qkv_block(ga, layer, k), NT)
    out = pltpu.make_async_copy(s.stage_a, ra.at[layer], s.sems.at[4])
    out.start()
    s.ow[...] = s.gn[...].astype(BF)
    through, dg, ds = norm_back(from_windows_of(maps, layer, s.ow), x[...], gain[layer, 0:1])
    dgain[layer, 0:1] = dg
    dshift[layer, 0:1] = ds
    g[...] += through
    out.wait()


class Feed:
    def __init__(self, gb, gc, wb, wc, sems):
        self.gb, self.gc, self.wb, self.wc, self.sems = gb, gc, wb, wc, sems

    def copies(self, layer, t):
        slot, z = t % 2, pl.ds(2 * (t // 2), 2)
        return (
            pltpu.make_async_copy(self.gb.at[layer, t % 2, :, z], self.wb.at[slot], self.sems.at[slot]),
            pltpu.make_async_copy(self.gc.at[layer, t % 2, :, :, z], self.wc.at[slot], self.sems.at[2 + slot]),
        )

    def fetch(self, layer, t):
        for one in self.copies(layer, t):
            one.start()

    def take(self, t):
        for one in self.copies(0, t):
            one.wait()
        return t % 2


class Scratch:
    names = ("low", "n1w", "qkv", "kept", "ow", "att", "mid", "n2", "hid", "gn", "stage_a", "stage_b", "stage_c", "sems")

    def __init__(self, refs):
        for name, ref in zip(self.names, refs):
            setattr(self, name, ref)

    @staticmethod
    def shapes():
        return [
            pltpu.VMEM((ROWS, WIDTH), BF),
            pltpu.VMEM((2, PADDED, WIDTH), BF),
            pltpu.VMEM((2, PADDED, 3 * WIDTH), BF),
            pltpu.VMEM((2, 32, 64, 512), BF),
            pltpu.VMEM((PADDED, WIDTH), BF),
            pltpu.VMEM((2, ROWS, WIDTH), BF),
            pltpu.VMEM((2, ROWS, WIDTH), F32),
            pltpu.VMEM((2, ROWS, WIDTH), BF),
            pltpu.VMEM((2, 4, ROWS, WIDTH), BF),
            pltpu.VMEM((PADDED, WIDTH), F32),
            pltpu.VMEM((2, 4, 4, 4, 4, 16, 128), BF),
            pltpu.VMEM((2, 4, 2, 4, 4, 16, 128), BF),
            pltpu.VMEM((2, 4, 4, 2, 4, 16, 128), BF),
            pltpu.SemaphoreType.DMA((8,)),
        ]

    def mlp_copies(self, rb, rc, layer, slot, zh, c):
        z = pl.ds(2 * zh, 2)
        return (
            pltpu.make_async_copy(self.stage_b.at[slot], rb.at[layer, c, :, z], self.sems.at[slot]),
            pltpu.make_async_copy(self.stage_c.at[slot], rc.at[layer, c, :, :, z], self.sems.at[2 + slot]),
        )

    def send_mlp(self, rb, rc, layer, slot, zh, c):
        for one in self.mlp_copies(rb, rc, layer, slot, zh, c):
            one.start()

    def wait_mlp(self, rb, rc, layer, slot):
        for one in self.mlp_copies(rb, rc, layer, slot, 0, 0):
            one.wait()


def core_kernel(x, cot, ga_h, gb, gc, gain, shift, bias, mask, maps, pack,
                out, g, ra, rb, rc, dgain, dshift, gbias, ga, wb, wc, x1, wp, feeds, *rest):
    s = Scratch(rest)
    feed = Feed(gb, gc, wb, wc, feeds)
    load = pltpu.make_async_copy(ga_h, ga, s.sems.at[5])
    load.start()
    start = pltpu.make_async_copy(cot, g, s.sems.at[4])
    start.start()
    feed.fetch(0, 0)
    gbias[...] = jnp.zeros(gbias.shape, F32)
    load.wait()
    start.wait()
    for layer in range(2):
        for block in range(8):
            tiles = []
            for n in range(16):
                dev = block * 16 + n
                t, (y, xx, zl) = dev // 32, PLACES[dev % 32]
                tiles.append(ga[layer, t % 2, 2 * (t // 2) + zl, y, xx, 3])
            tiles = rows_of(tiles)
            for q in range(4):
                wp[layer, block * 64 : block * 64 + 64, q * 128 : q * 128 + 128] = mul(pack[q], tiles).astype(BF)
    forward(0, x, x1, gain, shift, ga, feed, wp, maps, bias, mask, s)
    forward(1, x1, out, gain, shift, ga, feed, wp, maps, bias, mask, s)
    backward(1, x1, g, gain, ga, feed, ra, rb, rc, wp, maps, pack, dgain, dshift, gbias, s)
    backward(0, x, g, gain, ga, feed, ra, rb, rc, wp, maps, pack, dgain, dshift, gbias, s)


def core(x, cot, ga, gb, gc, gain, shift, bias, mask):
    maps = jnp.asarray(window_maps(), BF)
    pack = jnp.asarray(proj_maps(), BF)
    tiles = jax.ShapeDtypeStruct((2, 2, 4, 4, 4, 4, 16, 128), BF)
    rows = jax.ShapeDtypeStruct((ROWS, WIDTH), F32)
    vector = jax.ShapeDtypeStruct((2, 2, WIDTH), F32)
    vmem, far = pl.BlockSpec(memory_space=pltpu.VMEM), pl.BlockSpec(memory_space=pl.ANY)
    return pl.pallas_call(
        core_kernel,
        out_shape=(rows, rows, tiles, tiles, tiles, vector, vector, jax.ShapeDtypeStruct((2, 2, 64, 512), F32)),
        in_specs=[vmem] + [far] * 4 + [vmem] * 6,
        out_specs=[vmem] * 2 + [far] * 3 + [vmem] * 3,
        scratch_shapes=[
            pltpu.VMEM(tiles.shape, BF),
            pltpu.VMEM((2, 4, 2, 4, 4, 16, 128), BF),
            pltpu.VMEM((2, 4, 4, 2, 4, 16, 128), BF),
            pltpu.VMEM((ROWS, WIDTH), F32),
            pltpu.VMEM((2, WIDTH, WIDTH), BF),
            pltpu.SemaphoreType.DMA((4,)),
        ] + Scratch.shapes(),
        compiler_params=pltpu.CompilerParams(vmem_limit_bytes=63 * 2**20),
        name="both_blocks",
    )(x, cot, ga, gb, gc, gain, shift, bias, mask, maps, pack)


def score_terms(table_all, region, rel_index):
    onehot = (rel_index.T.reshape(-1)[:, None] == jnp.arange(169, dtype=jnp.int32)[None, :]).astype(F32)
    tabs = table_all.transpose(1, 0, 2).reshape(169, 32)
    bias = jnp.dot(onehot, tabs, precision=lax.Precision.HIGHEST)
    bias = bias.reshape(49, 49, 2, 2, 8).transpose(2, 3, 0, 4, 1)
    bias = jnp.pad(bias, ((0, 0), (0, 0), (0, 0), (0, 0), (0, 15)))
    bias = jnp.pad(bias, ((0, 0), (0, 0), (0, 15), (0, 0), (0, 0)), constant_values=-1e30)
    region_win = to_windows(region.reshape(1, SIDE, SIDE, 1))[..., 0]
    same = region_win[:, :, None] == region_win[:, None, :]
    mask = jnp.where(same, F32(0.0), F32(-1e9))
    mask = jnp.pad(mask, ((0, 0), (0, 15), (0, 15)))
    mask = jnp.broadcast_to(mask[:, :, None, :], (4, 64, 8, 64)).reshape(4, 64, 512)
    return bias.reshape(2, 2, 64, 512), mask, onehot


def table_grads(gbias, onehot):
    back = gbias.reshape(2, 2, 64, 8, 64)[:, :, :49, :, :49].transpose(2, 4, 0, 1, 3).reshape(2401, 32)
    out = jnp.einsum("pr,ph->rh", onehot, back, precision=lax.Precision.HIGHEST)
    return out.reshape(169, 2, 16).transpose(1, 0, 2)


def pack_shards(w_qkv, w_proj, w_up, w_down):
    qkv = w_qkv.transpose(0, 2, 1, 3)
    proj = w_proj.reshape(2, 1, 16, 128)
    a = jnp.concatenate([qkv, proj], axis=1)
    b = w_up.reshape(2, 16, 4, 128).transpose(0, 2, 1, 3)
    c = w_down.reshape(2, 16, 4, 128).transpose(0, 2, 1, 3)
    return a, b, c


def shards(
    inputs, w_qkv, w_proj, w_up, w_down, ln_gain, ln_shift, tables, region, rel_index, cotangent
):
    dp, tp = lax.axis_index("dp"), lax.axis_index("tensor")
    a, b, c = pack_shards(w_qkv, w_proj, w_up, w_down)
    flat = jnp.pad(tables.reshape(-1), (0, 32 * 44 - 2 * 169 * 4))
    piece = lax.dynamic_slice(flat, (dp * 44,), (44,))
    small = jnp.concatenate([ln_gain.reshape(-1), ln_shift.reshape(-1), piece])
    small = jnp.pad(small, (0, 1024 - 76)).reshape(8, 128)
    ga, gb, gc, gd = gather_all(a, b, c, small)
    tiny = gd.reshape(2, 2, 2, 4, 4, 1024)[..., :76].transpose(3, 4, 2, 1, 0, 5).reshape(32, 4, 76)
    gain_all = tiny[:, :, :16].reshape(32, 4, 2, 2, 4).transpose(2, 3, 0, 1, 4).reshape(2, 2, 512)
    shift_all = tiny[:, :, 16:32].reshape(32, 4, 2, 2, 4).transpose(2, 3, 0, 1, 4).reshape(2, 2, 512)
    table_all = tiny[:, :, 32:].transpose(1, 0, 2).reshape(4, 32 * 44)[:, : 2 * 169 * 4]
    table_all = table_all.reshape(4, 2, 169, 4).transpose(1, 2, 0, 3).reshape(2, 169, 16)
    bias, mask, onehot = score_terms(table_all, region, rel_index)
    state, grad, ra, rb, rc, gains, shifts, gbias = core(
        inputs, cotangent, ga, gb, gc, gain_all, shift_all, bias, mask
    )
    tabs = table_grads(gbias, onehot)
    rest = jnp.concatenate(
        [gains.reshape(-1), shifts.reshape(-1), tabs.reshape(-1)]
    )
    rest = jnp.pad(rest, (0, 80 * 128 - rest.shape[0])).reshape(80, 128)
    oa, ob, oc, od = scatter_all(ra, rb, rc, rest)
    od = od.reshape(-1)
    me = (dp * 4 + tp) * 4
    grad_gain = lax.dynamic_slice(od[:2048].reshape(2, 2, 512), (0, 0, me), (2, 2, 4))
    grad_shift = lax.dynamic_slice(od[2048:4096].reshape(2, 2, 512), (0, 0, me), (2, 2, 4))
    grad_tables = lax.dynamic_slice(
        od[4096 : 4096 + 2 * 169 * 16].reshape(2, 169, 16), (0, 0, tp * 4), (2, 169, 4)
    )
    return (
        state,
        grad,
        oa[:, :3].transpose(0, 2, 1, 3),
        oa[:, 3].reshape(2, 4, 512),
        ob.transpose(0, 2, 1, 3).reshape(2, 16, 512),
        oc.transpose(0, 2, 1, 3).reshape(2, 16, 512),
        grad_gain,
        grad_shift,
        grad_tables,
    )


def solution(mesh):
    return jax.shard_map(
        shards,
        mesh=mesh,
        in_specs=(
            P(("dp", "tensor"), None),
            P(None, "dp", None, "tensor"),
            P(None, ("tensor", "dp"), None),
            P(None, "dp", "tensor"),
            P(None, ("tensor", "dp"), None),
            P(None, None, ("dp", "tensor")),
            P(None, None, ("dp", "tensor")),
            P(None, None, "tensor"),
            P(),
            P(),
            P(("dp", "tensor"), None),
        ),
        out_specs=(
            P(("dp", "tensor"), None),
            P(("dp", "tensor"), None),
            P(None, "dp", None, "tensor"),
            P(None, ("tensor", "dp"), None),
            P(None, "dp", "tensor"),
            P(None, ("tensor", "dp"), None),
            P(None, None, ("dp", "tensor")),
            P(None, None, ("dp", "tensor")),
            P(None, None, "tensor"),
        ),
        check_vma=False,
    )
```

```python
import functools
import jax
import jax.numpy as jnp
import numpy as np
from jax import lax
from jax.experimental import pallas as pl
from jax.experimental.pallas import tpu as pltpu
from jax.sharding import PartitionSpec as P

MESH = pl.DeviceIdType.MESH
ORDERS = (("x", "y", "z"), ("y", "z", "x"), ("z", "x", "y"))


def coords():
    dp, tp = lax.axis_index("dp"), lax.axis_index("tensor")
    return {
        "y": dp // 8,
        "x": (dp // 2) % 4,
        "z": (tp // 2) * 2 + dp % 2,
        "c": tp % 2,
    }


def device(at):
    return (at["y"] * 8 + at["x"] * 2 + at["z"] % 2, (at["z"] // 2) * 2 + at["c"])


def moved(at, axis, step):
    size = 2 if axis == "c" else 4
    return device({**at, axis: (at[axis] + step) % size})


NEIGHBOURS = (("x", 1), ("x", 3), ("y", 1), ("y", 3), ("z", 1), ("z", 3), ("c", 1))


def enter(at, peers=NEIGHBOURS):
    barrier = pltpu.get_barrier_semaphore()
    for axis, step in peers:
        pl.semaphore_signal(barrier, inc=1, device_id=moved(at, axis, step), device_id_type=MESH)
    pl.semaphore_wait(barrier, len(peers))


PEERS = NEIGHBOURS + (("x", 2), ("y", 2), ("z", 2))
COPIES = 224


class Copier:
    def __init__(self, at, send, recv):
        self.at, self.send, self.recv, self.made = at, send, recv, []

    def __call__(self, src, dst, axis, step):
        slot = len(self.made)
        copy = pltpu.make_async_remote_copy(
            src_ref=src,
            dst_ref=dst,
            send_sem=self.send.at[slot],
            recv_sem=self.recv.at[slot],
            device_id=moved(self.at, axis, step),
            device_id_type=MESH,
        )
        copy.start()
        self.made.append(copy)
        return copy

    def finish(self):
        for copy in self.made:
            copy.wait_send()


def add_into(dst, *terms):
    lead = dst.shape[:-2]
    count = 1
    for size in lead:
        count *= size

    def body(n, carry):
        index = []
        for size in reversed(lead):
            index.append(n % size)
            n = n // size
        index = tuple(reversed(index)) or slice(None)
        total = dst[index].astype(jnp.float32)
        for term in terms:
            total = total + term[index].astype(jnp.float32)
        dst[index] = total.astype(dst.dtype)
        return carry

    lax.fori_loop(0, count, body, 0)


def half_of(ref, n):
    if len(ref.shape) == 2:
        return ref.at[:, n * 256 : n * 256 + 256]
    return ref.at[2 * n : 2 * n + 2]


def ring_scatter(copy, axis, index, slot, half_r, half_l, full_r, full_l):
    left, right, far = (index + 3) % 4, (index + 1) % 4, (index + 2) % 4
    held = {}

    def first():
        held["r"] = copy(half_of(slot(far), 0), half_r, axis, 1)
        held["l"] = copy(half_of(slot(far), 1), half_l, axis, 3)

    def second():
        held["r"].wait_recv()
        add_into(half_of(slot(right), 0), half_r)
        held["r2"] = copy(slot(right), full_r, axis, 1)
        held["l"].wait_recv()
        add_into(half_of(slot(left), 1), half_l)
        held["l2"] = copy(slot(left), full_l, axis, 3)

    def third():
        held["r2"].wait_recv()
        held["l2"].wait_recv()
        add_into(slot(index), full_r, full_l)

    return first, second, third


def scatter_kernel(ga, gb, gc, d, oa, ob, oc, od, sums, landed, h3, f3, h2, f2, h1, f1, dsum, dland, send, recv, local):
    at = coords()
    core = at["c"]
    copy = Copier(at, send, recv)
    puts = {}
    for layer in (1, 0):
        for family, src in enumerate((ga, gb, gc)):
            put = pltpu.make_async_copy(src.at[layer, core], sums.at[layer, family], local.at[layer * 3 + family])
            put.start()
            puts[layer, family] = put
    enter(at, PEERS)
    plans = {0: [], 1: []}
    for layer in (1, 0):
        for family, src in enumerate((ga, gb, gc)):
            order = ORDERS[family]
            i1, i2, i3 = (at[axis] for axis in order)
            whole = sums.at[layer, family]
            put = puts[layer, family]
            land = landed.at[layer, family]

            def core_first(src=src, land=land, layer=layer, held=None):
                return copy(src.at[layer, 1 - core], land, "c", 1)

            plans[layer].append(
                (
                    core_first,
                    put,
                    whole,
                    land,
                    ring_scatter(
                        copy, order[2], i3, lambda j, w=whole: w.at[j],
                        *(h3.at[layer, family, k] for k in range(2)), *(f3.at[layer, family, k] for k in range(2)),
                    ),
                    ring_scatter(
                        copy, order[1], i2, lambda j, w=whole, p=i3: w.at[p, j],
                        *(h2.at[layer, family, k] for k in range(2)), *(f2.at[layer, family, k] for k in range(2)),
                    ),
                    ring_scatter(
                        copy, order[0], i1, lambda j, w=whole, p=i3, q=i2: w.at[p, q, j],
                        *(h1.at[layer, family, k] for k in range(2)), *(f1.at[layer, family, k] for k in range(2)),
                    ),
                    whole.at[i3, i2, i1],
                )
            )

    def stages(layer):
        crossed = []

        def begin():
            for plan in plans[layer]:
                crossed.append(plan[0]())

        def joined():
            for plan, sent in zip(plans[layer], crossed):
                plan[1].wait()
                sent.wait_recv()
                add_into(plan[2], plan[3])

        def one(phase, step):
            def run():
                for plan in plans[layer]:
                    plan[4 + phase][step]()

            return run

        def last():
            for plan, out in zip(plans[layer], (oa, ob, oc)):
                out[layer] = plan[7][...].astype(jnp.float32)

        return [begin, joined] + [one(phase, step) for phase in range(3) for step in range(3)] + [last]

    dsum[...] = d[...]
    turns = []
    for phase, (axis, size) in enumerate((("c", 2), ("x", 4), ("y", 4), ("z", 4))):
        sent = []

        def start(axis=axis, size=size, phase=phase, sent=sent):
            mine = at[axis]
            dland[phase, mine] = dsum[...]
            for step in range(1, size):
                sent.append(copy(dland.at[phase, mine], dland.at[phase, mine], axis, step))

        def end(size=size, phase=phase, sent=sent):
            for one in sent:
                one.wait_recv()
            total = dland[phase, 0]
            for k in range(1, size):
                total = total + dland[phase, k]
            dsum[...] = total

        turns += [start, end]

    high, low = stages(1), stages(0)
    for step in range(14):
        if step < len(high):
            high[step]()
        if step < len(turns):
            turns[step]()
        if step >= 2:
            low[step - 2]()
    od[...] = dsum[...]
    copy.finish()


def scatter_all(ga, gb, gc, d):
    out = jax.ShapeDtypeStruct((2, 16, 512), jnp.float32)
    bf = jnp.bfloat16
    return pl.pallas_call(
        scatter_kernel,
        out_shape=(out, out, out, jax.ShapeDtypeStruct(d.shape, jnp.float32)),
        in_specs=[pl.BlockSpec(memory_space=pl.ANY)] * 3 + [pl.BlockSpec(memory_space=pltpu.VMEM)],
        out_specs=[pl.BlockSpec(memory_space=pltpu.VMEM)] * 4,
        scratch_shapes=[
            pltpu.VMEM((2, 3, 4, 4, 4, 16, 512), bf),
            pltpu.VMEM((2, 3, 4, 4, 4, 16, 512), bf),
            pltpu.VMEM((2, 3, 2, 2, 4, 16, 512), bf),
            pltpu.VMEM((2, 3, 2, 4, 4, 16, 512), bf),
            pltpu.VMEM((2, 3, 2, 2, 16, 512), bf),
            pltpu.VMEM((2, 3, 2, 4, 16, 512), bf),
            pltpu.VMEM((2, 3, 2, 16, 256), bf),
            pltpu.VMEM((2, 3, 2, 16, 512), bf),
            pltpu.VMEM(d.shape, jnp.float32),
            pltpu.VMEM((4, 4) + d.shape, jnp.float32),
            pltpu.SemaphoreType.DMA((COPIES,)),
            pltpu.SemaphoreType.DMA((COPIES,)),
            pltpu.SemaphoreType.DMA((8,)),
        ],
        compiler_params=pltpu.CompilerParams(
            collective_id=1, has_side_effects=True, vmem_limit_bytes=48 * 2**20
        ),
        name="scatter_grads",
    )(ga, gb, gc, d)


WINDOW = 7
SIDE = 14
EPS = 1e-05


def to_windows(field):
    count, side, _, width = field.shape
    per = side // WINDOW
    field = field.reshape(count, per, WINDOW, per, WINDOW, width).transpose(0, 1, 3, 2, 4, 5)
    return field.reshape(count * per * per, WINDOW * WINDOW, width)


BF, F32 = jnp.bfloat16, jnp.float32
SCALE = 32.0 ** -0.5
ROWS, PADDED, WIDTH = 784, 1024, 512
NN = (((1,), (0,)), ((), ()))
NT = (((1,), (1,)), ((), ()))
TN = (((0,), (0,)), ((), ()))


def mul(a, b, dims=NN):
    return lax.dot_general(a, b, dims, preferred_element_type=F32)


def window_maps():
    maps = np.zeros((2, 2, 512, 400), np.float32)
    for layer in range(2):
        for pair in range(2):
            for image in range(2):
                for window in range(4):
                    for r in range(7):
                        for c in range(7):
                            row = 7 * (window // 2) + r
                            col = 7 * (window % 2) + c
                            if layer:
                                row, col = (row + 3) % 14, (col + 3) % 14
                            to = image * 256 + window * 64 + r * 7 + c
                            maps[layer, pair, to, image * 196 + row * 14 + col + 8 * pair] = 1
    return maps


def proj_maps():
    maps = np.zeros((4, 64, 256), np.float32)
    for q in range(4):
        for dev in range(16):
            for r in range(4):
                maps[q, dev * 4 + r, dev * 16 + r * 4 + q] = 1
    return maps


PLACES = [(y, x, zl) for y in range(4) for x in range(4) for zl in range(2)]


def rows_of(tiles):
    return jnp.concatenate(tiles, axis=0)


def up_block(wb, slot):
    return rows_of([wb[slot, x, zl, y] for y, x, zl in PLACES])


def down_block(wc, slot):
    return rows_of([wc[slot, y, x, zl] for y, x, zl in PLACES])


def qkv_block(ga, layer, s):
    return jnp.concatenate(
        [
            rows_of([ga[layer, t % 2, 2 * (t // 2) + zl, y, x, :, s * 128 : s * 128 + 128] for y, x, zl in PLACES])
            for t in range(4)
        ],
        axis=1,
    )


def norm_parts(values):
    mean = jnp.mean(values, axis=1, keepdims=True)
    centered = values - mean
    r = lax.rsqrt(jnp.mean(centered * centered, axis=1, keepdims=True) + EPS)
    return centered * r, r


def norm_back(grad, values, gain):
    xhat, r = norm_parts(values)
    e = grad * gain
    through = r * (
        e - jnp.mean(e, axis=1, keepdims=True) - xhat * jnp.mean(e * xhat, axis=1, keepdims=True)
    )
    return (
        through,
        jnp.sum(grad * xhat, axis=0, keepdims=True),
        jnp.sum(grad, axis=0, keepdims=True),
    )


C0, C1 = 0.7978845608028654, 0.044715


def gelu(u):
    return 0.5 * u * (1.0 + jnp.tanh(C0 * u * (1.0 + C1 * (u * u))))


def gelu_both(u):
    square = u * u
    t = jnp.tanh(C0 * u * (1.0 + C1 * square))
    half = 0.5 * (1.0 + t)
    slope = half + (0.5 * C0) * u * (1.0 - t * t) * (1.0 + (3.0 * C1) * square)
    return u * half, slope


def to_windows_of(maps, layer, tokens):
    return [mul(maps[layer, pair], tokens[pair * 384 : pair * 384 + 400, :]) for pair in range(2)]


def from_windows_of(maps, layer, rows):
    first = mul(maps[layer, 0], rows[0:512, :], TN)
    second = mul(maps[layer, 1], rows[512:1024, :], TN)
    return jnp.concatenate(
        [first[:384], first[384:400] + second[:16], second[16:]], axis=0
    )


def head_masks():
    lane = lax.broadcasted_iota(jnp.int32, (1, 128), 1) // 32
    return [lane == h for h in range(4)]


def spread(v, masks):
    none = jnp.zeros((64, 128), v.dtype)
    rows = []
    for h in range(8):
        half = h // 4
        part = jnp.where(masks[h % 4], v[:, half * 128 : half * 128 + 128], jnp.zeros((), v.dtype))
        rows.append(jnp.concatenate([none, part] if half else [part, none], axis=1))
    return jnp.concatenate(rows, axis=0)


def fold(r, masks):
    halves = []
    for half in range(2):
        out = None
        for h in range(4):
            at = (half * 4 + h) * 64
            part = r[at : at + 64, half * 128 : half * 128 + 128]
            out = part if out is None else jnp.where(masks[h], part, out)
        halves.append(out)
    return jnp.concatenate(halves, axis=1)


UNROLL = 4


def columns(s, g):
    return slice(s * 512 + g * 256, s * 512 + g * 256 + 256)


def attend(layer, qkv, bias, mask, kept, out):
    masks = head_masks()

    def some(n, carry):
        items = [(n * UNROLL + u, u, g) for u in range(UNROLL) for g in range(2)]

        def rows(w):
            return pl.ds(pl.multiple_of(w * 64, 64), 64)

        scores = [
            mul(qkv[layer, rows(w), columns(1, g)], spread(qkv[layer, rows(w), columns(0, g)], masks), NT)
            for w, u, g in items
        ]
        probs = []
        for (w, u, g), s in zip(items, scores):
            s = s * SCALE + bias[layer, g]
            if layer:
                s = s + mask[u % 4]
            e = jnp.exp(s - jnp.max(s, axis=0, keepdims=True))
            p = (e * (1.0 / jnp.sum(e, axis=0, keepdims=True))).astype(BF)
            kept[layer, w * 2 + g] = p
            probs.append(p)
        for (w, u, g), p in zip(items, probs):
            r = mul(p, qkv[layer, rows(w), columns(2, g)], TN)
            out[rows(w), g * 256 : g * 256 + 256] = fold(r, masks).astype(BF)
        return carry

    lax.fori_loop(0, 16 // UNROLL, some, 0)


def attend_back(layer, qkv, kept, gout, gbias):
    masks = head_masks()

    def some(n, carry):
        items = [(n * UNROLL + u, g) for u in range(UNROLL) for g in range(2)]

        def rows(w):
            return pl.ds(pl.multiple_of(w * 64, 64), 64)

        gprobs, gvs = [], []
        for w, g in items:
            d = spread(gout[rows(w), g * 256 : g * 256 + 256], masks)
            gprobs.append(mul(qkv[layer, rows(w), columns(2, g)], d, NT))
            gvs.append(mul(kept[layer, w * 2 + g], d))
        for (w, g), gv in zip(items, gvs):
            qkv[layer, rows(w), columns(2, g)] = gv.astype(BF)
        gscores = []
        for (w, g), gp in zip(items, gprobs):
            p = kept[layer, w * 2 + g].astype(F32)
            pg = p * gp
            gscores.append(pg - p * jnp.sum(pg, axis=0, keepdims=True))
        for g in range(2):
            total = gbias[layer, g]
            for (w, h), gs in zip(items, gscores):
                if h == g:
                    total = total + gs
            gbias[layer, g] = total
        for (w, g), gs in zip(items, gscores):
            ds = gs.astype(BF)
            q = qkv[layer, rows(w), columns(0, g)]
            k = qkv[layer, rows(w), columns(1, g)]
            gk = mul(ds, spread(q, masks)) * SCALE
            gq = fold(mul(ds, k, TN), masks) * SCALE
            qkv[layer, rows(w), columns(0, g)] = gq.astype(BF)
            qkv[layer, rows(w), columns(1, g)] = gk.astype(BF)
        return carry

    lax.fori_loop(0, 16 // UNROLL, some, 0)


def forward(layer, x, result, gain, shift, ga, feed, wp, maps, bias, mask, s, poll):
    xhat, _ = norm_parts(x[...])
    s.low[...] = (xhat * gain[layer][0] + shift[layer][0]).astype(BF)
    for pair, part in enumerate(to_windows_of(maps, layer, s.low)):
        s.n1w[layer, pair * 512 : pair * 512 + 512, :] = part.astype(BF)
    for k in range(3):
        s.qkv[layer, :, k * 512 : k * 512 + 512] = mul(s.n1w[layer], qkv_block(ga, layer, k)).astype(BF)
    poll()
    attend(layer, s.qkv, bias, mask, s.kept, s.ow)
    poll()
    s.att[layer] = from_windows_of(maps, layer, s.ow).astype(BF)
    s.mid[layer] = x[...] + mul(s.att[layer], wp[layer])
    poll()
    xhat, _ = norm_parts(s.mid[layer])
    s.n2[layer] = (xhat * gain[layer][1] + shift[layer][1]).astype(BF)
    result[...] = s.mid[layer]

    def chunk(t, carry):
        slot = feed.take(t)
        feed.fetch(jnp.where(t == 3, 1, layer), (t + 1) % 4)
        hidden = mul(s.n2[layer], up_block(feed.wb, slot))
        s.hid[layer, t] = hidden.astype(BF)
        result[...] += mul(gelu(hidden).astype(BF), down_block(feed.wc, slot))
        return carry

    lax.fori_loop(0, 4, chunk, 0)


def backward(layer, x, g, gain, ga, feed, ra, rb, rc, wp, maps, pack, dgain, dshift, gbias, s):
    s.low[...] = g[...].astype(BF)
    s.gn[0:ROWS, :] = jnp.zeros((ROWS, WIDTH), F32)

    def chunk(t, carry):
        zh, c = t // 2, t % 2
        slot = feed.take(t)
        if layer:
            feed.fetch(jnp.where(t == 3, 0, 1), (t + 1) % 4)
        else:
            pl.when(t < 3)(lambda: feed.fetch(0, (t + 1) % 4))

        @pl.when(t >= 2)
        def _():
            s.wait_mlp(rb, rc, layer, slot)

        active, slope = gelu_both(s.hid[layer, t].astype(F32))
        gh = (mul(s.low[...], down_block(feed.wc, slot), NT) * slope).astype(BF)
        gdown = mul(active.astype(BF), s.low[...], TN).astype(BF)
        for n, (y, xx, zl) in enumerate(PLACES):
            s.stage_c[slot, y, xx, zl] = gdown[n * 16 : n * 16 + 16]
        gup = mul(s.n2[layer], gh, TN).astype(BF)
        for n, (y, xx, zl) in enumerate(PLACES):
            s.stage_b[slot, xx, zl, y] = gup[n * 16 : n * 16 + 16]
        s.send_mlp(rb, rc, layer, slot, zh, c)
        s.gn[0:ROWS, :] += mul(gh, up_block(feed.wb, slot), NT)
        return carry

    lax.fori_loop(0, 4, chunk, 0)
    for slot in range(2):
        s.wait_mlp(rb, rc, layer, slot)
    through, dg, ds = norm_back(s.gn[0:ROWS, :], s.mid[layer], gain[layer][1])
    dgain[layer, 1:2] = dg
    dshift[layer, 1:2] = ds
    g[...] += through
    s.low[...] = g[...].astype(BF)
    gproj = mul(s.att[layer], s.low[...], TN).astype(BF)
    for block in range(8):
        part = gproj[block * 64 : block * 64 + 64]
        packed = mul(pack[0], part[:, 0:128], TN)
        for q in range(1, 4):
            packed = packed + mul(pack[q], part[:, q * 128 : q * 128 + 128], TN)
        packed = packed.astype(BF)
        for n in range(16):
            dev = block * 16 + n
            t, (y, xx, zl) = dev // 32, PLACES[dev % 32]
            s.stage_a[t % 2, 2 * (t // 2) + zl, y, xx, :, 384:512] = packed[n * 16 : n * 16 + 16]
    for pair, part in enumerate(to_windows_of(maps, layer, s.low)):
        s.ow[pair * 512 : pair * 512 + 512, :] = part.astype(BF)
    s.ow[...] = mul(s.ow[...], wp[layer], NT).astype(BF)
    attend_back(layer, s.qkv, s.kept, s.ow, gbias)
    s.gn[...] = jnp.zeros((PADDED, WIDTH), F32)
    for k in range(3):
        grads = s.qkv[layer, :, k * 512 : k * 512 + 512]
        gw = mul(s.n1w[layer], grads, TN).astype(BF)
        for t in range(4):
            for n, (y, xx, zl) in enumerate(PLACES):
                s.stage_a[t % 2, 2 * (t // 2) + zl, y, xx, :, k * 128 : k * 128 + 128] = gw[
                    n * 16 : n * 16 + 16, t * 128 : t * 128 + 128
                ]
        s.gn[...] += mul(grads, qkv_block(ga, layer, k), NT)
    out = pltpu.make_async_copy(s.stage_a, ra.at[layer], s.sems.at[4])
    out.start()
    s.ow[...] = s.gn[...].astype(BF)
    through, dg, ds = norm_back(from_windows_of(maps, layer, s.ow), x[...], gain[layer][0])
    dgain[layer, 0:1] = dg
    dshift[layer, 0:1] = ds
    g[...] += through
    out.wait()


class Feed:
    def __init__(self, gb, gc, wb, wc, sems):
        self.gb, self.gc, self.wb, self.wc, self.sems = gb, gc, wb, wc, sems

    def copies(self, layer, t):
        slot, z = t % 2, pl.ds(2 * (t // 2), 2)
        return (
            pltpu.make_async_copy(self.gb.at[layer, t % 2, :, z], self.wb.at[slot], self.sems.at[slot]),
            pltpu.make_async_copy(self.gc.at[layer, t % 2, :, :, z], self.wc.at[slot], self.sems.at[2 + slot]),
        )

    def fetch(self, layer, t):
        for one in self.copies(layer, t):
            one.start()

    def take(self, t):
        for one in self.copies(0, t):
            one.wait()
        return t % 2


class Scratch:
    names = ("low", "n1w", "qkv", "kept", "ow", "att", "mid", "n2", "hid", "gn", "stage_a", "stage_b", "stage_c", "sems")

    def __init__(self, refs):
        for name, ref in zip(self.names, refs):
            setattr(self, name, ref)

    @staticmethod
    def shapes():
        return [
            pltpu.VMEM((ROWS, WIDTH), BF),
            pltpu.VMEM((2, PADDED, WIDTH), BF),
            pltpu.VMEM((2, PADDED, 3 * WIDTH), BF),
            pltpu.VMEM((2, 32, 64, 512), BF),
            pltpu.VMEM((PADDED, WIDTH), BF),
            pltpu.VMEM((2, ROWS, WIDTH), BF),
            pltpu.VMEM((2, ROWS, WIDTH), F32),
            pltpu.VMEM((2, ROWS, WIDTH), BF),
            pltpu.VMEM((2, 4, ROWS, WIDTH), BF),
            pltpu.VMEM((PADDED, WIDTH), F32),
            pltpu.VMEM((2, 4, 4, 4, 16, 512), BF),
            pltpu.VMEM((2, 4, 2, 4, 16, 512), BF),
            pltpu.VMEM((2, 4, 4, 2, 16, 512), BF),
            pltpu.SemaphoreType.DMA((8,)),
        ]

    def mlp_copies(self, rb, rc, layer, slot, zh, c):
        z = pl.ds(2 * zh, 2)
        return (
            pltpu.make_async_copy(self.stage_b.at[slot], rb.at[layer, c, :, z], self.sems.at[slot]),
            pltpu.make_async_copy(self.stage_c.at[slot], rc.at[layer, c, :, :, z], self.sems.at[2 + slot]),
        )

    def send_mlp(self, rb, rc, layer, slot, zh, c):
        for one in self.mlp_copies(rb, rc, layer, slot, zh, c):
            one.start()

    def wait_mlp(self, rb, rc, layer, slot):
        for one in self.mlp_copies(rb, rc, layer, slot, 0, 0):
            one.wait()


def axis_slots(whole, i2, i3):
    return (
        lambda j: whole.at[i3, i2, j],
        lambda j: whole.at[i3, j],
        lambda j: whole.at[j],
    )


class Gather:
    def __init__(self, copy, at, wholes):
        self.copy, self.at, self.across = copy, at, []
        self.plans = []
        for order, whole in zip(ORDERS, wholes):
            i1, i2, i3 = (at[axis] for axis in order)
            self.plans.append((order, (i1, i2, i3), axis_slots(whole.at[at["c"]], i2, i3)))
        self.held = [{} for _ in self.plans]
        self.stages = [
            self.first, self.second_start, self.second_forward, self.third_start, self.third_forward,
            self.third_end, self.finish,
        ]

    def pass_on(self, ref):
        self.across.append(self.copy(ref, ref, "c", 1))

    def first(self):
        for (order, (i1, _, _), slots), held in zip(self.plans, self.held):
            held["1"] = [self.copy(slots[0](i1), slots[0](i1), order[0], step) for step in (1, 3, 2)]

    def start(self, phase):
        for (order, places, slots), held in zip(self.plans, self.held):
            for one in held.get("1", ()):
                one.wait_recv()
            held["1"] = ()
            for one in held.get("f", ()):
                one.wait_recv()
            ref = slots[phase](places[phase])
            held["s"] = [self.copy(ref, ref, order[phase], step) for step in (1, 3)]
            if phase == 2:
                self.pass_on(ref)

    def forward(self, phase):
        for (order, places, slots), held in zip(self.plans, self.held):
            held["f"] = []
            for n, (step, back) in enumerate(((1, 3), (3, 1))):
                held["s"][n].wait_recv()
                ref = slots[phase]((places[phase] + back) % 4)
                half = ref.at[2 * n : 2 * n + 2]
                held["f"].append(self.copy(half, half, order[phase], step))
                if phase == 2:
                    self.pass_on(ref)

    def second_start(self):
        self.start(1)

    def second_forward(self):
        self.forward(1)

    def third_start(self):
        self.start(2)

    def third_forward(self):
        self.forward(2)

    def third_end(self):
        for (order, places, slots), held in zip(self.plans, self.held):
            for one in held["f"]:
                one.wait_recv()
            self.pass_on(slots[2]((places[2] + 2) % 4))

    def finish(self):
        for one in self.across:
            one.wait_recv()


def split3(v):
    high = v.astype(BF)
    rest = v - high.astype(F32)
    mid = rest.astype(BF)
    low = (rest - mid.astype(F32)).astype(BF)
    return jnp.concatenate([high, mid, low], axis=0)


def unsplit3(v):
    rows = v.shape[0] // 3
    return v[:rows] + v[rows : 2 * rows] + v[2 * rows :]


def build_bias(tb, rel, bias):
    sides = [split3(jnp.concatenate([tb[t, p] for t in range(4)], axis=0)) for p in range(2)]
    row = lax.broadcasted_iota(jnp.int32, (256, 64), 0)

    def keys(block, carry):
        eight = pl.ds(pl.multiple_of(block * 8, 8), 8)
        named = rel[eight, 0:64]
        both = []
        for k in range(8):
            hot = (row == named[k : k + 1]).astype(F32).astype(BF)
            both.append(jnp.concatenate([unsplit3(mul(side, hot)) for side in sides], axis=1))
        for t in range(4):
            for layer in range(2):
                for m in range(2):
                    n = t * 8 + layer * 2 + m
                    at = (t % 2) * 256 + m * 128
                    bias[layer, t // 2, eight, at : at + 128] = rows_of([one[n : n + 1] for one in both])
        return carry

    lax.fori_loop(0, 7, keys, 0)
    unused = lax.broadcasted_iota(jnp.int32, (16, 512), 0) >= 1
    for layer in range(2):
        for g in range(2):
            bias[layer, g, 48:64] = jnp.where(unused, F32(-1e30), bias[layer, g, 48:64])


def core_kernel(x, cot, a, b, c, tiny, tables, rel, mask, maps, pack,
                out, g, ra, rb, rc, dgain, dshift, gbias, gb, gc,
                ga, wb, wc, x1, wp, bias, vecs, gd, tb, feeds, send, recv, local, *rest):
    at = coords()
    core = at["c"]
    s = Scratch(rest)
    feed = Feed(gb, gc, wb, wc, feeds)
    copy = Copier(at, send, recv)
    own = []

    def place(src, dst):
        put = pltpu.make_async_copy(src, dst, local.at[len(own)])
        put.start()
        own.append(put)

    wholes = [[w.at[layer] for w in (ga, gb, gc)] for layer in range(2)]
    for layer in range(2):
        for order, src, whole in zip(ORDERS, (a, b, c), wholes[layer]):
            i1, i2, i3 = (at[axis] for axis in order)
            place(src.at[layer], whole.at[core, i3, i2, i1])
    start = pltpu.make_async_copy(cot, g, s.sems.at[4])
    start.start()
    gd[core, at["z"], at["y"], at["x"]] = tiny[...]
    mine = (at["z"] // 2) * 2 + core
    tb[mine] = tables[...]
    enter(at, PEERS)
    for put in own:
        put.wait()
    low, high = Gather(copy, at, wholes[0]), Gather(copy, at, wholes[1])
    small = {}

    def small_start(axis, ref):
        steps = (1,) if axis == "c" else (1, 2, 3)
        small[axis] = [copy(ref, ref, axis, step) for step in steps]

    def small_end(axis):
        for one in small[axis]:
            one.wait_recv()

    low.stages[0]()
    small_start("x", gd.at[core, at["z"], at["y"], at["x"]])
    pair = copy(tb.at[mine], tb.at[mine], "z", 2)
    low.stages[1]()
    high.stages[0]()
    small_end("x")
    small_start("y", gd.at[core, at["z"], at["y"]])
    pair.wait_recv()
    other = (mine + 2) % 4
    across = [copy(tb.at[k], tb.at[k], "c", 1) for k in (mine, other)]
    gbias[...] = jnp.zeros(gbias.shape, F32)
    low.stages[2]()
    high.stages[1]()
    small_end("y")
    small_start("z", gd.at[core, at["z"]])
    low.stages[3]()
    high.stages[2]()
    small_end("z")
    small_start("c", gd.at[core])
    for one in across:
        one.wait_recv()
    build_bias(tb, rel, bias)
    low.stages[4]()
    high.stages[3]()
    small_end("c")
    for y in range(4):
        total = gd[0, 0, y, 0]
        for n in range(1, 32):
            total = total + gd[n // 16, n // 4 % 4, y, n % 4]
        vecs[:, y * 128 : y * 128 + 128] = total
    low.stages[5]()
    high.stages[4]()
    low.stages[6]()
    feed.fetch(0, 0)
    gain = [[vecs[l * 2 + k : l * 2 + k + 1] for k in range(2)] for l in range(2)]
    shift = [[vecs[4 + l * 2 + k : 5 + l * 2 + k] for k in range(2)] for l in range(2)]
    start.wait()

    def unpack_proj(layer):
        for block in range(8):
            tiles = []
            for n in range(16):
                dev = block * 16 + n
                t, (y, xx, zl) = dev // 32, PLACES[dev % 32]
                tiles.append(ga[layer, t % 2, 2 * (t // 2) + zl, y, xx, :, 384:512])
            tiles = rows_of(tiles)
            for q in range(4):
                wp[layer, block * 64 : block * 64 + 64, q * 128 : q * 128 + 128] = mul(pack[q], tiles).astype(BF)

    later = high.stages[5:]

    def poll():
        if later:
            later.pop(0)()

    unpack_proj(0)
    forward(0, x, x1, gain, shift, ga, feed, wp, maps, bias, mask, s, poll)
    unpack_proj(1)
    forward(1, x1, out, gain, shift, ga, feed, wp, maps, bias, mask, s, poll)
    backward(1, x1, g, gain, ga, feed, ra, rb, rc, wp, maps, pack, dgain, dshift, gbias, s)
    backward(0, x, g, gain, ga, feed, ra, rb, rc, wp, maps, pack, dgain, dshift, gbias, s)
    copy.finish()


def core(x, cot, a, b, c, tiny, tables, rel, mask):
    maps = jnp.asarray(window_maps(), BF)
    pack = jnp.asarray(proj_maps(), BF)
    tiles = jax.ShapeDtypeStruct((2, 2, 4, 4, 4, 16, 512), BF)
    rows = jax.ShapeDtypeStruct((ROWS, WIDTH), F32)
    vector = jax.ShapeDtypeStruct((2, 2, WIDTH), F32)
    vmem, far = pl.BlockSpec(memory_space=pltpu.VMEM), pl.BlockSpec(memory_space=pl.ANY)
    scores = (2, 2, 64, 512)
    return pl.pallas_call(
        core_kernel,
        out_shape=(rows, rows, tiles, tiles, tiles, vector, vector, jax.ShapeDtypeStruct(scores, F32), tiles, tiles),
        in_specs=[vmem] + [far] * 4 + [vmem] * 6,
        out_specs=[vmem] * 2 + [far] * 3 + [vmem] * 3 + [far] * 2,
        scratch_shapes=[
            pltpu.VMEM(tiles.shape, BF),
            pltpu.VMEM((2, 4, 2, 4, 16, 512), BF),
            pltpu.VMEM((2, 4, 4, 2, 16, 512), BF),
            pltpu.VMEM((ROWS, WIDTH), F32),
            pltpu.VMEM((2, WIDTH, WIDTH), BF),
            pltpu.VMEM(scores, F32),
            pltpu.VMEM((8, WIDTH), F32),
            pltpu.VMEM((2, 4, 4, 4, 8, 128), F32),
            pltpu.VMEM((4, 2, 8, 256), F32),
            pltpu.SemaphoreType.DMA((4,)),
            pltpu.SemaphoreType.DMA((COPIES,)),
            pltpu.SemaphoreType.DMA((COPIES,)),
            pltpu.SemaphoreType.DMA((8,)),
        ] + Scratch.shapes(),
        compiler_params=pltpu.CompilerParams(
            vmem_limit_bytes=63 * 2**20, collective_id=0, has_side_effects=True
        ),
        name="both_blocks",
    )(x, cot, a, b, c, tiny, tables, rel, mask, maps, pack)[:8]


def region_mask(region):
    region_win = to_windows(region.reshape(1, SIDE, SIDE, 1))[..., 0]
    same = region_win[:, :, None] == region_win[:, None, :]
    mask = jnp.where(same, F32(0.0), F32(-1e9))
    mask = jnp.pad(mask, ((0, 0), (0, 15), (0, 15)))
    return jnp.broadcast_to(mask[:, :, None, :], (4, 64, 8, 64)).reshape(4, 64, 512)


def table_grads(gbias, rel_index):
    onehot = (rel_index.T.reshape(-1)[:, None] == jnp.arange(169, dtype=jnp.int32)[None, :]).astype(F32)
    back = gbias.reshape(2, 2, 64, 8, 64)[:, :, :49, :, :49].transpose(2, 4, 0, 1, 3).reshape(2401, 32)
    out = jnp.einsum("pr,ph->rh", onehot, back, precision=lax.Precision.HIGHEST)
    return out.reshape(169, 2, 16).transpose(1, 0, 2)


def pack_shards(w_qkv, w_proj, w_up, w_down):
    qkv = w_qkv.reshape(2, 16, 384)
    proj = w_proj.reshape(2, 16, 128)
    return jnp.concatenate([qkv, proj], axis=2), w_up, w_down


def shards(
    inputs, w_qkv, w_proj, w_up, w_down, ln_gain, ln_shift, tables, region, rel_index, cotangent
):
    dp, tp = lax.axis_index("dp"), lax.axis_index("tensor")
    a, b, c = pack_shards(w_qkv, w_proj, w_up, w_down)
    eight = jnp.concatenate([ln_gain.reshape(4, 4), ln_shift.reshape(4, 4)], axis=0)
    here = jnp.arange(128, dtype=jnp.int32) // 4 == (dp * 4 + tp) % 32
    tiny = jnp.where(here[None], jnp.tile(eight, (1, 32)), F32(0.0))
    tabs = tables.reshape(2, 169, 2, 2).transpose(3, 0, 2, 1).reshape(2, 4, 169)
    tabs = jnp.pad(tabs, ((0, 0), (0, 4), (0, 87)))
    rel = jnp.pad(rel_index.T, ((0, 15), (0, 79)), constant_values=-1)
    state, grad, ra, rb, rc, gains, shifts, gbias = core(
        inputs, cotangent, a, b, c, tiny, tabs, rel, region_mask(region)
    )
    tabs = table_grads(gbias, rel_index)
    rest = jnp.concatenate([gains.reshape(-1), shifts.reshape(-1), tabs.reshape(-1)])
    rest = jnp.pad(rest, (0, 80 * 128 - rest.shape[0])).reshape(80, 128)
    oa, ob, oc, od = scatter_all(ra, rb, rc, rest)
    od = od.reshape(-1)
    me = (dp * 4 + tp) * 4
    grad_gain = lax.dynamic_slice(od[:2048].reshape(2, 2, 512), (0, 0, me), (2, 2, 4))
    grad_shift = lax.dynamic_slice(od[2048:4096].reshape(2, 2, 512), (0, 0, me), (2, 2, 4))
    grad_tables = lax.dynamic_slice(
        od[4096 : 4096 + 2 * 169 * 16].reshape(2, 169, 16), (0, 0, tp * 4), (2, 169, 4)
    )
    return (
        state,
        grad,
        oa[:, :, :384].reshape(2, 16, 3, 128),
        oa[:, :, 384:].reshape(2, 4, 512),
        ob,
        oc,
        grad_gain,
        grad_shift,
        grad_tables,
    )


def solution(mesh):
    return jax.shard_map(
        shards,
        mesh=mesh,
        in_specs=(
            P(("dp", "tensor"), None),
            P(None, "dp", None, "tensor"),
            P(None, ("tensor", "dp"), None),
            P(None, "dp", "tensor"),
            P(None, ("tensor", "dp"), None),
            P(None, None, ("dp", "tensor")),
            P(None, None, ("dp", "tensor")),
            P(None, None, "tensor"),
            P(),
            P(),
            P(("dp", "tensor"), None),
        ),
        out_specs=(
            P(("dp", "tensor"), None),
            P(("dp", "tensor"), None),
            P(None, "dp", None, "tensor"),
            P(None, ("tensor", "dp"), None),
            P(None, "dp", "tensor"),
            P(None, ("tensor", "dp"), None),
            P(None, None, ("dp", "tensor")),
            P(None, None, ("dp", "tensor")),
            P(None, None, "tensor"),
        ),
        check_vma=False,
    )
```

```python
import functools
import jax
import jax.numpy as jnp
import numpy as np
from jax import lax
from jax.experimental import pallas as pl
from jax.experimental.pallas import tpu as pltpu
from jax.sharding import PartitionSpec as P

MESH = pl.DeviceIdType.MESH
ORDERS = (("x", "y", "z"), ("y", "z", "x"), ("z", "x", "y"))


def coords():
    dp, tp = lax.axis_index("dp"), lax.axis_index("tensor")
    return {
        "y": dp // 8,
        "x": (dp // 2) % 4,
        "z": (tp // 2) * 2 + dp % 2,
        "c": tp % 2,
    }


def device(at):
    return (at["y"] * 8 + at["x"] * 2 + at["z"] % 2, (at["z"] // 2) * 2 + at["c"])


def moved(at, axis, step):
    size = 2 if axis == "c" else 4
    return device({**at, axis: (at[axis] + step) % size})


NEIGHBOURS = (("x", 1), ("x", 3), ("y", 1), ("y", 3), ("z", 1), ("z", 3), ("c", 1))


def enter(at, peers=NEIGHBOURS):
    barrier = pltpu.get_barrier_semaphore()
    for axis, step in peers:
        pl.semaphore_signal(barrier, inc=1, device_id=moved(at, axis, step), device_id_type=MESH)
    pl.semaphore_wait(barrier, len(peers))


PEERS = NEIGHBOURS + (("x", 2), ("y", 2), ("z", 2))
COPIES = 256


class Copier:
    def __init__(self, at, send, recv):
        self.at, self.send, self.recv, self.made = at, send, recv, []

    def __call__(self, src, dst, axis, step):
        slot = len(self.made)
        copy = pltpu.make_async_remote_copy(
            src_ref=src,
            dst_ref=dst,
            send_sem=self.send.at[slot],
            recv_sem=self.recv.at[slot],
            device_id=moved(self.at, axis, step),
            device_id_type=MESH,
        )
        copy.start()
        self.made.append(copy)
        return copy

    def finish(self):
        for copy in self.made:
            copy.wait_send()


def add_into(dst, *terms):
    lead = dst.shape[:-3]
    count = 1
    for size in lead:
        count *= size

    def body(n, carry):
        index = []
        for size in reversed(lead):
            index.append(n % size)
            n = n // size
        index = tuple(reversed(index)) or slice(None)
        total = dst[index].astype(jnp.float32)
        for term in terms:
            total = total + term[index].astype(jnp.float32)
        dst[index] = total.astype(dst.dtype)
        return carry

    if count == 1:
        body(0, 0)
    else:
        lax.fori_loop(0, count, body, 0)


class Scatter:
    def __init__(self, copy, at, families, crossing):
        self.copy, self.at, self.families, self.crossing = copy, at, families, crossing
        self.held = [{} for _ in families]
        self.stages = [self.join, self.along, self.second, self.third, self.finish]

    def places(self, family):
        i1, i2, i3 = (self.at[axis] for axis in family["order"])
        return i1, i2, i3

    def join(self):
        for n, (family, held) in enumerate(zip(self.families, self.held)):
            self.crossing(n)
            _, _, i3 = self.places(family)
            axis, sums, landed = family["order"][2], family["sums"], family["landed"]
            far = (i3 + 2) % 4
            add_into(sums.at[far], landed.at[far])
            held["r"] = self.copy(sums.at[far, 0:2], family["half"].at[0], axis, 1)
            held["l"] = self.copy(sums.at[far, 2:4], family["half"].at[1], axis, 3)
        for family in self.families:
            _, _, i3 = self.places(family)
            for step in (1, 3, 0):
                j = (i3 + step) % 4
                add_into(family["sums"].at[j], family["landed"].at[j])

    def along(self):
        for family, held in zip(self.families, self.held):
            _, _, i3 = self.places(family)
            axis, sums = family["order"][2], family["sums"]
            right, left = (i3 + 1) % 4, (i3 + 3) % 4
            held["r"].wait_recv()
            add_into(sums.at[right, 0:2], family["half"].at[0])
            held["r2"] = self.copy(sums.at[right], family["full"].at[0], axis, 1)
            held["l"].wait_recv()
            add_into(sums.at[left, 2:4], family["half"].at[1])
            held["l2"] = self.copy(sums.at[left], family["full"].at[1], axis, 3)

    def second(self):
        for family, held in zip(self.families, self.held):
            _, i2, i3 = self.places(family)
            axis, sums = family["order"][1], family["sums"]
            held["r2"].wait_recv()
            held["l2"].wait_recv()
            add_into(sums.at[i3], family["full"].at[0], family["full"].at[1])
            held["2"] = [
                self.copy(sums.at[i3, (i2 + step) % 4], family["two"].at[step - 1], axis, step) for step in (2, 1, 3)
            ]

    def third(self):
        for family, held in zip(self.families, self.held):
            i1, i2, i3 = self.places(family)
            axis, sums = family["order"][0], family["sums"]
            for one in held["2"]:
                one.wait_recv()
            add_into(sums.at[i3, i2], *(family["two"].at[k] for k in range(3)))
            held["1"] = [
                self.copy(sums.at[i3, i2, (i1 + step) % 4], family["one"].at[step - 1], axis, step)
                for step in (2, 1, 3)
            ]

    def finish(self):
        for family, held in zip(self.families, self.held):
            i1, i2, i3 = self.places(family)
            for one in held["1"]:
                one.wait_recv()
            total = family["sums"][i3, i2, i1].astype(jnp.float32)
            for k in range(3):
                total = total + family["one"][k].astype(jnp.float32)
            family["out"](total)


def landing_shapes(width):
    bf = jnp.bfloat16
    return {
        "landed": pltpu.VMEM((4, 4, 4, 16, width), bf),
        "half": pltpu.VMEM((2, 2, 4, 16, width), bf),
        "full": pltpu.VMEM((2, 4, 4, 16, width), bf),
        "two": pltpu.VMEM((3, 4, 16, width), bf),
        "one": pltpu.VMEM((3, 16, width), bf),
    }


WINDOW = 7
SIDE = 14
EPS = 1e-05


def to_windows(field):
    count, side, _, width = field.shape
    per = side // WINDOW
    field = field.reshape(count, per, WINDOW, per, WINDOW, width).transpose(0, 1, 3, 2, 4, 5)
    return field.reshape(count * per * per, WINDOW * WINDOW, width)


BF, F32 = jnp.bfloat16, jnp.float32
SCALE = 32.0 ** -0.5
ROWS, PADDED, WIDTH = 784, 1024, 512
NN = (((1,), (0,)), ((), ()))
NT = (((1,), (1,)), ((), ()))
TN = (((0,), (0,)), ((), ()))


def mul(a, b, dims=NN):
    return lax.dot_general(a, b, dims, preferred_element_type=F32)


def window_maps():
    maps = np.zeros((2, 2, 512, 400), np.float32)
    for layer in range(2):
        for pair in range(2):
            for image in range(2):
                for window in range(4):
                    for r in range(7):
                        for c in range(7):
                            row = 7 * (window // 2) + r
                            col = 7 * (window % 2) + c
                            if layer:
                                row, col = (row + 3) % 14, (col + 3) % 14
                            to = image * 256 + window * 64 + r * 7 + c
                            maps[layer, pair, to, image * 196 + row * 14 + col + 8 * pair] = 1
    return maps


def proj_maps():
    maps = np.zeros((4, 64, 256), np.float32)
    for q in range(4):
        for dev in range(16):
            for r in range(4):
                maps[q, dev * 4 + r, dev * 16 + r * 4 + q] = 1
    return maps


PLACES = [(y, x, zl) for y in range(4) for x in range(4) for zl in range(2)]


def rows_of(tiles):
    return jnp.concatenate(tiles, axis=0)


def up_block(wb, slot):
    return rows_of([wb[slot, x, zl, y] for y, x, zl in PLACES])


def down_block(wc, slot):
    return rows_of([wc[slot, y, x, zl] for y, x, zl in PLACES])


def qkv_block(ga, layer, s):
    return jnp.concatenate(
        [
            rows_of([ga[layer, t % 2, 2 * (t // 2) + zl, y, x, :, s * 128 : s * 128 + 128] for y, x, zl in PLACES])
            for t in range(4)
        ],
        axis=1,
    )


def norm_parts(values):
    mean = jnp.mean(values, axis=1, keepdims=True)
    centered = values - mean
    r = lax.rsqrt(jnp.mean(centered * centered, axis=1, keepdims=True) + EPS)
    return centered * r, r


def norm_back(grad, values, gain):
    xhat, r = norm_parts(values)
    e = grad * gain
    through = r * (
        e - jnp.mean(e, axis=1, keepdims=True) - xhat * jnp.mean(e * xhat, axis=1, keepdims=True)
    )
    return (
        through,
        jnp.sum(grad * xhat, axis=0, keepdims=True),
        jnp.sum(grad, axis=0, keepdims=True),
    )


C0, C1 = 0.7978845608028654, 0.044715


def gelu(u):
    return 0.5 * u * (1.0 + jnp.tanh(C0 * u * (1.0 + C1 * (u * u))))


def gelu_both(u):
    square = u * u
    t = jnp.tanh(C0 * u * (1.0 + C1 * square))
    half = 0.5 * (1.0 + t)
    slope = half + (0.5 * C0) * u * (1.0 - t * t) * (1.0 + (3.0 * C1) * square)
    return u * half, slope


def to_windows_of(maps, layer, tokens):
    return [mul(maps[layer, pair], tokens[pair * 384 : pair * 384 + 400, :]) for pair in range(2)]


def from_windows_of(maps, layer, rows):
    first = mul(maps[layer, 0], rows[0:512, :], TN)
    second = mul(maps[layer, 1], rows[512:1024, :], TN)
    return jnp.concatenate(
        [first[:384], first[384:400] + second[:16], second[16:]], axis=0
    )


def head_masks():
    lane = lax.broadcasted_iota(jnp.int32, (1, 128), 1) // 32
    return [lane == h for h in range(4)]


def spread(v, masks):
    none = jnp.zeros((64, 128), v.dtype)
    rows = []
    for h in range(8):
        half = h // 4
        part = jnp.where(masks[h % 4], v[:, half * 128 : half * 128 + 128], jnp.zeros((), v.dtype))
        rows.append(jnp.concatenate([none, part] if half else [part, none], axis=1))
    return jnp.concatenate(rows, axis=0)


def fold(r, masks):
    halves = []
    for half in range(2):
        out = None
        for h in range(4):
            at = (half * 4 + h) * 64
            part = r[at : at + 64, half * 128 : half * 128 + 128]
            out = part if out is None else jnp.where(masks[h], part, out)
        halves.append(out)
    return jnp.concatenate(halves, axis=1)


UNROLL = 4


def columns(s, g):
    return slice(s * 512 + g * 256, s * 512 + g * 256 + 256)


def attend(layer, qkv, bias, mask, kept, out):
    masks = head_masks()

    def some(n, carry):
        items = [(n * UNROLL + u, u, g) for u in range(UNROLL) for g in range(2)]

        def rows(w):
            return pl.ds(pl.multiple_of(w * 64, 64), 64)

        scores = [
            mul(qkv[rows(w), columns(1, g)], spread(qkv[rows(w), columns(0, g)], masks), NT)
            for w, u, g in items
        ]
        probs = []
        for (w, u, g), s in zip(items, scores):
            s = s * SCALE + bias[layer, g]
            if layer:
                s = s + mask[u % 4]
            e = jnp.exp(s - jnp.max(s, axis=0, keepdims=True))
            p = (e * (1.0 / jnp.sum(e, axis=0, keepdims=True))).astype(BF)
            kept[w * 2 + g] = p
            probs.append(p)
        for (w, u, g), p in zip(items, probs):
            r = mul(p, qkv[rows(w), columns(2, g)], TN)
            out[rows(w), g * 256 : g * 256 + 256] = fold(r, masks).astype(BF)
        return carry

    lax.fori_loop(0, 16 // UNROLL, some, 0)


def attend_back(layer, qkv, kept, gout, gbias, part):
    masks = head_masks()

    def some(n, carry):
        items = [(n * UNROLL + u, g) for u in range(UNROLL) for g in range(2)]

        def rows(w):
            return pl.ds(pl.multiple_of(w * 64, 64), 64)

        gprobs, gvs = [], []
        for w, g in items:
            d = spread(gout[rows(w), g * 256 : g * 256 + 256], masks)
            gprobs.append(mul(qkv[rows(w), columns(2, g)], d, NT))
            gvs.append(mul(kept[w * 2 + g], d))
        for (w, g), gv in zip(items, gvs):
            qkv[rows(w), columns(2, g)] = gv.astype(BF)
        gscores = []
        for (w, g), gp in zip(items, gprobs):
            p = kept[w * 2 + g].astype(F32)
            pg = p * gp
            gscores.append(pg - p * jnp.sum(pg, axis=0, keepdims=True))
        for g in range(2):
            total = gbias[layer, g]
            for (w, h), gs in zip(items, gscores):
                if h == g:
                    total = total + gs
            gbias[layer, g] = total
        for (w, g), gs in zip(items, gscores):
            ds = gs.astype(BF)
            q = qkv[rows(w), columns(0, g)]
            k = qkv[rows(w), columns(1, g)]
            gk = mul(ds, spread(q, masks)) * SCALE
            gq = fold(mul(ds, k, TN), masks) * SCALE
            qkv[rows(w), columns(0, g)] = gq.astype(BF)
            qkv[rows(w), columns(1, g)] = gk.astype(BF)
        return carry

    lax.fori_loop(part * 8 // UNROLL, (part + 1) * 8 // UNROLL, some, 0)


SPILLED = ("n1w", "qkv", "kept", "att", "mid", "n2", "hid")


def forward(layer, x, result, gain, shift, ga, feed, wp, maps, bias, mask, s, poll):
    def ready(name):
        if layer:
            s.spilled(name)

    def done(name):
        if not layer:
            s.spill(name)

    xhat, _ = norm_parts(x[...])
    s.low[...] = (xhat * gain[layer][0] + shift[layer][0]).astype(BF)
    ready("n1w")
    for pair, part in enumerate(to_windows_of(maps, layer, s.low)):
        s.n1w[pair * 512 : pair * 512 + 512, :] = part.astype(BF)
    done("n1w")
    ready("qkv")
    for k in range(3):
        s.qkv[:, k * 512 : k * 512 + 512] = mul(s.n1w[...], qkv_block(ga, layer, k)).astype(BF)
    done("qkv")
    poll()
    ready("kept")
    attend(layer, s.qkv, bias, mask, s.kept, s.ow)
    done("kept")
    poll()
    ready("att")
    s.att[...] = from_windows_of(maps, layer, s.ow).astype(BF)
    done("att")
    ready("mid")
    s.mid[...] = x[...] + mul(s.att[...], wp[layer])
    done("mid")
    poll()
    ready("n2")
    xhat, _ = norm_parts(s.mid[...])
    s.n2[...] = (xhat * gain[layer][1] + shift[layer][1]).astype(BF)
    done("n2")
    result[...] = s.mid[...]
    ready("hid")

    def chunk(t, carry):
        slot = feed.take(t)

        @pl.when(t < 3)
        def _():
            feed.fetch(layer, t + 1, t + 1)

        if layer:
            pl.when(t == 3)(lambda: feed.fetch(1, feed.turn(1, 0), 0))
        else:
            pl.when(t == 3)(lambda: feed.fetch(1, 0, 0))
        hidden = mul(s.n2[...], up_block(feed.wb, slot))
        s.hid[t] = hidden.astype(BF)
        result[...] += mul(gelu(hidden).astype(BF), down_block(feed.wc, slot))
        return carry

    lax.fori_loop(0, 4, chunk, 0)
    done("hid")


def backward_mlp(layer, g, gain, feed, s, vec, send_grads, wait_grads, poll):
    if not layer:
        s.returned("hid")
        s.returned("n2")
    s.low[...] = g[...].astype(BF)
    s.gn[0:ROWS, :] = jnp.zeros((ROWS, WIDTH), F32)

    def chunk(n, carry):
        t = feed.turn(layer, n)
        slot = feed.take(n)

        @pl.when(n < 3)
        def _():
            feed.fetch(layer, feed.turn(layer, n + 1), n + 1)

        if layer:
            pl.when(n == 3)(lambda: feed.fetch(0, feed.turn(0, 0), 0))

        active, slope = gelu_both(s.hid[t].astype(F32))
        gh = (mul(s.low[...], down_block(feed.wc, slot), NT) * slope).astype(BF)
        pl.when(n >= 2)(lambda: wait_grads(n - 2))
        gdown = mul(active.astype(BF), s.low[...], TN).astype(BF)
        for k, (y, xx, zl) in enumerate(PLACES):
            s.stage_c[slot, y, xx, zl] = gdown[k * 16 : k * 16 + 16]
        gup = mul(s.n2[...], gh, TN).astype(BF)
        for k, (y, xx, zl) in enumerate(PLACES):
            s.stage_b[slot, xx, zl, y] = gup[k * 16 : k * 16 + 16]
        send_grads(n)
        s.gn[0:ROWS, :] += mul(gh, up_block(feed.wb, slot), NT)
        return carry

    lax.fori_loop(0, 2, chunk, 0)
    poll("chunks")
    lax.fori_loop(2, 4, chunk, 0)
    wait_grads(jnp.int32(2))
    wait_grads(jnp.int32(3))
    poll("feed_forward")
    if layer:
        s.bring("hid")
        s.bring("n2")
    else:
        s.returned("mid")
    through, dg, ds = norm_back(s.gn[0:ROWS, :], s.mid[...], gain[layer][1])
    vec[layer * 2 + 1 : layer * 2 + 2] = dg
    vec[layer * 2 + 5 : layer * 2 + 6] = ds
    if layer:
        s.bring("mid")
    g[...] += through


def backward_heads(layer, x, g, gain, ga, wp, maps, pack, gbias, s, vec, both, poll, cross):
    def slot(k, dev):
        t, (y, xx, zl) = dev // 32, PLACES[dev % 32]
        at = {"x": xx, "y": y, "z": 2 * (t // 2) + zl}
        return (t % 2,) + tuple(at[axis] for axis in reversed(ORDERS[k]))

    s.low[...] = g[...].astype(BF)
    if not layer:
        s.returned("att")
    gproj = mul(s.att[...], s.low[...], TN).astype(BF)
    if layer:
        s.bring("att")
    for block in range(8):
        part = gproj[block * 64 : block * 64 + 64]
        packed = mul(pack[0], part[:, 0:128], TN)
        for q in range(1, 4):
            packed = packed + mul(pack[q], part[:, q * 128 : q * 128 + 128], TN)
        packed = packed.astype(BF)
        for n in range(16):
            both[2][slot(2, block * 16 + n) + (slice(None), slice(128, 256))] = packed[n * 16 : n * 16 + 16]
    poll("proj")
    for pair, part in enumerate(to_windows_of(maps, layer, s.low)):
        s.ow[pair * 512 : pair * 512 + 512, :] = part.astype(BF)
    s.ow[...] = mul(s.ow[...], wp[layer], NT).astype(BF)
    poll("gatt")
    if not layer:
        s.returned("qkv")
        s.returned("kept")
    attend_back(layer, s.qkv, s.kept, s.ow, gbias, 0)
    poll("half_scores")
    attend_back(layer, s.qkv, s.kept, s.ow, gbias, 1)
    if layer:
        s.bring("kept")
    poll("scores")
    if not layer:
        s.returned("n1w")
    for k in range(3):
        gw = mul(s.n1w[...], s.qkv[:, k * 512 : k * 512 + 512], TN).astype(BF)
        for dev in range(128):
            t, n = dev // 32, dev % 32
            both[k][slot(k, dev) + (slice(None), slice(0, 128))] = gw[n * 16 : n * 16 + 16, t * 128 : t * 128 + 128]
        cross(k)
    poll("qkv")
    if layer:
        s.bring("n1w")
    total = mul(s.qkv[:, 0:512], qkv_block(ga, layer, 0), NT)
    for k in range(1, 3):
        total = total + mul(s.qkv[:, k * 512 : k * 512 + 512], qkv_block(ga, layer, k), NT)
    s.ow[...] = total.astype(BF)
    if layer:
        s.bring("qkv")
    poll("gn1")
    through, dg, ds = norm_back(from_windows_of(maps, layer, s.ow), x[...], gain[layer][0])
    vec[layer * 2 : layer * 2 + 1] = dg
    vec[layer * 2 + 4 : layer * 2 + 5] = ds
    g[...] += through
    poll("end")


class Feed:
    def __init__(self, core, gb, gc, wb, wc, sems):
        self.core, self.gb, self.gc, self.wb, self.wc, self.sems = core, gb, gc, wb, wc, sems

    def turn(self, layer, n):
        mine = self.core if layer == 0 else 1 - self.core
        first = jnp.where(n < 2, mine, 1 - mine)
        return 2 * (n % 2) + first

    def copies(self, layer, t, n):
        slot, z = n % 2, pl.ds(2 * (t // 2), 2)
        return (
            pltpu.make_async_copy(self.gb.at[layer, t % 2, :, z], self.wb.at[slot], self.sems.at[slot]),
            pltpu.make_async_copy(self.gc.at[layer, t % 2, :, :, z], self.wc.at[slot], self.sems.at[2 + slot]),
        )

    def fetch(self, layer, t, n):
        for one in self.copies(layer, t, n):
            one.start()

    def take(self, n):
        for one in self.copies(0, 0, n):
            one.wait()
        return n % 2


class Scratch:
    shapes = {
        "low": pltpu.VMEM((ROWS, WIDTH), BF),
        "n1w": pltpu.VMEM((PADDED, WIDTH), BF),
        "qkv": pltpu.VMEM((PADDED, 3 * WIDTH), BF),
        "kept": pltpu.VMEM((32, 64, 512), BF),
        "ow": pltpu.VMEM((PADDED, WIDTH), BF),
        "att": pltpu.VMEM((ROWS, WIDTH), BF),
        "mid": pltpu.VMEM((ROWS, WIDTH), F32),
        "n2": pltpu.VMEM((ROWS, WIDTH), BF),
        "hid": pltpu.VMEM((4, ROWS, WIDTH), BF),
        "gn": pltpu.VMEM((ROWS, WIDTH), F32),
        "stage_b": pltpu.VMEM((2, 4, 2, 4, 16, 512), BF),
        "stage_c": pltpu.VMEM((2, 4, 4, 2, 16, 512), BF),
    }

    def __init__(self, refs, far, sems):
        self.__dict__.update(refs)
        self.far, self.sems = far, sems

    def out_copy(self, name):
        return pltpu.make_async_copy(getattr(self, name), self.far[name], self.sems.at[SPILLED.index(name)])

    def in_copy(self, name):
        return pltpu.make_async_copy(self.far[name], getattr(self, name), self.sems.at[SPILLED.index(name)])

    def spill(self, name):
        self.out_copy(name).start()

    def spilled(self, name):
        self.out_copy(name).wait()

    def bring(self, name):
        self.in_copy(name).start()

    def returned(self, name):
        self.in_copy(name).wait()


def axis_slots(whole, i2, i3):
    return (
        lambda j: whole.at[i3, i2, j],
        lambda j: whole.at[i3, j],
        lambda j: whole.at[j],
    )


class Gather:
    def __init__(self, copy, at, wholes):
        self.copy, self.at, self.across = copy, at, []
        self.plans = []
        for order, whole in zip(ORDERS, wholes):
            i1, i2, i3 = (at[axis] for axis in order)
            self.plans.append((order, (i1, i2, i3), axis_slots(whole.at[at["c"]], i2, i3)))
        self.held = [{} for _ in self.plans]
        self.stages = [
            self.first, self.second_start, self.second_forward, self.third_start, self.third_forward,
            self.third_end, self.finish,
        ]

    def pass_on(self, ref):
        self.across.append(self.copy(ref, ref, "c", 1))

    def first(self):
        for (order, (i1, _, _), slots), held in zip(self.plans, self.held):
            held["1"] = [self.copy(slots[0](i1), slots[0](i1), order[0], step) for step in (1, 3, 2)]

    def start(self, phase):
        for (order, places, slots), held in zip(self.plans, self.held):
            for one in held.get("1", ()):
                one.wait_recv()
            held["1"] = ()
            for one in held.get("f", ()):
                one.wait_recv()
            ref = slots[phase](places[phase])
            held["s"] = [self.copy(ref, ref, order[phase], step) for step in (1, 3)]
            if phase == 2:
                self.pass_on(ref)

    def forward(self, phase):
        for (order, places, slots), held in zip(self.plans, self.held):
            held["f"] = []
            for n, (step, back) in enumerate(((1, 3), (3, 1))):
                held["s"][n].wait_recv()
                ref = slots[phase]((places[phase] + back) % 4)
                half = ref.at[2 * n : 2 * n + 2]
                held["f"].append(self.copy(half, half, order[phase], step))
                if phase == 2:
                    self.pass_on(ref)

    def second_start(self):
        self.start(1)

    def second_forward(self):
        self.forward(1)

    def third_start(self):
        self.start(2)

    def third_forward(self):
        self.forward(2)

    def third_end(self):
        for (order, places, slots), held in zip(self.plans, self.held):
            for one in held["f"]:
                one.wait_recv()
            self.pass_on(slots[2]((places[2] + 2) % 4))

    def finish(self):
        for one in self.across:
            one.wait_recv()


def split3(v):
    high = v.astype(BF)
    rest = v - high.astype(F32)
    mid = rest.astype(BF)
    low = (rest - mid.astype(F32)).astype(BF)
    return jnp.concatenate([high, mid, low], axis=0)


def unsplit3(v):
    rows = v.shape[0] // 3
    return v[:rows] + v[rows : 2 * rows] + v[2 * rows :]


def build_bias(tb, rel, bias):
    sides = [split3(jnp.concatenate([tb[t, p] for t in range(4)], axis=0)) for p in range(2)]
    row = lax.broadcasted_iota(jnp.int32, (256, 64), 0)

    def keys(block, carry):
        eight = pl.ds(pl.multiple_of(block * 8, 8), 8)
        named = rel[eight, 0:64]
        both = []
        for k in range(8):
            hot = (row == named[k : k + 1]).astype(F32).astype(BF)
            both.append(jnp.concatenate([unsplit3(mul(side, hot)) for side in sides], axis=1))
        for t in range(4):
            for layer in range(2):
                for m in range(2):
                    n = t * 8 + layer * 2 + m
                    at = (t % 2) * 256 + m * 128
                    bias[layer, t // 2, eight, at : at + 128] = rows_of([one[n : n + 1] for one in both])
        return carry

    lax.fori_loop(0, 7, keys, 0)
    unused = lax.broadcasted_iota(jnp.int32, (16, 512), 0) >= 1
    for layer in range(2):
        for g in range(2):
            bias[layer, g, 48:64] = jnp.where(unused, F32(-1e30), bias[layer, g, 48:64])


def table_sums(gbias, rel, tab):
    row = lax.broadcasted_iota(jnp.int32, (512, 128), 0)
    lane = lax.broadcasted_iota(jnp.int32, (512, 128), 1)
    side = row // 256 == lane // 64
    named_row = jnp.where(side, row % 256, -2)
    none = jnp.zeros((4, 128), F32)

    def keys(block, total):
        eight = pl.ds(pl.multiple_of(block * 8, 8), 8)
        named = rel[eight, :]
        parts = {}
        for t in range(4):
            for layer in range(2):
                for m in range(2):
                    at = (t % 2) * 256 + m * 128
                    parts[t, layer, m] = gbias[layer, t // 2, eight, at : at + 128]
        for k in range(8):
            hot = (named_row == named[k : k + 1]).astype(F32).astype(BF)
            rows = []
            for t in range(4):
                rows += [parts[t, layer, m][k : k + 1] for layer in range(2) for m in range(2)] + [none]
            total = total + unsplit3(mul(split3(rows_of(rows)), hot, NT))
        return total

    total = lax.fori_loop(0, 7, keys, jnp.zeros((32, 512), F32))
    for t in range(4):
        tab[t % 2, t // 2] = total[t * 8 : t * 8 + 8]


class Sums:
    def __init__(self, copy, at, phases):
        self.stages = []
        sent = []

        def start(axis, size, part, landing):
            mine = at[axis]
            landing[mine] = (part(mine) if callable(part) else part)[...]
            for step in range(1, size):
                src = part((mine + step) % size) if callable(part) else landing.at[mine]
                sent.append(copy(src, landing.at[mine], axis, step))

        def end(size, landing, keep):
            while sent:
                sent.pop().wait_recv()
            total = landing[0]
            for k in range(1, size):
                total = total + landing[k]
            keep(total)

        for n, (axis, size, part, landing, keep) in enumerate(phases):
            before = phases[n - 1] if n else None

            def stage(axis=axis, size=size, part=part, landing=landing, before=before):
                if before:
                    end(before[1], before[3], before[4])
                start(axis, size, part, landing)

            self.stages.append(stage)
        last = phases[-1]
        self.stages.append(lambda: end(last[1], last[3], last[4]))


FAMILIES = ((ORDERS[0], 128), (ORDERS[1], 128), (ORDERS[2], 256), (ORDERS[1], 512), (ORDERS[2], 512))


def scratch_list():
    tiles = (2, 2, 4, 4, 4, 16, 512)
    one = (4, 4, 4, 16)
    shapes = {
        "ga": pltpu.VMEM(tiles, BF),
        "wb": pltpu.VMEM((2, 4, 2, 4, 16, 512), BF),
        "wc": pltpu.VMEM((2, 4, 4, 2, 16, 512), BF),
        "x1": pltpu.VMEM((ROWS, WIDTH), F32),
        "wp": pltpu.VMEM((2, WIDTH, WIDTH), BF),
        "bias": pltpu.VMEM((2, 2, 64, 512), F32),
        "gbias": pltpu.VMEM((2, 2, 64, 512), F32),
        "vecs": pltpu.VMEM((8, WIDTH), F32),
        "vec": pltpu.VMEM((8, WIDTH), F32),
        "gd": pltpu.VMEM((2, 4, 4, 4, 8, 128), F32),
        "tb": pltpu.VMEM((4, 2, 8, 256), F32),
        "tab": pltpu.VMEM((2, 2, 8, 512), F32),
        "vec_sum": pltpu.VMEM((8, 128), F32),
        "vec_land": pltpu.VMEM((4, 4, 8, 128), F32),
        "tab_pair": pltpu.VMEM((2, 8, 512), F32),
        "tab_sum": pltpu.VMEM((8, 512), F32),
        "tab_cross": pltpu.VMEM((2, 2, 8, 512), F32),
        "tab_land": pltpu.VMEM((3, 4, 8, 512), F32),
        "feeds": pltpu.SemaphoreType.DMA((4,)),
        "send": pltpu.SemaphoreType.DMA((COPIES,)),
        "recv": pltpu.SemaphoreType.DMA((COPIES,)),
        "local": pltpu.SemaphoreType.DMA((12,)),
        "spills": pltpu.SemaphoreType.DMA((len(SPILLED),)),
        "cross_send": pltpu.SemaphoreType.DMA((8,)),
        "cross_recv": pltpu.SemaphoreType.DMA((8,)),
    }
    for k in range(3):
        width = FAMILIES[k][1]
        for layer in range(2):
            shapes[f"both{k}_{layer}"] = pltpu.VMEM((2,) + one + (width,), BF)
            for name, shape in landing_shapes(width).items():
                shapes[f"{name}{k}_{layer}"] = shape
    for k in (3, 4):
        for layer in range(2):
            shapes[f"sums{k}_{layer}"] = pltpu.VMEM(one + (512,), BF)
        for name, shape in landing_shapes(512).items():
            shapes[f"{name}{k}"] = shape
    shapes.update(Scratch.shapes)
    return shapes


def core_kernel(x, cot, a, b, c, tiny, tables, rel, mask, maps, pack, out, g, oa, ob, oc, ovec, otab, gb, gc, *rest):
    far, rest = dict(zip(SPILLED, rest[: len(SPILLED)])), rest[len(SPILLED) :]
    r = dict(zip(scratch_list(), rest))
    at = coords()
    core = at["c"]
    s = Scratch({name: r[name] for name in Scratch.shapes}, far, r["spills"])
    ga, wp, gd, tb, local, vec = r["ga"], r["wp"], r["gd"], r["tb"], r["local"], r["vec"]
    feed = Feed(core, gb, gc, r["wb"], r["wc"], r["feeds"])
    copy = Copier(at, r["send"], r["recv"])
    own = []

    def place(src, dst):
        put = pltpu.make_async_copy(src, dst, local.at[len(own)])
        put.start()
        own.append(put)

    wholes = [[w.at[layer] for w in (ga, gb, gc)] for layer in range(2)]
    for layer in range(2):
        for order, src, whole in zip(ORDERS, (a, b, c), wholes[layer]):
            i1, i2, i3 = (at[axis] for axis in order)
            place(src.at[layer], whole.at[core, i3, i2, i1])
    start = pltpu.make_async_copy(cot, g, local.at[8])
    start.start()
    gd[core, at["z"], at["y"], at["x"]] = tiny[...]
    mine = (at["z"] // 2) * 2 + core
    tb[mine] = tables[...]
    enter(at, PEERS)
    for put in own:
        put.wait()
    low, high = Gather(copy, at, wholes[0]), Gather(copy, at, wholes[1])
    small = {}

    def small_start(axis, ref):
        steps = (1,) if axis == "c" else (1, 2, 3)
        small[axis] = [copy(ref, ref, axis, step) for step in steps]

    def small_end(axis):
        for one in small[axis]:
            one.wait_recv()

    low.stages[0]()
    small_start("x", gd.at[core, at["z"], at["y"], at["x"]])
    pair = copy(tb.at[mine], tb.at[mine], "z", 2)
    low.stages[1]()
    high.stages[0]()
    small_end("x")
    small_start("y", gd.at[core, at["z"], at["y"]])
    pair.wait_recv()
    other = (mine + 2) % 4
    across = [copy(tb.at[k], tb.at[k], "c", 1) for k in (mine, other)]
    r["gbias"][...] = jnp.zeros(r["gbias"].shape, F32)
    low.stages[2]()
    high.stages[1]()
    small_end("y")
    small_start("z", gd.at[core, at["z"]])
    low.stages[3]()
    high.stages[2]()
    small_end("z")
    small_start("c", gd.at[core])
    for one in across:
        one.wait_recv()
    build_bias(tb, rel, r["bias"])
    low.stages[4]()
    high.stages[3]()
    small_end("c")
    vecs = r["vecs"]
    for y in range(4):
        total = gd[0, 0, y, 0]
        for n in range(1, 32):
            total = total + gd[n // 16, n // 4 % 4, y, n % 4]
        vecs[:, y * 128 : y * 128 + 128] = total
    low.stages[5]()
    high.stages[4]()
    low.stages[6]()
    feed.fetch(0, 0, 0)
    gain = [[vecs[l * 2 + k : l * 2 + k + 1] for k in range(2)] for l in range(2)]
    shift = [[vecs[4 + l * 2 + k : 5 + l * 2 + k] for k in range(2)] for l in range(2)]
    start.wait()

    def unpack_proj(layer):
        for block in range(8):
            tiles = []
            for n in range(16):
                dev = block * 16 + n
                t, (y, xx, zl) = dev // 32, PLACES[dev % 32]
                tiles.append(ga[layer, t % 2, 2 * (t // 2) + zl, y, xx, :, 384:512])
            tiles = rows_of(tiles)
            for q in range(4):
                wp[layer, block * 64 : block * 64 + 64, q * 128 : q * 128 + 128] = mul(pack[q], tiles).astype(BF)

    later = high.stages[5:]

    def poll():
        if later:
            later.pop(0)()

    unpack_proj(0)
    x1 = r["x1"]
    forward(0, x, x1, gain, shift, ga, feed, wp, maps, r["bias"], mask, s, poll)
    unpack_proj(1)
    forward(1, x1, out, gain, shift, ga, feed, wp, maps, r["bias"], mask, s, poll)

    def chunk_part(ref, k, n):
        z = pl.ds(2 * (n % 2), 2)
        return ref.at[:, z] if k == 3 else ref.at[:, :, z]

    def chunk_over(k, n):
        sem = (k - 3) * 4 + n
        return pltpu.make_async_remote_copy(
            src_ref=(s.stage_b if k == 3 else s.stage_c).at[n % 2],
            dst_ref=chunk_part(r[f"landed{k}"], k, n),
            send_sem=r["cross_send"].at[sem],
            recv_sem=r["cross_recv"].at[sem],
            device_id=moved(at, "c", 1),
            device_id_type=MESH,
        )

    def chunk_here(layer, k, n):
        src = (s.stage_b if k == 3 else s.stage_c).at[n % 2]
        return pltpu.make_async_copy(
            src, chunk_part(r[f"sums{k}_{layer}"], k, n), r["cross_send"].at[(k - 3) * 4 + n]
        )

    def grads_of(layer):
        first = 0 if layer else 2

        def away(n):
            return jnp.logical_and(n >= first, n < first + 2)

        def send_grads(n):
            for k in (3, 4):
                pl.when(away(n))(lambda k=k: chunk_over(k, n).start())
                pl.when(jnp.logical_not(away(n)))(lambda k=k: chunk_here(layer, k, n).start())

        def wait_grads(n):
            for k in (3, 4):
                pl.when(away(n))(lambda k=k: chunk_over(k, n).wait_send())
                pl.when(jnp.logical_not(away(n)))(lambda k=k: chunk_here(layer, k, n).wait())

        def arrived(k):
            for n in (first, first + 1):
                chunk_over(k, n).wait_recv()

        return send_grads, wait_grads, arrived

    def out_of(ref, layer, lanes):
        def put(total):
            ref[layer, :, lanes] = total

        return put

    def feed_forward_scatter(layer):
        families = []
        for k, ref in ((3, ob), (4, oc)):
            family = {name: r[f"{name}{k}"] for name in landing_shapes(512)}
            family.update(order=FAMILIES[k][0], sums=r[f"sums{k}_{layer}"], out=out_of(ref, layer, slice(0, 512)))
            families.append(family)
        arrived = grads_of(layer)[2]
        return Scatter(copy, at, families, lambda n: arrived(n + 3))

    def heads_scatter(layer):
        families, crossing = [], []
        lanes = (slice(0, 128), slice(128, 256), slice(256, 512))
        for k in range(3):
            family = {name: r[f"{name}{k}_{layer}"] for name in landing_shapes(128)}
            both = r[f"both{k}_{layer}"]
            family.update(order=FAMILIES[k][0], sums=both.at[core], out=out_of(oa, layer, lanes[k]))
            families.append(family)

        def cross(k):
            crossing.append(copy(r[f"both{k}_{layer}"].at[1 - core], r[f"landed{k}_{layer}"], "c", 1))

        return Scatter(copy, at, families, lambda n: crossing[n].wait_recv()), cross

    wide = {layer: feed_forward_scatter(layer) for layer in (0, 1)}
    heads = {layer: heads_scatter(layer) for layer in (0, 1)}
    tab, tab_pair, tab_sum, vec_sum = r["tab"], r["tab_pair"], r["tab_sum"], r["vec_sum"]
    vec_land, tab_cross, tab_land = r["vec_land"], r["tab_cross"], r["tab_land"]

    def keep_in(ref):
        def keep(total):
            ref[...] = total

        return keep

    vec_sums = Sums(
        copy,
        at,
        [
            ("y", 4, lambda j: vec.at[:, pl.ds(pl.multiple_of(j * 128, 128), 128)], vec_land.at[0], keep_in(vec_sum)),
            ("x", 4, vec_sum, vec_land.at[1], keep_in(vec_sum)),
            ("z", 4, vec_sum, vec_land.at[2], keep_in(vec_sum)),
            ("c", 2, vec_sum, vec_land.at[3], keep_in(ovec)),
        ],
    )
    tab_sums = Sums(
        copy,
        at,
        [
            ("c", 2, lambda j: tab.at[j], tab_cross, keep_in(tab_pair)),
            ("z", 4, lambda j: tab_pair.at[j // 2], tab_land.at[0], keep_in(tab_sum)),
            ("x", 4, tab_sum, tab_land.at[1], keep_in(tab_sum)),
            ("y", 4, tab_sum, tab_land.at[2], keep_in(otab)),
        ],
    )

    def tables_done():
        table_sums(r["gbias"], rel, tab)

    def stage(sums, n):
        return lambda: sums.stages[n]()

    high_wide, low_wide, high_heads, low_heads = wide[1], wide[0], heads[1][0], heads[0][0]
    plans = {
        1: {
            "feed_forward": [stage(high_wide, 0)],
            "half_scores": [stage(high_wide, 1)],
            "end": [stage(high_wide, 2)],
        },
        0: {
            "chunks": [stage(high_wide, 3), stage(high_heads, 0)],
            "feed_forward": [stage(high_heads, 1), stage(low_wide, 0), stage(high_wide, 4)],
            "half_scores": [stage(high_heads, 2), stage(low_wide, 1)],
            "scores": [tables_done, stage(tab_sums, 0), stage(high_heads, 3)],
            "qkv": [stage(tab_sums, 1), stage(low_wide, 2), stage(high_heads, 4)],
            "gn1": [stage(low_heads, 0), stage(tab_sums, 2)],
            "end": [
                stage(vec_sums, 0),
                stage(low_heads, 1),
                stage(tab_sums, 3),
                stage(vec_sums, 1),
                stage(low_wide, 3),
                stage(low_heads, 2),
                stage(tab_sums, 4),
                stage(vec_sums, 2),
                stage(low_wide, 4),
                stage(low_heads, 3),
                stage(vec_sums, 3),
                stage(low_heads, 4),
                stage(vec_sums, 4),
            ],
        },
    }
    for layer, before in ((1, x1), (0, x)):

        def poll(name, plan=plans[layer]):
            for one in plan.get(name, ()):
                one()

        send, wait, _ = grads_of(layer)
        backward_mlp(layer, g, gain, feed, s, vec, send, wait, poll)
        backward_heads(
            layer, before, g, gain, ga, wp, maps, pack, r["gbias"], s, vec,
            [r[f"both{k}_{layer}"] for k in range(3)], poll, heads[layer][1],
        )
    copy.finish()


def core(x, cot, a, b, c, tiny, tables, rel, mask):
    maps = jnp.asarray(window_maps(), BF)
    pack = jnp.asarray(proj_maps(), BF)
    tiles = jax.ShapeDtypeStruct((2, 2, 4, 4, 4, 16, 512), BF)
    rows = jax.ShapeDtypeStruct((ROWS, WIDTH), F32)
    shard = jax.ShapeDtypeStruct((2, 16, 512), F32)
    vmem, far = pl.BlockSpec(memory_space=pltpu.VMEM), pl.BlockSpec(memory_space=pl.ANY)
    spills = [jax.ShapeDtypeStruct(Scratch.shapes[name].shape, Scratch.shapes[name].dtype) for name in SPILLED]
    return pl.pallas_call(
        core_kernel,
        out_shape=[rows, rows, shard, shard, shard]
        + [jax.ShapeDtypeStruct((8, 128), F32), jax.ShapeDtypeStruct((8, 512), F32), tiles, tiles]
        + spills,
        in_specs=[vmem] + [far] * 4 + [vmem] * 6,
        out_specs=[vmem] * 7 + [far] * (2 + len(spills)),
        scratch_shapes=list(scratch_list().values()),
        compiler_params=pltpu.CompilerParams(
            vmem_limit_bytes=63 * 2**20, collective_id=0, has_side_effects=True
        ),
        name="both_blocks",
    )(x, cot, a, b, c, tiny, tables, rel, mask, maps, pack)[:7]


def region_mask(region):
    region_win = to_windows(region.reshape(1, SIDE, SIDE, 1))[..., 0]
    same = region_win[:, :, None] == region_win[:, None, :]
    mask = jnp.where(same, F32(0.0), F32(-1e9))
    mask = jnp.pad(mask, ((0, 0), (0, 15), (0, 15)))
    return jnp.broadcast_to(mask[:, :, None, :], (4, 64, 8, 64)).reshape(4, 64, 512)


def pack_shards(w_qkv, w_proj, w_up, w_down):
    qkv = w_qkv.reshape(2, 16, 384)
    proj = w_proj.reshape(2, 16, 128)
    return jnp.concatenate([qkv, proj], axis=2), w_up, w_down


def shards(
    inputs, w_qkv, w_proj, w_up, w_down, ln_gain, ln_shift, tables, region, rel_index, cotangent
):
    dp, tp = lax.axis_index("dp"), lax.axis_index("tensor")
    a, b, c = pack_shards(w_qkv, w_proj, w_up, w_down)
    eight = jnp.concatenate([ln_gain.reshape(4, 4), ln_shift.reshape(4, 4)], axis=0)
    here = jnp.arange(128, dtype=jnp.int32) // 4 == (dp * 4 + tp) % 32
    tiny = jnp.where(here[None], jnp.tile(eight, (1, 32)), F32(0.0))
    tabs = tables.reshape(2, 169, 2, 2).transpose(3, 0, 2, 1).reshape(2, 4, 169)
    tabs = jnp.pad(tabs, ((0, 0), (0, 4), (0, 87)))
    rel = jnp.pad(rel_index.T, ((0, 15), (0, 15)), constant_values=-1)
    rel = jnp.concatenate([rel, rel], axis=1)
    state, grad, oa, ob, oc, vec, tab = core(
        inputs, cotangent, a, b, c, tiny, tabs, rel, region_mask(region)
    )
    mine = lax.dynamic_slice(vec, (0, 4 * ((dp * 4 + tp) % 32)), (8, 4))
    grad_tables = tab[:4].reshape(2, 2, 2, 256)[..., :169].transpose(0, 3, 1, 2).reshape(2, 169, 4)
    return (
        state,
        grad,
        oa[:, :, :384].reshape(2, 16, 3, 128),
        oa[:, :, 384:].reshape(2, 4, 512),
        ob,
        oc,
        mine[:4].reshape(2, 2, 4),
        mine[4:].reshape(2, 2, 4),
        grad_tables,
    )


def solution(mesh):
    return jax.shard_map(
        shards,
        mesh=mesh,
        in_specs=(
            P(("dp", "tensor"), None),
            P(None, "dp", None, "tensor"),
            P(None, ("tensor", "dp"), None),
            P(None, "dp", "tensor"),
            P(None, ("tensor", "dp"), None),
            P(None, None, ("dp", "tensor")),
            P(None, None, ("dp", "tensor")),
            P(None, None, "tensor"),
            P(),
            P(),
            P(("dp", "tensor"), None),
        ),
        out_specs=(
            P(("dp", "tensor"), None),
            P(("dp", "tensor"), None),
            P(None, "dp", None, "tensor"),
            P(None, ("tensor", "dp"), None),
            P(None, "dp", "tensor"),
            P(None, ("tensor", "dp"), None),
            P(None, None, ("dp", "tensor")),
            P(None, None, ("dp", "tensor")),
            P(None, None, "tensor"),
        ),
        check_vma=False,
    )
```

```python
import functools
import jax
import jax.numpy as jnp
from jax import lax
from jax.experimental import pallas as pl
from jax.experimental.pallas import tpu as pltpu
from jax.sharding import PartitionSpec as P

MESH = pl.DeviceIdType.MESH
ORDERS = (("x", "y", "z"), ("y", "z", "x"), ("z", "x", "y"))


def coords():
    dp, tp = lax.axis_index("dp"), lax.axis_index("tensor")
    return {
        "y": dp // 8,
        "x": (dp // 2) % 4,
        "z": (tp // 2) * 2 + dp % 2,
        "c": tp % 2,
    }


def device(at):
    return (at["y"] * 8 + at["x"] * 2 + at["z"] % 2, (at["z"] // 2) * 2 + at["c"])


def moved(at, axis, step):
    size = 2 if axis == "c" else 4
    return device({**at, axis: (at[axis] + step) % size})


NEIGHBOURS = (("x", 1), ("x", 3), ("y", 1), ("y", 3), ("z", 1), ("z", 3), ("c", 1))


def enter(at, peers=NEIGHBOURS):
    barrier = pltpu.get_barrier_semaphore()
    for axis, step in peers:
        pl.semaphore_signal(barrier, inc=1, device_id=moved(at, axis, step), device_id_type=MESH)
    pl.semaphore_wait(barrier, len(peers))


PEERS = NEIGHBOURS + (("x", 2), ("y", 2), ("z", 2))
COPIES = 320


class Copier:
    def __init__(self, at, send, recv):
        self.at, self.send, self.recv, self.made = at, send, recv, []

    def __call__(self, src, dst, axis, step):
        slot = len(self.made)
        assert slot < COPIES
        copy = pltpu.make_async_remote_copy(
            src_ref=src,
            dst_ref=dst,
            send_sem=self.send.at[slot],
            recv_sem=self.recv.at[slot],
            device_id=moved(self.at, axis, step),
            device_id_type=MESH,
        )
        copy.start()
        self.made.append(copy)
        return copy

    def finish(self):
        for copy in self.made:
            copy.wait_send()


def add_into(dst, *terms):
    lead = dst.shape[:-3]
    count = 1
    for size in lead:
        count *= size

    def body(n, carry):
        index = []
        for size in reversed(lead):
            index.append(n % size)
            n = n // size
        index = tuple(reversed(index)) or slice(None)
        total = dst[index].astype(jnp.float32)
        for term in terms:
            total = total + term[index].astype(jnp.float32)
        dst[index] = total.astype(dst.dtype)
        return carry

    if count == 1:
        body(0, 0)
    else:
        lax.fori_loop(0, count, body, 0)


class Scatter:
    def __init__(self, copy, at, families, crossing):
        self.copy, self.at, self.families, self.crossing = copy, at, families, crossing
        self.held = [{} for _ in families]
        self.stages = [self.join, self.along, self.second, self.third, self.finish]

    def places(self, family):
        i1, i2, i3 = (self.at[axis] for axis in family["order"])
        return i1, i2, i3

    def join(self):
        for n, (family, held) in enumerate(zip(self.families, self.held)):
            self.crossing(n)
            _, _, i3 = self.places(family)
            axis, sums, landed = family["order"][2], family["sums"], family["landed"]
            far = (i3 + 2) % 4
            add_into(sums.at[far], landed.at[far])
            held["r"] = self.copy(sums.at[far, 0:2], family["half"].at[0], axis, 1)
            held["l"] = self.copy(sums.at[far, 2:4], family["half"].at[1], axis, 3)
        for family in self.families:
            _, _, i3 = self.places(family)
            for step in (1, 3, 0):
                j = (i3 + step) % 4
                add_into(family["sums"].at[j], family["landed"].at[j])

    def along(self):
        for family, held in zip(self.families, self.held):
            _, _, i3 = self.places(family)
            axis, sums = family["order"][2], family["sums"]
            right, left = (i3 + 1) % 4, (i3 + 3) % 4
            held["r"].wait_recv()
            add_into(sums.at[right, 0:2], family["half"].at[0])
            held["r2"] = self.copy(sums.at[right], family["full"].at[0], axis, 1)
            held["l"].wait_recv()
            add_into(sums.at[left, 2:4], family["half"].at[1])
            held["l2"] = self.copy(sums.at[left], family["full"].at[1], axis, 3)

    def second(self):
        for family, held in zip(self.families, self.held):
            _, i2, i3 = self.places(family)
            axis, sums = family["order"][1], family["sums"]
            held["r2"].wait_recv()
            held["l2"].wait_recv()
            add_into(sums.at[i3], family["full"].at[0], family["full"].at[1])
            held["2"] = [
                self.copy(sums.at[i3, (i2 + step) % 4], family["two"].at[step - 1], axis, step) for step in (2, 1, 3)
            ]

    def third(self):
        for family, held in zip(self.families, self.held):
            i1, i2, i3 = self.places(family)
            axis, sums = family["order"][0], family["sums"]
            for one in held["2"]:
                one.wait_recv()
            add_into(sums.at[i3, i2], *(family["two"].at[k] for k in range(3)))
            held["1"] = [
                self.copy(sums.at[i3, i2, (i1 + step) % 4], family["one"].at[step - 1], axis, step)
                for step in (2, 1, 3)
            ]

    def finish(self):
        for family, held in zip(self.families, self.held):
            i1, i2, i3 = self.places(family)
            for one in held["1"]:
                one.wait_recv()
            total = family["sums"][i3, i2, i1].astype(jnp.float32)
            for k in range(3):
                total = total + family["one"][k].astype(jnp.float32)
            family["out"](total)


def landing_shapes(width):
    bf = jnp.bfloat16
    return {
        "landed": pltpu.VMEM((4, 4, 4, 16, width), bf),
        "half": pltpu.VMEM((2, 2, 4, 16, width), bf),
        "full": pltpu.VMEM((2, 4, 4, 16, width), bf),
        "two": pltpu.VMEM((3, 4, 16, width), bf),
        "one": pltpu.VMEM((3, 16, width), bf),
    }


WINDOW = 7
SIDE = 14
EPS = 1e-05


BF, F32 = jnp.bfloat16, jnp.float32
SCALE = 32.0 ** -0.5
ROWS, PADDED, WIDTH = 784, 1024, 512
NN = (((1,), (0,)), ((), ()))
NT = (((1,), (1,)), ((), ()))
TN = (((0,), (0,)), ((), ()))


def mul(a, b, dims=NN):
    return lax.dot_general(a, b, dims, preferred_element_type=F32)


def window_maps(maps):
    n = lax.broadcasted_iota(jnp.int32, (512, 1), 0)
    place = n % 64
    token = lax.broadcasted_iota(jnp.int32, (512, 400), 1)
    for layer in range(2):
        row = n // 128 % 2 * 7 + place // 7
        col = n // 64 % 2 * 7 + place % 7
        if layer:
            row, col = (row + 3) % 14, (col + 3) % 14
        taken = jnp.where(place < 49, n // 256 * 196 + row * 14 + col, -100)
        for pair in range(2):
            maps[layer, pair] = (token == taken + 8 * pair).astype(F32).astype(BF)


def proj_maps(pack):
    n = lax.broadcasted_iota(jnp.int32, (64, 1), 0)
    packed = lax.broadcasted_iota(jnp.int32, (64, 256), 1)
    for q in range(4):
        pack[q] = (packed == n // 4 * 16 + n % 4 * 4 + q).astype(F32).astype(BF)


PLACES = [(y, x, zl) for y in range(4) for x in range(4) for zl in range(2)]


def rows_of(tiles):
    return jnp.concatenate(tiles, axis=0)


def up_block(wb, slot):
    return rows_of([wb[slot, x, zl, y] for y, x, zl in PLACES])


def down_block(wc, slot):
    return rows_of([wc[slot, y, x, zl] for y, x, zl in PLACES])


def slot_of(k, dev):
    t, (y, x, zl) = dev // 32, PLACES[dev % 32]
    at = {"x": x, "y": y, "z": 2 * (t // 2) + zl}
    return (t % 2,) + tuple(at[axis] for axis in reversed(ORDERS[k]))


def qkv_block(ga, layer, s):
    return jnp.concatenate(
        [rows_of([ga[s][(layer,) + slot_of(s, t * 32 + n)] for n in range(32)]) for t in range(4)], axis=1
    )


def norm_parts(values):
    mean = jnp.mean(values, axis=1, keepdims=True)
    centered = values - mean
    r = lax.rsqrt(jnp.mean(centered * centered, axis=1, keepdims=True) + EPS)
    return centered * r, r


def norm_back(grad, values, gain):
    xhat, r = norm_parts(values)
    e = grad * gain
    through = r * (
        e - jnp.mean(e, axis=1, keepdims=True) - xhat * jnp.mean(e * xhat, axis=1, keepdims=True)
    )
    return (
        through,
        jnp.sum(grad * xhat, axis=0, keepdims=True),
        jnp.sum(grad, axis=0, keepdims=True),
    )


C0, C1 = 0.7978845608028654, 0.044715


def gelu(u):
    return 0.5 * u * (1.0 + jnp.tanh(C0 * u * (1.0 + C1 * (u * u))))


def gelu_both(u):
    square = u * u
    t = jnp.tanh(C0 * u * (1.0 + C1 * square))
    half = 0.5 * (1.0 + t)
    slope = half + (0.5 * C0) * u * (1.0 - t * t) * (1.0 + (3.0 * C1) * square)
    return u * half, slope


def to_windows_of(maps, layer, tokens):
    return [mul(maps[layer, pair], tokens[pair * 384 : pair * 384 + 400, :]) for pair in range(2)]


def from_windows_of(maps, layer, rows):
    first = mul(maps[layer, 0], rows[0:512, :], TN)
    second = mul(maps[layer, 1], rows[512:1024, :], TN)
    return jnp.concatenate(
        [first[:384], first[384:400] + second[:16], second[16:]], axis=0
    )


def head_masks():
    lane = lax.broadcasted_iota(jnp.int32, (1, 128), 1) // 32
    return [lane == h for h in range(4)]


def spread(v, masks):
    none = jnp.zeros((64, 128), v.dtype)
    rows = []
    for h in range(8):
        half = h // 4
        part = jnp.where(masks[h % 4], v[:, half * 128 : half * 128 + 128], jnp.zeros((), v.dtype))
        rows.append(jnp.concatenate([none, part] if half else [part, none], axis=1))
    return jnp.concatenate(rows, axis=0)


def fold(r, masks):
    halves = []
    for half in range(2):
        out = None
        for h in range(4):
            at = (half * 4 + h) * 64
            part = r[at : at + 64, half * 128 : half * 128 + 128]
            out = part if out is None else jnp.where(masks[h], part, out)
        halves.append(out)
    return jnp.concatenate(halves, axis=1)


UNROLL = 4


def columns(s, g):
    return slice(s * 512 + g * 256, s * 512 + g * 256 + 256)


def attend(layer, qkv, bias, mask, kept, out, part):
    masks = head_masks()

    def some(n, carry):
        items = [(n * UNROLL + u, u, g) for u in range(UNROLL) for g in range(2)]

        def rows(w):
            return pl.ds(pl.multiple_of(w * 64, 64), 64)

        scores = [
            mul(qkv[rows(w), columns(1, g)], spread(qkv[rows(w), columns(0, g)], masks), NT)
            for w, u, g in items
        ]
        probs = []
        for (w, u, g), s in zip(items, scores):
            s = s * SCALE + bias[layer, g]
            if layer:
                s = s + mask[u % 4]
            e = jnp.exp(s - jnp.max(s, axis=0, keepdims=True))
            p = (e * (1.0 / jnp.sum(e, axis=0, keepdims=True))).astype(BF)
            kept[w * 2 + g] = p
            probs.append(p)
        for (w, u, g), p in zip(items, probs):
            r = mul(p, qkv[rows(w), columns(2, g)], TN)
            out[rows(w), g * 256 : g * 256 + 256] = fold(r, masks).astype(BF)
        return carry

    lax.fori_loop(part * 8 // UNROLL, (part + 1) * 8 // UNROLL, some, 0)


def attend_back(layer, qkv, kept, gout, gbias, part):
    masks = head_masks()

    def some(n, carry):
        items = [(n * UNROLL + u, g) for u in range(UNROLL) for g in range(2)]

        def rows(w):
            return pl.ds(pl.multiple_of(w * 64, 64), 64)

        gprobs, gvs = [], []
        for w, g in items:
            d = spread(gout[rows(w), g * 256 : g * 256 + 256], masks)
            gprobs.append(mul(qkv[rows(w), columns(2, g)], d, NT))
            gvs.append(mul(kept[w * 2 + g], d))
        for (w, g), gv in zip(items, gvs):
            qkv[rows(w), columns(2, g)] = gv.astype(BF)
        gscores = []
        for (w, g), gp in zip(items, gprobs):
            p = kept[w * 2 + g].astype(F32)
            pg = p * gp
            gscores.append(pg - p * jnp.sum(pg, axis=0, keepdims=True))
        for g in range(2):
            total = gbias[layer, g]
            for (w, h), gs in zip(items, gscores):
                if h == g:
                    total = total + gs
            gbias[layer, g] = total
        for (w, g), gs in zip(items, gscores):
            ds = gs.astype(BF)
            q = qkv[rows(w), columns(0, g)]
            k = qkv[rows(w), columns(1, g)]
            gk = mul(ds, spread(q, masks)) * SCALE
            gq = fold(mul(ds, k, TN), masks) * SCALE
            qkv[rows(w), columns(0, g)] = gq.astype(BF)
            qkv[rows(w), columns(1, g)] = gk.astype(BF)
        return carry

    lax.fori_loop(part * 8 // UNROLL, (part + 1) * 8 // UNROLL, some, 0)


SPILLED = ("n1w", "qkv", "kept", "att", "mid", "n2", "hid")


def forward(layer, x, result, gain, shift, ga, feed, wp, maps, bias, mask, s, poll):
    def ready(name):
        if layer:
            s.spilled(name)

    def done(name):
        if not layer:
            s.spill(name)

    xhat, _ = norm_parts(x[...])
    s.low[...] = (xhat * gain[layer][0] + shift[layer][0]).astype(BF)
    ready("n1w")
    for pair, part in enumerate(to_windows_of(maps, layer, s.low)):
        s.n1w[pair * 512 : pair * 512 + 512, :] = part.astype(BF)
    done("n1w")
    ready("qkv")
    for k in range(3):
        s.qkv[:, k * 512 : k * 512 + 512] = mul(s.n1w[...], qkv_block(ga, layer, k)).astype(BF)
    done("qkv")
    poll("qkv")
    ready("kept")
    attend(layer, s.qkv, bias, mask, s.kept, s.ow, 0)
    poll("half_scores")
    attend(layer, s.qkv, bias, mask, s.kept, s.ow, 1)
    done("kept")
    poll("scores")
    ready("att")
    s.att[...] = from_windows_of(maps, layer, s.ow).astype(BF)
    done("att")
    ready("mid")
    s.mid[...] = x[...] + mul(s.att[...], wp[layer])
    done("mid")
    poll("feed_forward")
    feed.fetch(layer, 0, 0)
    ready("n2")
    xhat, _ = norm_parts(s.mid[...])
    s.n2[...] = (xhat * gain[layer][1] + shift[layer][1]).astype(BF)
    done("n2")
    result[...] = s.mid[...]
    ready("hid")

    def chunk(t, carry):
        slot = feed.take(t)

        @pl.when(t < 3)
        def _():
            feed.fetch(layer, t + 1, t + 1)

        if layer:
            pl.when(t == 3)(lambda: feed.fetch(1, feed.turn(1, 0), 0))
        hidden = mul(s.n2[...], up_block(feed.wb, slot))
        s.hid[t] = hidden.astype(BF)
        result[...] += mul(gelu(hidden).astype(BF), down_block(feed.wc, slot))
        return carry

    lax.fori_loop(0, 2, chunk, 0)
    poll("chunks")
    lax.fori_loop(2, 4, chunk, 0)
    done("hid")
    poll("end")


def backward_mlp(layer, g, gain, feed, s, vec, send_grads, wait_grads, poll):
    if not layer:
        s.returned("hid")
        s.returned("n2")
    s.low[...] = g[...].astype(BF)
    s.gn[0:ROWS, :] = jnp.zeros((ROWS, WIDTH), F32)

    def chunk(n, carry):
        t = feed.turn(layer, n)
        slot = feed.take(n)

        @pl.when(n < 3)
        def _():
            feed.fetch(layer, feed.turn(layer, n + 1), n + 1)

        if layer:
            pl.when(n == 3)(lambda: feed.fetch(0, feed.turn(0, 0), 0))

        active, slope = gelu_both(s.hid[t].astype(F32))
        gh = (mul(s.low[...], down_block(feed.wc, slot), NT) * slope).astype(BF)
        pl.when(n >= 2)(lambda: wait_grads(n - 2))
        gdown = mul(active.astype(BF), s.low[...], TN).astype(BF)
        for k, (y, xx, zl) in enumerate(PLACES):
            s.stage_c[slot, y, xx, zl] = gdown[k * 16 : k * 16 + 16]
        gup = mul(s.n2[...], gh, TN).astype(BF)
        for k, (y, xx, zl) in enumerate(PLACES):
            s.stage_b[slot, xx, zl, y] = gup[k * 16 : k * 16 + 16]
        send_grads(n)
        s.gn[0:ROWS, :] += mul(gh, up_block(feed.wb, slot), NT)
        return carry

    lax.fori_loop(0, 2, chunk, 0)
    poll("chunks")
    lax.fori_loop(2, 4, chunk, 0)
    wait_grads(jnp.int32(2))
    wait_grads(jnp.int32(3))
    poll("feed_forward")
    if layer:
        s.bring("hid")
        s.bring("n2")
    else:
        s.returned("mid")
    through, dg, ds = norm_back(s.gn[0:ROWS, :], s.mid[...], gain[layer][1])
    vec[layer * 2 + 1 : layer * 2 + 2] = dg
    vec[layer * 2 + 5 : layer * 2 + 6] = ds
    if layer:
        s.bring("mid")
    g[...] += through


def backward_heads(layer, x, g, gain, ga, wp, maps, pack, gbias, s, vec, both, poll, cross):
    s.low[...] = g[...].astype(BF)
    if not layer:
        s.returned("att")
    gproj = mul(s.att[...], s.low[...], TN).astype(BF)
    if layer:
        s.bring("att")
    for block in range(8):
        part = gproj[block * 64 : block * 64 + 64]
        packed = mul(pack[0], part[:, 0:128], TN)
        for q in range(1, 4):
            packed = packed + mul(pack[q], part[:, q * 128 : q * 128 + 128], TN)
        packed = packed.astype(BF)
        for n in range(16):
            both[2][slot_of(2, block * 16 + n) + (slice(None), slice(128, 256))] = packed[n * 16 : n * 16 + 16]
    poll("proj")
    for pair, part in enumerate(to_windows_of(maps, layer, s.low)):
        s.ow[pair * 512 : pair * 512 + 512, :] = part.astype(BF)
    s.ow[...] = mul(s.ow[...], wp[layer], NT).astype(BF)
    poll("gatt")
    if not layer:
        s.returned("qkv")
        s.returned("kept")
    attend_back(layer, s.qkv, s.kept, s.ow, gbias, 0)
    poll("half_scores")
    attend_back(layer, s.qkv, s.kept, s.ow, gbias, 1)
    if layer:
        s.bring("kept")
    poll("scores")
    if not layer:
        s.returned("n1w")
    for k in range(3):
        gw = mul(s.n1w[...], s.qkv[:, k * 512 : k * 512 + 512], TN).astype(BF)
        for dev in range(128):
            t, n = dev // 32, dev % 32
            both[k][slot_of(k, dev) + (slice(None), slice(0, 128))] = gw[n * 16 : n * 16 + 16, t * 128 : t * 128 + 128]
        cross(k)
    poll("qkv")
    if layer:
        s.bring("n1w")
    total = mul(s.qkv[:, 0:512], qkv_block(ga, layer, 0), NT)
    for k in range(1, 3):
        total = total + mul(s.qkv[:, k * 512 : k * 512 + 512], qkv_block(ga, layer, k), NT)
    s.ow[...] = total.astype(BF)
    if layer:
        s.bring("qkv")
    poll("gn1")
    through, dg, ds = norm_back(from_windows_of(maps, layer, s.ow), x[...], gain[layer][0])
    vec[layer * 2 : layer * 2 + 1] = dg
    vec[layer * 2 + 4 : layer * 2 + 5] = ds
    g[...] += through
    poll("end")


class Feed:
    def __init__(self, core, gb, gc, wb, wc, sems):
        self.core, self.gb, self.gc, self.wb, self.wc, self.sems = core, gb, gc, wb, wc, sems

    def turn(self, layer, n):
        mine = self.core if layer == 0 else 1 - self.core
        first = jnp.where(n < 2, mine, 1 - mine)
        return 2 * (n % 2) + first

    def copies(self, layer, t, n):
        slot, z = n % 2, pl.ds(2 * (t // 2), 2)
        return (
            pltpu.make_async_copy(self.gb.at[layer, t % 2, :, z], self.wb.at[slot], self.sems.at[slot]),
            pltpu.make_async_copy(self.gc.at[layer, t % 2, :, :, z], self.wc.at[slot], self.sems.at[2 + slot]),
        )

    def fetch(self, layer, t, n):
        for one in self.copies(layer, t, n):
            one.start()

    def take(self, n):
        for one in self.copies(0, 0, n):
            one.wait()
        return n % 2


class Scratch:
    shapes = {
        "low": pltpu.VMEM((ROWS, WIDTH), BF),
        "n1w": pltpu.VMEM((PADDED, WIDTH), BF),
        "qkv": pltpu.VMEM((PADDED, 3 * WIDTH), BF),
        "kept": pltpu.VMEM((32, 64, 512), BF),
        "ow": pltpu.VMEM((PADDED, WIDTH), BF),
        "att": pltpu.VMEM((ROWS, WIDTH), BF),
        "mid": pltpu.VMEM((ROWS, WIDTH), F32),
        "n2": pltpu.VMEM((ROWS, WIDTH), BF),
        "hid": pltpu.VMEM((4, ROWS, WIDTH), BF),
        "gn": pltpu.VMEM((ROWS, WIDTH), F32),
        "stage_b": pltpu.VMEM((2, 4, 2, 4, 16, 512), BF),
        "stage_c": pltpu.VMEM((2, 4, 4, 2, 16, 512), BF),
    }

    def __init__(self, refs, far, sems):
        self.__dict__.update(refs)
        self.far, self.sems = far, sems

    def out_copy(self, name):
        return pltpu.make_async_copy(getattr(self, name), self.far[name], self.sems.at[SPILLED.index(name)])

    def in_copy(self, name):
        return pltpu.make_async_copy(self.far[name], getattr(self, name), self.sems.at[SPILLED.index(name)])

    def spill(self, name):
        self.out_copy(name).start()

    def spilled(self, name):
        self.out_copy(name).wait()

    def bring(self, name):
        self.in_copy(name).start()

    def returned(self, name):
        self.in_copy(name).wait()


def axis_slots(whole, i2, i3):
    return (
        lambda j: whole.at[i3, i2, j],
        lambda j: whole.at[i3, j],
        lambda j: whole.at[j],
    )


class Gather:
    def __init__(self, copy, at, families, ring):
        self.copy, self.at, self.across = copy, at, []
        self.plans = []
        for order, whole in families:
            i1, i2, i3 = (at[axis] for axis in order)
            self.plans.append((order, (i1, i2, i3), axis_slots(whole.at[at["c"]], i2, i3), {}))
        if ring:
            self.stages = [self.first, self.second, self.third, self.forward, self.end, self.finish]
        else:
            self.stages = [self.first, self.second, self.straight, self.landed, self.finish]

    def pass_on(self, ref):
        self.across.append(self.copy(ref, ref, "c", 1))

    def first(self):
        for order, places, slots, held in self.plans:
            ref = slots[0](places[0])
            held["1"] = [self.copy(ref, ref, order[0], step) for step in (2, 1, 3)]

    def second(self):
        for order, places, slots, held in self.plans:
            for one in held["1"]:
                one.wait_recv()
            ref = slots[1](places[1])
            held["2"] = [self.copy(ref, ref, order[1], step) for step in (2, 1, 3)]

    def straight(self):
        for order, places, slots, held in self.plans:
            for one in held["2"]:
                one.wait_recv()
            ref = slots[2](places[2])
            held["3"] = [(step, self.copy(ref, ref, order[2], step)) for step in (1, 3, 2)]
            self.pass_on(ref)

    def landed(self):
        for n in range(3):
            for order, places, slots, held in self.plans:
                step, one = held["3"][n]
                one.wait_recv()
                self.pass_on(slots[2]((places[2] + 4 - step) % 4))

    def third(self):
        for order, places, slots, held in self.plans:
            for one in held["2"]:
                one.wait_recv()
            ref = slots[2](places[2])
            held["s"] = [self.copy(ref, ref, order[2], step) for step in (1, 3)]
            self.pass_on(ref)

    def forward(self):
        for order, places, slots, held in self.plans:
            held["f"] = []
            for n, (step, back) in enumerate(((1, 3), (3, 1))):
                held["s"][n].wait_recv()
                ref = slots[2]((places[2] + back) % 4)
                half = ref.at[2 * n : 2 * n + 2]
                held["f"].append(self.copy(half, half, order[2], step))
                self.pass_on(ref)

    def end(self):
        for order, places, slots, held in self.plans:
            for one in held["f"]:
                one.wait_recv()
            self.pass_on(slots[2]((places[2] + 2) % 4))

    def finish(self):
        for one in self.across:
            one.wait_recv()


def split3(v):
    high = v.astype(BF)
    rest = v - high.astype(F32)
    mid = rest.astype(BF)
    low = (rest - mid.astype(F32)).astype(BF)
    return jnp.concatenate([high, mid, low], axis=0)


def unsplit3(v):
    rows = v.shape[0] // 3
    return v[:rows] + v[rows : 2 * rows] + v[2 * rows :]


def build_bias(tb, rel, bias):
    sides = [split3(jnp.concatenate([tb[t, p] for t in range(4)], axis=0)) for p in range(2)]
    row = lax.broadcasted_iota(jnp.int32, (256, 64), 0)

    def keys(block, carry):
        eight = pl.ds(pl.multiple_of(block * 8, 8), 8)
        named = rel[eight, 0:64]
        both = []
        for k in range(8):
            hot = (row == named[k : k + 1]).astype(F32).astype(BF)
            both.append(jnp.concatenate([unsplit3(mul(side, hot)) for side in sides], axis=1))
        for t in range(4):
            for layer in range(2):
                for m in range(2):
                    n = t * 8 + layer * 2 + m
                    at = (t % 2) * 256 + m * 128
                    bias[layer, t // 2, eight, at : at + 128] = rows_of([one[n : n + 1] for one in both])
        return carry

    lax.fori_loop(0, 7, keys, 0)
    unused = lax.broadcasted_iota(jnp.int32, (16, 512), 0) >= 1
    for layer in range(2):
        for g in range(2):
            bias[layer, g, 48:64] = jnp.where(unused, F32(-1e30), bias[layer, g, 48:64])


def table_sums(gbias, rel, tab):
    row = lax.broadcasted_iota(jnp.int32, (512, 128), 0)
    lane = lax.broadcasted_iota(jnp.int32, (512, 128), 1)
    side = row // 256 == lane // 64
    named_row = jnp.where(side, row % 256, -2)
    none = jnp.zeros((4, 128), F32)

    def keys(block, total):
        eight = pl.ds(pl.multiple_of(block * 8, 8), 8)
        named = rel[eight, :]
        parts = {}
        for t in range(4):
            for layer in range(2):
                for m in range(2):
                    at = (t % 2) * 256 + m * 128
                    parts[t, layer, m] = gbias[layer, t // 2, eight, at : at + 128]
        for k in range(8):
            hot = (named_row == named[k : k + 1]).astype(F32).astype(BF)
            rows = []
            for t in range(4):
                rows += [parts[t, layer, m][k : k + 1] for layer in range(2) for m in range(2)] + [none]
            total = total + unsplit3(mul(split3(rows_of(rows)), hot, NT))
        return total

    total = lax.fori_loop(0, 7, keys, jnp.zeros((32, 512), F32))
    for t in range(4):
        tab[t % 2, t // 2] = total[t * 8 : t * 8 + 8]


class Sums:
    def __init__(self, copy, at, phases):
        self.stages = []
        sent = []

        def start(axis, size, part, landing):
            mine = at[axis]
            landing[mine] = (part(mine) if callable(part) else part)[...]
            for step in range(1, size):
                src = part((mine + step) % size) if callable(part) else landing.at[mine]
                sent.append(copy(src, landing.at[mine], axis, step))

        def end(size, landing, keep):
            while sent:
                sent.pop().wait_recv()
            total = landing[0]
            for k in range(1, size):
                total = total + landing[k]
            keep(total)

        for n, (axis, size, part, landing, keep) in enumerate(phases):
            before = phases[n - 1] if n else None

            def stage(axis=axis, size=size, part=part, landing=landing, before=before):
                if before:
                    end(before[1], before[3], before[4])
                start(axis, size, part, landing)

            self.stages.append(stage)
        last = phases[-1]
        self.stages.append(lambda: end(last[1], last[3], last[4]))


FAMILIES = ((ORDERS[0], 128), (ORDERS[1], 128), (ORDERS[2], 256), (ORDERS[1], 512), (ORDERS[2], 512))


def scratch_list():
    one = (4, 4, 4, 16)
    shapes = {
        **{f"ga{k}": pltpu.VMEM((2, 2, 4, 4, 4, 16, 128), BF) for k in range(4)},
        "wb": pltpu.VMEM((2, 4, 2, 4, 16, 512), BF),
        "wc": pltpu.VMEM((2, 4, 4, 2, 16, 512), BF),
        "x1": pltpu.VMEM((ROWS, WIDTH), F32),
        "wp": pltpu.VMEM((2, WIDTH, WIDTH), BF),
        "bias": pltpu.VMEM((2, 2, 64, 512), F32),
        "mask": pltpu.VMEM((4, 64, 512), F32),
        "rel": pltpu.VMEM((128, 128), jnp.int32),
        "maps": pltpu.VMEM((2, 2, 512, 400), BF),
        "pack": pltpu.VMEM((4, 64, 256), BF),
        "gbias": pltpu.VMEM((2, 2, 64, 512), F32),
        "vecs": pltpu.VMEM((8, WIDTH), F32),
        "vec": pltpu.VMEM((8, WIDTH), F32),
        "gd": pltpu.VMEM((2, 4, 4, 4, 8, 128), F32),
        "tb": pltpu.VMEM((4, 2, 8, 256), F32),
        "tab": pltpu.VMEM((2, 2, 8, 512), F32),
        "vec_sum": pltpu.VMEM((8, 128), F32),
        "vec_land": pltpu.VMEM((4, 4, 8, 128), F32),
        "tab_pair": pltpu.VMEM((2, 8, 512), F32),
        "tab_sum": pltpu.VMEM((8, 512), F32),
        "tab_cross": pltpu.VMEM((2, 2, 8, 512), F32),
        "tab_land": pltpu.VMEM((3, 4, 8, 512), F32),
        "feeds": pltpu.SemaphoreType.DMA((4,)),
        "send": pltpu.SemaphoreType.DMA((COPIES,)),
        "recv": pltpu.SemaphoreType.DMA((COPIES,)),
        "local": pltpu.SemaphoreType.DMA((12,)),
        "spills": pltpu.SemaphoreType.DMA((len(SPILLED),)),
        "cross_send": pltpu.SemaphoreType.DMA((8,)),
        "cross_recv": pltpu.SemaphoreType.DMA((8,)),
    }
    for k in range(3):
        width = FAMILIES[k][1]
        for layer in range(2):
            shapes[f"both{k}_{layer}"] = pltpu.VMEM((2,) + one + (width,), BF)
            for name, shape in landing_shapes(width).items():
                shapes[f"{name}{k}_{layer}"] = shape
    for k in (3, 4):
        for layer in range(2):
            shapes[f"sums{k}_{layer}"] = pltpu.VMEM(one + (512,), BF)
        for name, shape in landing_shapes(512).items():
            shapes[f"{name}{k}"] = shape
    shapes.update(Scratch.shapes)
    return shapes


def prepare_mask(region, maps, mask):
    named = lax.broadcasted_iota(jnp.int32, (128, 400), 0)
    row = jnp.concatenate([region[...], jnp.full((1, 204), -1, jnp.int32)], axis=1)
    hot = (named == row).astype(F32).astype(BF)
    places = mul(maps[0, 0, 0:256, :], hot, NT).astype(BF)
    for w in range(4):
        one = places[w * 64 : w * 64 + 64]
        off = (mul(one, one, NT) - 1.0) * 1e9
        off = jnp.concatenate([off, off], axis=1)
        mask[w] = jnp.concatenate([off] * 4, axis=1)


def place_vectors(ln_gain, ln_shift, lane):
    eight = jnp.concatenate([ln_gain[0], ln_gain[1], ln_shift[0], ln_shift[1]], axis=0)
    at = lax.broadcasted_iota(jnp.int32, (8, 128), 1) - lane
    out = jnp.zeros((8, 128), F32)
    for e in range(4):
        out = jnp.where(at == e, eight[:, e : e + 1], out)
    return out


def core_kernel(x, cot, w_qkv, w_proj, b, c, ln_gain, ln_shift, tables, region, rel_index,
                out, g, o_qkv, o_proj, ob, oc, o_gain, o_shift, o_tables, gb, gc, *rest):
    far, rest = dict(zip(SPILLED, rest[: len(SPILLED)])), rest[len(SPILLED) :]
    r = dict(zip(scratch_list(), rest))
    at = coords()
    core = at["c"]
    s = Scratch({name: r[name] for name in Scratch.shapes}, far, r["spills"])
    ga, wp, gd, tb, local, vec = [r[f"ga{k}"] for k in range(4)], r["wp"], r["gd"], r["tb"], r["local"], r["vec"]
    feed = Feed(core, gb, gc, r["wb"], r["wc"], r["feeds"])
    copy = Copier(at, r["send"], r["recv"])
    own = []

    def place(src, dst):
        put = pltpu.make_async_copy(src, dst, local.at[len(own)])
        put.start()
        own.append(put)

    wholes = [[w.at[layer] for w in ga + [gb, gc]] for layer in range(2)]
    orders = (ORDERS[0], ORDERS[1], ORDERS[2], ORDERS[0], ORDERS[1], ORDERS[2])
    for layer in range(2):
        for order, src, whole in zip(orders[4:], (b, c), wholes[layer][4:]):
            i1, i2, i3 = (at[axis] for axis in order)
            place(src.at[layer], whole.at[core, i3, i2, i1])
        for k in range(4):
            i1, i2, i3 = (at[axis] for axis in orders[k])
            if k < 3:
                tile = w_qkv[layer, k]
            else:
                four = w_proj[layer].astype(F32)
                tile = rows_of([four[n // 4 : n // 4 + 1, n % 4 * 128 : n % 4 * 128 + 128] for n in range(16)])
            ga[k][layer, core, i3, i2, i1] = tile.astype(BF)
    start = pltpu.make_async_copy(cot, g, local.at[8])
    start.start()
    lane = 4 * ((at["x"] * 2 + at["z"] % 2) * 4 + (at["z"] // 2) * 2 + core)
    gd[core, at["z"], at["y"], at["x"]] = place_vectors(ln_gain, ln_shift, lane)
    mine = (at["z"] // 2) * 2 + core
    rel = r["rel"]
    rel[...] = jnp.full(rel.shape, -1, jnp.int32)
    rel[0:49, 0:49] = rel_index[...]
    turned = rel[...].T
    rel[...] = jnp.full(rel.shape, -1, jnp.int32)
    rel[0:64, 0:64] = turned[0:64, 0:64]
    rel[0:64, 64:128] = turned[0:64, 0:64]
    tb[mine] = jnp.zeros((2, 8, 256), F32)
    for layer in range(2):
        for k in range(4):
            tb[mine, k % 2, layer * 2 + k // 2 : layer * 2 + k // 2 + 1, 0:169] = tables[layer, k : k + 1, :]
    enter(at, PEERS)
    for put in own:
        put.wait()
    def some(layer, ks, ring=False):
        return Gather(copy, at, [(orders[k], wholes[layer][k]) for k in ks], ring).stages

    early, mid, late = some(0, (0, 1, 2)), some(0, (3,)), some(0, (4, 5), True)
    next_early, next_late = some(1, (0, 1, 2, 3)), some(1, (4, 5), True)
    small = {}

    def small_start(axis, ref):
        steps = (1,) if axis == "c" else (1, 2, 3)
        small[axis] = [copy(ref, ref, axis, step) for step in steps]

    def small_end(axis):
        for one in small[axis]:
            one.wait_recv()

    early[0]()
    small_start("x", gd.at[core, at["z"], at["y"], at["x"]])
    pair = copy(tb.at[mine], tb.at[mine], "z", 2)
    for one in (mid, late, next_early, next_late):
        one[0]()
    maps, pack = r["maps"], r["pack"]
    window_maps(maps)
    proj_maps(pack)
    prepare_mask(region, maps, r["mask"])
    r["gbias"][...] = jnp.zeros(r["gbias"].shape, F32)
    early[1]()
    late[1]()
    mid[1]()
    small_end("x")
    small_start("y", gd.at[core, at["z"], at["y"]])
    pair.wait_recv()
    other = (mine + 2) % 4
    across = [copy(tb.at[k], tb.at[k], "c", 1) for k in (mine, other)]
    early[2]()
    small_end("y")
    small_start("z", gd.at[core, at["z"]])
    late[2]()
    mid[2]()
    for one in across:
        one.wait_recv()
    build_bias(tb, rel, r["bias"])
    small_end("z")
    small_start("c", gd.at[core])
    early[3]()
    small_end("c")
    vecs = r["vecs"]
    for y in range(4):
        total = gd[0, 0, y, 0]
        for n in range(1, 32):
            total = total + gd[n // 16, n // 4 % 4, y, n % 4]
        vecs[:, y * 128 : y * 128 + 128] = total
    early[4]()
    gain = [[vecs[l * 2 + k : l * 2 + k + 1] for k in range(2)] for l in range(2)]
    shift = [[vecs[4 + l * 2 + k : 5 + l * 2 + k] for k in range(2)] for l in range(2)]
    start.wait()

    def unpack_proj(layer):
        for block in range(8):
            tiles = []
            for n in range(16):
                tiles.append(ga[3][(layer,) + slot_of(0, block * 16 + n)])
            tiles = rows_of(tiles)
            for q in range(4):
                wp[layer, block * 64 : block * 64 + 64, q * 128 : q * 128 + 128] = mul(pack[q], tiles).astype(BF)

    forward_plans = (
        {
            "qkv": [mid[3], next_early[1], next_late[1]],
            "half_scores": [late[3]],
            "scores": [mid[4], lambda: unpack_proj(0), next_early[2]],
            "feed_forward": [late[4], next_late[2], late[5]],
            "chunks": [next_early[3]],
            "end": [next_early[4], lambda: unpack_proj(1)],
        },
        {"qkv": [next_late[3]], "feed_forward": [next_late[4], next_late[5]]},
    )
    x1 = r["x1"]
    for layer, before, after in ((0, x, x1), (1, x1, out)):

        def reached(name, plan=forward_plans[layer]):
            for one in plan.get(name, ()):
                one()

        forward(layer, before, after, gain, shift, ga, feed, wp, maps, r["bias"], r["mask"], s, reached)

    def chunk_part(ref, k, n):
        z = pl.ds(2 * (n % 2), 2)
        return ref.at[:, z] if k == 3 else ref.at[:, :, z]

    def chunk_over(k, n):
        sem = (k - 3) * 4 + n
        return pltpu.make_async_remote_copy(
            src_ref=(s.stage_b if k == 3 else s.stage_c).at[n % 2],
            dst_ref=chunk_part(r[f"landed{k}"], k, n),
            send_sem=r["cross_send"].at[sem],
            recv_sem=r["cross_recv"].at[sem],
            device_id=moved(at, "c", 1),
            device_id_type=MESH,
        )

    def chunk_here(layer, k, n):
        src = (s.stage_b if k == 3 else s.stage_c).at[n % 2]
        return pltpu.make_async_copy(
            src, chunk_part(r[f"sums{k}_{layer}"], k, n), r["cross_send"].at[(k - 3) * 4 + n]
        )

    def grads_of(layer):
        first = 0 if layer else 2

        def away(n):
            return jnp.logical_and(n >= first, n < first + 2)

        def send_grads(n):
            for k in (3, 4):
                pl.when(away(n))(lambda k=k: chunk_over(k, n).start())
                pl.when(jnp.logical_not(away(n)))(lambda k=k: chunk_here(layer, k, n).start())

        def wait_grads(n):
            for k in (3, 4):
                pl.when(away(n))(lambda k=k: chunk_over(k, n).wait_send())
                pl.when(jnp.logical_not(away(n)))(lambda k=k: chunk_here(layer, k, n).wait())

        def arrived(k):
            for n in (first, first + 1):
                chunk_over(k, n).wait_recv()

        return send_grads, wait_grads, arrived

    def out_of(ref, layer, lanes):
        def put(total):
            ref[layer, :, lanes] = total

        return put

    def feed_forward_scatter(layer):
        families = []
        for k, ref in ((3, ob), (4, oc)):
            family = {name: r[f"{name}{k}"] for name in landing_shapes(512)}
            family.update(order=FAMILIES[k][0], sums=r[f"sums{k}_{layer}"], out=out_of(ref, layer, slice(0, 512)))
            families.append(family)
        arrived = grads_of(layer)[2]
        return Scatter(copy, at, families, lambda n: arrived(n + 3))

    def heads_out(layer, k):
        def put(total):
            o_qkv[layer, k] = total[:, 0:128]
            if k == 2:
                for n in range(16):
                    lanes = slice(n % 4 * 128, n % 4 * 128 + 128)
                    o_proj[layer, n // 4 : n // 4 + 1, lanes] = total[n : n + 1, 128:256]

        return put

    def heads_scatter(layer):
        families, crossing = [], []
        for k in range(3):
            family = {name: r[f"{name}{k}_{layer}"] for name in landing_shapes(128)}
            both = r[f"both{k}_{layer}"]
            family.update(order=FAMILIES[k][0], sums=both.at[core], out=heads_out(layer, k))
            families.append(family)

        def cross(k):
            crossing.append(copy(r[f"both{k}_{layer}"].at[1 - core], r[f"landed{k}_{layer}"], "c", 1))

        return Scatter(copy, at, families, lambda n: crossing[n].wait_recv()), cross

    wide = {layer: feed_forward_scatter(layer) for layer in (0, 1)}
    heads = {layer: heads_scatter(layer) for layer in (0, 1)}
    tab, tab_pair, tab_sum, vec_sum = r["tab"], r["tab_pair"], r["tab_sum"], r["vec_sum"]
    vec_land, tab_cross, tab_land = r["vec_land"], r["tab_cross"], r["tab_land"]

    def keep_in(ref):
        def keep(total):
            ref[...] = total

        return keep

    def keep_vectors(total):
        lanes = lax.broadcasted_iota(jnp.int32, (8, 128), 1) - lane
        four = jnp.concatenate(
            [jnp.sum(jnp.where(lanes == e, total, 0.0), axis=1, keepdims=True) for e in range(4)], axis=1
        )
        for layer in range(2):
            o_gain[layer] = four[layer * 2 : layer * 2 + 2]
            o_shift[layer] = four[layer * 2 + 4 : layer * 2 + 6]

    def keep_tables(total):
        for layer in range(2):
            for k in range(4):
                row = layer * 2 + k // 2
                o_tables[layer, k : k + 1, :] = total[row : row + 1, k % 2 * 256 : k % 2 * 256 + 169]

    vec_sums = Sums(
        copy,
        at,
        [
            ("y", 4, lambda j: vec.at[:, pl.ds(pl.multiple_of(j * 128, 128), 128)], vec_land.at[0], keep_in(vec_sum)),
            ("x", 4, vec_sum, vec_land.at[1], keep_in(vec_sum)),
            ("z", 4, vec_sum, vec_land.at[2], keep_in(vec_sum)),
            ("c", 2, vec_sum, vec_land.at[3], keep_vectors),
        ],
    )
    tab_sums = Sums(
        copy,
        at,
        [
            ("c", 2, lambda j: tab.at[j], tab_cross, keep_in(tab_pair)),
            ("z", 4, lambda j: tab_pair.at[j // 2], tab_land.at[0], keep_in(tab_sum)),
            ("x", 4, tab_sum, tab_land.at[1], keep_in(tab_sum)),
            ("y", 4, tab_sum, tab_land.at[2], keep_tables),
        ],
    )

    def tables_done():
        table_sums(r["gbias"], rel, tab)

    def stage(sums, n):
        return lambda: sums.stages[n]()

    high_wide, low_wide, high_heads, low_heads = wide[1], wide[0], heads[1][0], heads[0][0]
    plans = {
        1: {
            "feed_forward": [stage(high_wide, 0)],
            "half_scores": [stage(high_wide, 1)],
            "end": [stage(high_wide, 2)],
        },
        0: {
            "chunks": [stage(high_wide, 3), stage(high_heads, 0)],
            "feed_forward": [stage(high_heads, 1), stage(low_wide, 0), stage(high_wide, 4)],
            "half_scores": [stage(high_heads, 2), stage(low_wide, 1)],
            "scores": [tables_done, stage(tab_sums, 0), stage(high_heads, 3)],
            "qkv": [stage(tab_sums, 1), stage(low_wide, 2), stage(high_heads, 4)],
            "gn1": [stage(low_heads, 0), stage(tab_sums, 2)],
            "end": [
                stage(vec_sums, 0),
                stage(low_heads, 1),
                stage(tab_sums, 3),
                stage(vec_sums, 1),
                stage(low_wide, 3),
                stage(low_heads, 2),
                stage(tab_sums, 4),
                stage(vec_sums, 2),
                stage(low_wide, 4),
                stage(low_heads, 3),
                stage(vec_sums, 3),
                stage(low_heads, 4),
                stage(vec_sums, 4),
            ],
        },
    }
    for layer, before in ((1, x1), (0, x)):

        def poll(name, plan=plans[layer]):
            for one in plan.get(name, ()):
                one()

        send, wait, _ = grads_of(layer)
        backward_mlp(layer, g, gain, feed, s, vec, send, wait, poll)
        backward_heads(
            layer, before, g, gain, ga, wp, maps, pack, r["gbias"], s, vec,
            [r[f"both{k}_{layer}"] for k in range(3)], poll, heads[layer][1],
        )
    copy.finish()


def shards(
    inputs, w_qkv, w_proj, w_up, w_down, ln_gain, ln_shift, tables, region, rel_index, cotangent
):
    w_qkv, tables = w_qkv.transpose(0, 2, 1, 3), tables.transpose(0, 2, 1)
    tiles = jax.ShapeDtypeStruct((2, 2, 4, 4, 4, 16, 512), BF)
    rows = jax.ShapeDtypeStruct((ROWS, WIDTH), F32)
    vmem, far = pl.BlockSpec(memory_space=pltpu.VMEM), pl.BlockSpec(memory_space=pl.ANY)
    spills = [jax.ShapeDtypeStruct(Scratch.shapes[name].shape, Scratch.shapes[name].dtype) for name in SPILLED]
    grads = [
        jax.ShapeDtypeStruct(one.shape, F32) for one in (w_qkv, w_proj, w_up, w_down, ln_gain, ln_shift, tables)
    ]
    outs = pl.pallas_call(
        core_kernel,
        out_shape=[rows, rows] + grads + [tiles, tiles] + spills,
        in_specs=[vmem, far, vmem, vmem, far, far] + [vmem] * 5,
        out_specs=[vmem] * 9 + [far] * (2 + len(spills)),
        scratch_shapes=list(scratch_list().values()),
        compiler_params=pltpu.CompilerParams(
            vmem_limit_bytes=63 * 2**20, collective_id=0, has_side_effects=True
        ),
        name="both_blocks",
    )(
        inputs, cotangent, w_qkv, w_proj, w_up, w_down, ln_gain, ln_shift, tables, region.reshape(1, -1), rel_index
    )
    out, g, o_qkv, o_proj, ob, oc, o_gain, o_shift, o_tables = outs[:9]
    return out, g, o_qkv.transpose(0, 2, 1, 3), o_proj, ob, oc, o_gain, o_shift, o_tables.transpose(0, 2, 1)


def solution(mesh):
    return jax.shard_map(
        shards,
        mesh=mesh,
        in_specs=(
            P(("dp", "tensor"), None),
            P(None, "dp", None, "tensor"),
            P(None, ("tensor", "dp"), None),
            P(None, "dp", "tensor"),
            P(None, ("tensor", "dp"), None),
            P(None, None, ("dp", "tensor")),
            P(None, None, ("dp", "tensor")),
            P(None, None, "tensor"),
            P(),
            P(),
            P(("dp", "tensor"), None),
        ),
        out_specs=(
            P(("dp", "tensor"), None),
            P(("dp", "tensor"), None),
            P(None, "dp", None, "tensor"),
            P(None, ("tensor", "dp"), None),
            P(None, "dp", "tensor"),
            P(None, ("tensor", "dp"), None),
            P(None, None, ("dp", "tensor")),
            P(None, None, ("dp", "tensor")),
            P(None, None, "tensor"),
        ),
        check_vma=False,
    )
```

```python
import functools
import jax
import jax.numpy as jnp
from jax import lax
from jax.experimental import pallas as pl
from jax.experimental.pallas import tpu as pltpu
from jax.sharding import PartitionSpec as P

MESH = pl.DeviceIdType.MESH
ORDERS = (("x", "y", "z"), ("y", "z", "x"), ("z", "x", "y"))


def coords():
    dp, tp = lax.axis_index("dp"), lax.axis_index("tensor")
    return {
        "y": dp // 8,
        "x": (dp // 2) % 4,
        "z": (tp // 2) * 2 + dp % 2,
        "c": tp % 2,
    }


def device(at):
    return (at["y"] * 8 + at["x"] * 2 + at["z"] % 2, (at["z"] // 2) * 2 + at["c"])


def moved(at, axis, step):
    size = 2 if axis == "c" else 4
    return device({**at, axis: (at[axis] + step) % size})


NEIGHBOURS = (("x", 1), ("x", 3), ("y", 1), ("y", 3), ("z", 1), ("z", 3), ("c", 1))


def enter(at, peers=NEIGHBOURS):
    barrier = pltpu.get_barrier_semaphore()
    for axis, step in peers:
        pl.semaphore_signal(barrier, inc=1, device_id=moved(at, axis, step), device_id_type=MESH)
    pl.semaphore_wait(barrier, len(peers))


PEERS = NEIGHBOURS + (("x", 2), ("y", 2), ("z", 2))
COPIES = 320


class Copier:
    def __init__(self, at, send, recv):
        self.at, self.send, self.recv, self.made = at, send, recv, []

    def __call__(self, src, dst, axis, step):
        slot = len(self.made)
        assert slot < COPIES
        copy = pltpu.make_async_remote_copy(
            src_ref=src,
            dst_ref=dst,
            send_sem=self.send.at[slot],
            recv_sem=self.recv.at[slot],
            device_id=moved(self.at, axis, step),
            device_id_type=MESH,
        )
        copy.start()
        self.made.append(copy)
        return copy

    def finish(self):
        for copy in self.made:
            copy.wait_send()


def add_into(dst, *terms):
    lead = dst.shape[:-3]
    count = 1
    for size in lead:
        count *= size

    def body(n, carry):
        index = []
        for size in reversed(lead):
            index.append(n % size)
            n = n // size
        index = tuple(reversed(index)) or slice(None)
        total = dst[index].astype(jnp.float32)
        for term in terms:
            total = total + term[index].astype(jnp.float32)
        dst[index] = total.astype(dst.dtype)
        return carry

    if count == 1:
        body(0, 0)
    else:
        lax.fori_loop(0, count, body, 0)


class Scatter:
    def __init__(self, copy, at, families, crossing):
        self.copy, self.at, self.families, self.crossing = copy, at, families, crossing
        self.held = [{} for _ in families]
        self.stages = [self.join, self.along, self.second, self.third, self.finish]

    def places(self, family):
        i1, i2, i3 = (self.at[axis] for axis in family["order"])
        return i1, i2, i3

    def join(self):
        for n, (family, held) in enumerate(zip(self.families, self.held)):
            self.crossing(n)
            _, _, i3 = self.places(family)
            axis, sums, landed = family["order"][2], family["sums"], family["landed"]
            far = (i3 + 2) % 4
            add_into(sums.at[far], landed.at[far])
            held["r"] = self.copy(sums.at[far, 0:2], family["half"].at[0], axis, 1)
            held["l"] = self.copy(sums.at[far, 2:4], family["half"].at[1], axis, 3)
        for family in self.families:
            _, _, i3 = self.places(family)
            for step in (1, 3, 0):
                j = (i3 + step) % 4
                add_into(family["sums"].at[j], family["landed"].at[j])

    def along(self):
        for family, held in zip(self.families, self.held):
            _, _, i3 = self.places(family)
            axis, sums = family["order"][2], family["sums"]
            right, left = (i3 + 1) % 4, (i3 + 3) % 4
            held["r"].wait_recv()
            add_into(sums.at[right, 0:2], family["half"].at[0])
            held["r2"] = self.copy(sums.at[right], family["full"].at[0], axis, 1)
            held["l"].wait_recv()
            add_into(sums.at[left, 2:4], family["half"].at[1])
            held["l2"] = self.copy(sums.at[left], family["full"].at[1], axis, 3)

    def second(self):
        for family, held in zip(self.families, self.held):
            _, i2, i3 = self.places(family)
            axis, sums = family["order"][1], family["sums"]
            held["r2"].wait_recv()
            held["l2"].wait_recv()
            add_into(sums.at[i3], family["full"].at[0], family["full"].at[1])
            held["2"] = [
                self.copy(sums.at[i3, (i2 + step) % 4], family["two"].at[step - 1], axis, step) for step in (2, 1, 3)
            ]

    def third(self):
        for family, held in zip(self.families, self.held):
            i1, i2, i3 = self.places(family)
            axis, sums = family["order"][0], family["sums"]
            for one in held["2"]:
                one.wait_recv()
            add_into(sums.at[i3, i2], *(family["two"].at[k] for k in range(3)))
            held["1"] = [
                self.copy(sums.at[i3, i2, (i1 + step) % 4], family["one"].at[step - 1], axis, step)
                for step in (2, 1, 3)
            ]

    def finish(self):
        for family, held in zip(self.families, self.held):
            i1, i2, i3 = self.places(family)
            for one in held["1"]:
                one.wait_recv()
            total = family["sums"][i3, i2, i1].astype(jnp.float32)
            for k in range(3):
                total = total + family["one"][k].astype(jnp.float32)
            family["out"](total)


def landing_shapes(width):
    bf = jnp.bfloat16
    return {
        "landed": pltpu.VMEM((4, 4, 4, 16, width), bf),
        "half": pltpu.VMEM((2, 2, 4, 16, width), bf),
        "full": pltpu.VMEM((2, 4, 4, 16, width), bf),
        "two": pltpu.VMEM((3, 4, 16, width), bf),
        "one": pltpu.VMEM((3, 16, width), bf),
    }


WINDOW = 7
SIDE = 14
EPS = 1e-05


BF, F32 = jnp.bfloat16, jnp.float32
SCALE = 32.0 ** -0.5
ROWS, PADDED, WIDTH = 784, 1024, 512
NN = (((1,), (0,)), ((), ()))
NT = (((1,), (1,)), ((), ()))
TN = (((0,), (0,)), ((), ()))


def mul(a, b, dims=NN):
    return lax.dot_general(a, b, dims, preferred_element_type=F32)


def window_maps(maps):
    n = lax.broadcasted_iota(jnp.int32, (512, 1), 0)
    place = n % 64
    token = lax.broadcasted_iota(jnp.int32, (512, 400), 1)
    for layer in range(2):
        row = n // 128 % 2 * 7 + place // 7
        col = n // 64 % 2 * 7 + place % 7
        if layer:
            row, col = (row + 3) % 14, (col + 3) % 14
        taken = jnp.where(place < 49, n // 256 * 196 + row * 14 + col, -100)
        for pair in range(2):
            maps[layer, pair] = (token == taken + 8 * pair).astype(F32).astype(BF)


def proj_maps(pack):
    n = lax.broadcasted_iota(jnp.int32, (64, 1), 0)
    packed = lax.broadcasted_iota(jnp.int32, (64, 256), 1)
    for q in range(4):
        pack[q] = (packed == n // 4 * 16 + n % 4 * 4 + q).astype(F32).astype(BF)


PLACES = [(y, x, zl) for y in range(4) for x in range(4) for zl in range(2)]


def rows_of(tiles):
    return jnp.concatenate(tiles, axis=0)


def up_block(wb, slot):
    return rows_of([wb[slot, x, zl, y] for y, x, zl in PLACES])


def down_block(wc, slot):
    return rows_of([wc[slot, y, x, zl] for y, x, zl in PLACES])


def slot_of(k, dev):
    t, (y, x, zl) = dev // 32, PLACES[dev % 32]
    at = {"x": x, "y": y, "z": 2 * (t // 2) + zl}
    return (t % 2,) + tuple(at[axis] for axis in reversed(ORDERS[k]))


def qkv_block(ga, layer, s):
    return jnp.concatenate(
        [rows_of([ga[s][(layer,) + slot_of(s, t * 32 + n)] for n in range(32)]) for t in range(4)], axis=1
    )


def norm_parts(values):
    mean = jnp.mean(values, axis=1, keepdims=True)
    centered = values - mean
    r = lax.rsqrt(jnp.mean(centered * centered, axis=1, keepdims=True) + EPS)
    return centered * r, r


def norm_back(grad, values, gain):
    xhat, r = norm_parts(values)
    e = grad * gain
    through = r * (
        e - jnp.mean(e, axis=1, keepdims=True) - xhat * jnp.mean(e * xhat, axis=1, keepdims=True)
    )
    return (
        through,
        jnp.sum(grad * xhat, axis=0, keepdims=True),
        jnp.sum(grad, axis=0, keepdims=True),
    )


C0, C1 = 0.7978845608028654, 0.044715


def gelu(u):
    return 0.5 * u * (1.0 + jnp.tanh(C0 * u * (1.0 + C1 * (u * u))))


def gelu_both(u):
    square = u * u
    t = jnp.tanh(C0 * u * (1.0 + C1 * square))
    half = 0.5 * (1.0 + t)
    slope = half + (0.5 * C0) * u * (1.0 - t * t) * (1.0 + (3.0 * C1) * square)
    return u * half, slope


def to_windows_of(maps, layer, tokens):
    return [mul(maps[layer, pair], tokens[pair * 384 : pair * 384 + 400, :]) for pair in range(2)]


def from_windows_of(maps, layer, rows):
    first = mul(maps[layer, 0], rows[0:512, :], TN)
    second = mul(maps[layer, 1], rows[512:1024, :], TN)
    return jnp.concatenate(
        [first[:384], first[384:400] + second[:16], second[16:]], axis=0
    )


def head_masks():
    lane = lax.broadcasted_iota(jnp.int32, (1, 128), 1) // 32
    return [lane == h for h in range(4)]


def spread(v, masks):
    return jnp.concatenate([jnp.where(m, v, jnp.zeros((), v.dtype)) for m in masks], axis=0)


def fold(r, masks):
    out = r[0:64]
    for h in range(1, 4):
        out = jnp.where(masks[h], r[h * 64 : h * 64 + 64], out)
    return out


UNROLL = 4


def columns(s, q):
    return slice(s * 512 + q * 128, s * 512 + q * 128 + 128)


def scores_of(ref, layer, q):
    return ref.at[layer, q // 2, :, q % 2 * 256 : q % 2 * 256 + 256]


def window(w):
    return pl.ds(pl.multiple_of(w * 64, 64), 64)


def attend(layer, qkv, bias, mask, kept, out, part):
    masks = head_masks()

    def some(n, carry):
        items = [(n * UNROLL + u, u, q) for u in range(UNROLL) for q in range(4)]
        scores = [
            mul(qkv[window(w), columns(1, q)], spread(qkv[window(w), columns(0, q)], masks), NT) for w, u, q in items
        ]
        probs = []
        for (w, u, q), s in zip(items, scores):
            s = s * SCALE + scores_of(bias, layer, q)[...]
            if layer:
                s = s + mask[u % 4, :, 0:256]
            e = jnp.exp(s - jnp.max(s, axis=0, keepdims=True))
            p = (e * (1.0 / jnp.sum(e, axis=0, keepdims=True))).astype(BF)
            kept[w * 4 + q] = p
            probs.append(p)
        for (w, u, q), p in zip(items, probs):
            out[window(w), columns(0, q)] = fold(mul(p, qkv[window(w), columns(2, q)], TN), masks).astype(BF)
        return carry

    lax.fori_loop(part * 8 // UNROLL, (part + 1) * 8 // UNROLL, some, 0)


def attend_back(layer, qkv, kept, gout, gbias, part):
    masks = head_masks()

    def some(n, carry):
        items = [(n * UNROLL + u, q) for u in range(UNROLL) for q in range(4)]
        gprobs, gvs = [], []
        for w, q in items:
            d = spread(gout[window(w), columns(0, q)], masks)
            gprobs.append(mul(qkv[window(w), columns(2, q)], d, NT))
            gvs.append(mul(kept[w * 4 + q], d))
        for (w, q), gv in zip(items, gvs):
            qkv[window(w), columns(2, q)] = gv.astype(BF)
        gscores = []
        for (w, q), gp in zip(items, gprobs):
            p = kept[w * 4 + q].astype(F32)
            pg = p * gp
            gscores.append(pg - p * jnp.sum(pg, axis=0, keepdims=True))
        for q in range(4):
            place = scores_of(gbias, layer, q)
            total = place[...]
            for (w, h), gs in zip(items, gscores):
                if h == q:
                    total = total + gs
            place[...] = total
        for (w, q), gs in zip(items, gscores):
            ds = gs.astype(BF)
            query, key = qkv[window(w), columns(0, q)], qkv[window(w), columns(1, q)]
            gk = mul(ds, spread(query, masks)) * SCALE
            gq = fold(mul(ds, key, TN), masks) * SCALE
            qkv[window(w), columns(0, q)] = gq.astype(BF)
            qkv[window(w), columns(1, q)] = gk.astype(BF)
        return carry

    lax.fori_loop(part * 8 // UNROLL, (part + 1) * 8 // UNROLL, some, 0)


SPILLED = ("n1w", "qkv", "kept", "att", "mid", "n2", "hid")


def forward(layer, x, result, gain, shift, ga, feed, wp, maps, bias, mask, s, poll):
    def ready(name):
        if layer:
            s.spilled(name)

    def done(name):
        if not layer:
            s.spill(name)

    xhat, _ = norm_parts(x[...])
    s.low[...] = (xhat * gain[layer][0] + shift[layer][0]).astype(BF)
    ready("n1w")
    for pair, part in enumerate(to_windows_of(maps, layer, s.low)):
        s.n1w[pair * 512 : pair * 512 + 512, :] = part.astype(BF)
    done("n1w")
    ready("qkv")
    for k in range(3):
        s.qkv[:, k * 512 : k * 512 + 512] = mul(s.n1w[...], qkv_block(ga, layer, k)).astype(BF)
    done("qkv")
    poll("qkv")
    ready("kept")
    attend(layer, s.qkv, bias, mask, s.kept, s.ow, 0)
    poll("half_scores")
    attend(layer, s.qkv, bias, mask, s.kept, s.ow, 1)
    done("kept")
    poll("scores")
    ready("att")
    s.att[...] = from_windows_of(maps, layer, s.ow).astype(BF)
    done("att")
    ready("mid")
    s.mid[...] = x[...] + mul(s.att[...], wp[layer])
    done("mid")
    poll("feed_forward")
    feed.fetch(layer, 0, 0)
    ready("n2")
    xhat, _ = norm_parts(s.mid[...])
    s.n2[...] = (xhat * gain[layer][1] + shift[layer][1]).astype(BF)
    done("n2")
    result[...] = s.mid[...]
    ready("hid")

    def chunk(t, carry):
        slot = feed.take(t)

        @pl.when(t < 3)
        def _():
            feed.fetch(layer, t + 1, t + 1)

        if layer:
            pl.when(t == 3)(lambda: feed.fetch(1, feed.turn(1, 0), 0))
        hidden = mul(s.n2[...], up_block(feed.wb, slot))
        s.hid[t] = hidden.astype(BF)
        result[...] += mul(gelu(hidden).astype(BF), down_block(feed.wc, slot))
        return carry

    lax.fori_loop(0, 2, chunk, 0)
    poll("chunks")
    lax.fori_loop(2, 4, chunk, 0)
    done("hid")
    poll("end")


def backward_mlp(layer, g, gain, feed, s, vec, send_grads, wait_grads, poll):
    if not layer:
        s.returned("hid")
        s.returned("n2")
    s.low[...] = g[...].astype(BF)
    s.gn[0:ROWS, :] = jnp.zeros((ROWS, WIDTH), F32)

    def chunk(n, carry):
        t = feed.turn(layer, n)
        slot = feed.take(n)

        @pl.when(n < 3)
        def _():
            feed.fetch(layer, feed.turn(layer, n + 1), n + 1)

        if layer:
            pl.when(n == 3)(lambda: feed.fetch(0, feed.turn(0, 0), 0))

        active, slope = gelu_both(s.hid[t].astype(F32))
        gh = (mul(s.low[...], down_block(feed.wc, slot), NT) * slope).astype(BF)
        pl.when(n >= 2)(lambda: wait_grads(n - 2))
        gdown = mul(active.astype(BF), s.low[...], TN).astype(BF)
        for k, (y, xx, zl) in enumerate(PLACES):
            s.stage_c[slot, y, xx, zl] = gdown[k * 16 : k * 16 + 16]
        gup = mul(s.n2[...], gh, TN).astype(BF)
        for k, (y, xx, zl) in enumerate(PLACES):
            s.stage_b[slot, xx, zl, y] = gup[k * 16 : k * 16 + 16]
        send_grads(n)
        s.gn[0:ROWS, :] += mul(gh, up_block(feed.wb, slot), NT)
        return carry

    lax.fori_loop(0, 2, chunk, 0)
    poll("chunks")
    lax.fori_loop(2, 4, chunk, 0)
    wait_grads(jnp.int32(2))
    wait_grads(jnp.int32(3))
    poll("feed_forward")
    if layer:
        s.bring("hid")
        s.bring("n2")
    else:
        s.returned("mid")
    through, dg, ds = norm_back(s.gn[0:ROWS, :], s.mid[...], gain[layer][1])
    vec[layer * 2 + 1 : layer * 2 + 2] = dg
    vec[layer * 2 + 5 : layer * 2 + 6] = ds
    if layer:
        s.bring("mid")
    g[...] += through


def backward_heads(layer, x, g, gain, ga, wp, maps, pack, gbias, s, vec, both, poll, cross):
    s.low[...] = g[...].astype(BF)
    if not layer:
        s.returned("att")
    gproj = mul(s.att[...], s.low[...], TN).astype(BF)
    if layer:
        s.bring("att")
    for block in range(8):
        part = gproj[block * 64 : block * 64 + 64]
        packed = mul(pack[0], part[:, 0:128], TN)
        for q in range(1, 4):
            packed = packed + mul(pack[q], part[:, q * 128 : q * 128 + 128], TN)
        packed = packed.astype(BF)
        for n in range(16):
            both[2][slot_of(2, block * 16 + n) + (slice(None), slice(128, 256))] = packed[n * 16 : n * 16 + 16]
    poll("proj")
    for pair, part in enumerate(to_windows_of(maps, layer, s.low)):
        s.ow[pair * 512 : pair * 512 + 512, :] = part.astype(BF)
    s.ow[...] = mul(s.ow[...], wp[layer], NT).astype(BF)
    poll("gatt")
    if not layer:
        s.returned("qkv")
        s.returned("kept")
    attend_back(layer, s.qkv, s.kept, s.ow, gbias, 0)
    poll("half_scores")
    attend_back(layer, s.qkv, s.kept, s.ow, gbias, 1)
    if layer:
        s.bring("kept")
    poll("scores")
    if not layer:
        s.returned("n1w")
    for k in range(3):
        gw = mul(s.n1w[...], s.qkv[:, k * 512 : k * 512 + 512], TN).astype(BF)
        for dev in range(128):
            t, n = dev // 32, dev % 32
            both[k][slot_of(k, dev) + (slice(None), slice(0, 128))] = gw[n * 16 : n * 16 + 16, t * 128 : t * 128 + 128]
        cross(k)
    poll("qkv")
    if layer:
        s.bring("n1w")
    total = mul(s.qkv[:, 0:512], qkv_block(ga, layer, 0), NT)
    for k in range(1, 3):
        total = total + mul(s.qkv[:, k * 512 : k * 512 + 512], qkv_block(ga, layer, k), NT)
    s.ow[...] = total.astype(BF)
    if layer:
        s.bring("qkv")
    poll("gn1")
    through, dg, ds = norm_back(from_windows_of(maps, layer, s.ow), x[...], gain[layer][0])
    vec[layer * 2 : layer * 2 + 1] = dg
    vec[layer * 2 + 4 : layer * 2 + 5] = ds
    g[...] += through
    poll("end")


class Feed:
    def __init__(self, core, gb, gc, wb, wc, sems):
        self.core, self.gb, self.gc, self.wb, self.wc, self.sems = core, gb, gc, wb, wc, sems

    def turn(self, layer, n):
        mine = self.core if layer == 0 else 1 - self.core
        first = jnp.where(n < 2, mine, 1 - mine)
        return 2 * (n % 2) + first

    def copies(self, layer, t, n):
        slot, z = n % 2, pl.ds(2 * (t // 2), 2)
        return (
            pltpu.make_async_copy(self.gb.at[layer, t % 2, :, z], self.wb.at[slot], self.sems.at[slot]),
            pltpu.make_async_copy(self.gc.at[layer, t % 2, :, :, z], self.wc.at[slot], self.sems.at[2 + slot]),
        )

    def fetch(self, layer, t, n):
        for one in self.copies(layer, t, n):
            one.start()

    def take(self, n):
        for one in self.copies(0, 0, n):
            one.wait()
        return n % 2


class Scratch:
    shapes = {
        "low": pltpu.VMEM((ROWS, WIDTH), BF),
        "n1w": pltpu.VMEM((PADDED, WIDTH), BF),
        "qkv": pltpu.VMEM((PADDED, 3 * WIDTH), BF),
        "kept": pltpu.VMEM((64, 64, 256), BF),
        "ow": pltpu.VMEM((PADDED, WIDTH), BF),
        "att": pltpu.VMEM((ROWS, WIDTH), BF),
        "mid": pltpu.VMEM((ROWS, WIDTH), F32),
        "n2": pltpu.VMEM((ROWS, WIDTH), BF),
        "hid": pltpu.VMEM((4, ROWS, WIDTH), BF),
        "gn": pltpu.VMEM((ROWS, WIDTH), F32),
        "stage_b": pltpu.VMEM((2, 4, 2, 4, 16, 512), BF),
        "stage_c": pltpu.VMEM((2, 4, 4, 2, 16, 512), BF),
    }

    def __init__(self, refs, far, sems):
        self.__dict__.update(refs)
        self.far, self.sems = far, sems

    def out_copy(self, name):
        return pltpu.make_async_copy(getattr(self, name), self.far[name], self.sems.at[SPILLED.index(name)])

    def in_copy(self, name):
        return pltpu.make_async_copy(self.far[name], getattr(self, name), self.sems.at[SPILLED.index(name)])

    def spill(self, name):
        self.out_copy(name).start()

    def spilled(self, name):
        self.out_copy(name).wait()

    def bring(self, name):
        self.in_copy(name).start()

    def returned(self, name):
        self.in_copy(name).wait()


def axis_slots(whole, i2, i3):
    return (
        lambda j: whole.at[i3, i2, j],
        lambda j: whole.at[i3, j],
        lambda j: whole.at[j],
    )


class Gather:
    def __init__(self, copy, at, families, ring):
        self.copy, self.at, self.across = copy, at, []
        self.plans = []
        for order, whole in families:
            i1, i2, i3 = (at[axis] for axis in order)
            self.plans.append((order, (i1, i2, i3), axis_slots(whole.at[at["c"]], i2, i3), {}))
        if ring:
            self.stages = [self.first, self.second, self.third, self.forward, self.end, self.finish]
        else:
            self.stages = [self.first, self.second, self.straight, self.landed, self.finish]

    def pass_on(self, ref):
        self.across.append(self.copy(ref, ref, "c", 1))

    def first(self):
        for order, places, slots, held in self.plans:
            ref = slots[0](places[0])
            held["1"] = [self.copy(ref, ref, order[0], step) for step in (2, 1, 3)]

    def second(self):
        for order, places, slots, held in self.plans:
            for one in held["1"]:
                one.wait_recv()
            ref = slots[1](places[1])
            held["2"] = [self.copy(ref, ref, order[1], step) for step in (2, 1, 3)]

    def straight(self):
        for order, places, slots, held in self.plans:
            for one in held["2"]:
                one.wait_recv()
            ref = slots[2](places[2])
            held["3"] = [(step, self.copy(ref, ref, order[2], step)) for step in (1, 3, 2)]
            self.pass_on(ref)

    def landed(self):
        for n in range(3):
            for order, places, slots, held in self.plans:
                step, one = held["3"][n]
                one.wait_recv()
                self.pass_on(slots[2]((places[2] + 4 - step) % 4))

    def third(self):
        for order, places, slots, held in self.plans:
            for one in held["2"]:
                one.wait_recv()
            ref = slots[2](places[2])
            held["s"] = [self.copy(ref, ref, order[2], step) for step in (1, 3)]
            self.pass_on(ref)

    def forward(self):
        for order, places, slots, held in self.plans:
            held["f"] = []
            for n, (step, back) in enumerate(((1, 3), (3, 1))):
                held["s"][n].wait_recv()
                ref = slots[2]((places[2] + back) % 4)
                half = ref.at[2 * n : 2 * n + 2]
                held["f"].append(self.copy(half, half, order[2], step))
                self.pass_on(ref)

    def end(self):
        for order, places, slots, held in self.plans:
            for one in held["f"]:
                one.wait_recv()
            self.pass_on(slots[2]((places[2] + 2) % 4))

    def finish(self):
        for one in self.across:
            one.wait_recv()


def split3(v):
    high = v.astype(BF)
    rest = v - high.astype(F32)
    mid = rest.astype(BF)
    low = (rest - mid.astype(F32)).astype(BF)
    return jnp.concatenate([high, mid, low], axis=0)


def unsplit3(v):
    rows = v.shape[0] // 3
    return v[:rows] + v[rows : 2 * rows] + v[2 * rows :]


def build_bias(tb, rel, bias):
    sides = [split3(jnp.concatenate([tb[t, p] for t in range(4)], axis=0)) for p in range(2)]
    row = lax.broadcasted_iota(jnp.int32, (256, 64), 0)

    def keys(block, carry):
        eight = pl.ds(pl.multiple_of(block * 8, 8), 8)
        named = rel[eight, 0:64]
        both = []
        for k in range(8):
            hot = (row == named[k : k + 1]).astype(F32).astype(BF)
            both.append(jnp.concatenate([unsplit3(mul(side, hot)) for side in sides], axis=1))
        for t in range(4):
            for layer in range(2):
                for m in range(2):
                    n = t * 8 + layer * 2 + m
                    at = (t % 2) * 256 + m * 128
                    bias[layer, t // 2, eight, at : at + 128] = rows_of([one[n : n + 1] for one in both])
        return carry

    lax.fori_loop(0, 7, keys, 0)
    unused = lax.broadcasted_iota(jnp.int32, (16, 512), 0) >= 1
    for layer in range(2):
        for g in range(2):
            bias[layer, g, 48:64] = jnp.where(unused, F32(-1e30), bias[layer, g, 48:64])


def table_sums(gbias, rel, tab):
    row = lax.broadcasted_iota(jnp.int32, (512, 128), 0)
    lane = lax.broadcasted_iota(jnp.int32, (512, 128), 1)
    side = row // 256 == lane // 64
    named_row = jnp.where(side, row % 256, -2)
    none = jnp.zeros((4, 128), F32)

    def keys(block, total):
        eight = pl.ds(pl.multiple_of(block * 8, 8), 8)
        named = rel[eight, :]
        parts = {}
        for t in range(4):
            for layer in range(2):
                for m in range(2):
                    at = (t % 2) * 256 + m * 128
                    parts[t, layer, m] = gbias[layer, t // 2, eight, at : at + 128]
        for k in range(8):
            hot = (named_row == named[k : k + 1]).astype(F32).astype(BF)
            rows = []
            for t in range(4):
                rows += [parts[t, layer, m][k : k + 1] for layer in range(2) for m in range(2)] + [none]
            total = total + unsplit3(mul(split3(rows_of(rows)), hot, NT))
        return total

    total = lax.fori_loop(0, 7, keys, jnp.zeros((32, 512), F32))
    for t in range(4):
        tab[t % 2, t // 2] = total[t * 8 : t * 8 + 8]


class Sums:
    def __init__(self, copy, at, phases):
        self.stages = []
        sent = []

        def start(axis, size, part, landing):
            mine = at[axis]
            landing[mine] = (part(mine) if callable(part) else part)[...]
            for step in range(1, size):
                src = part((mine + step) % size) if callable(part) else landing.at[mine]
                sent.append(copy(src, landing.at[mine], axis, step))

        def end(size, landing, keep):
            while sent:
                sent.pop().wait_recv()
            total = landing[0]
            for k in range(1, size):
                total = total + landing[k]
            keep(total)

        for n, (axis, size, part, landing, keep) in enumerate(phases):
            before = phases[n - 1] if n else None

            def stage(axis=axis, size=size, part=part, landing=landing, before=before):
                if before:
                    end(before[1], before[3], before[4])
                start(axis, size, part, landing)

            self.stages.append(stage)
        last = phases[-1]
        self.stages.append(lambda: end(last[1], last[3], last[4]))


FAMILIES = ((ORDERS[0], 128), (ORDERS[1], 128), (ORDERS[2], 256), (ORDERS[1], 512), (ORDERS[2], 512))


def scratch_list():
    one = (4, 4, 4, 16)
    shapes = {
        **{f"ga{k}": pltpu.VMEM((2, 2, 4, 4, 4, 16, 128), BF) for k in range(4)},
        "wb": pltpu.VMEM((2, 4, 2, 4, 16, 512), BF),
        "wc": pltpu.VMEM((2, 4, 4, 2, 16, 512), BF),
        "x1": pltpu.VMEM((ROWS, WIDTH), F32),
        "wp": pltpu.VMEM((2, WIDTH, WIDTH), BF),
        "bias": pltpu.VMEM((2, 2, 64, 512), F32),
        "mask": pltpu.VMEM((4, 64, 512), F32),
        "rel": pltpu.VMEM((128, 128), jnp.int32),
        "maps": pltpu.VMEM((2, 2, 512, 400), BF),
        "pack": pltpu.VMEM((4, 64, 256), BF),
        "gbias": pltpu.VMEM((2, 2, 64, 512), F32),
        "vecs": pltpu.VMEM((8, WIDTH), F32),
        "vec": pltpu.VMEM((8, WIDTH), F32),
        "gd": pltpu.VMEM((2, 4, 4, 4, 8, 128), F32),
        "tb": pltpu.VMEM((4, 2, 8, 256), F32),
        "tab": pltpu.VMEM((2, 2, 8, 512), F32),
        "vec_sum": pltpu.VMEM((8, 128), F32),
        "vec_land": pltpu.VMEM((4, 4, 8, 128), F32),
        "tab_pair": pltpu.VMEM((2, 8, 512), F32),
        "tab_sum": pltpu.VMEM((8, 512), F32),
        "tab_cross": pltpu.VMEM((2, 2, 8, 512), F32),
        "tab_land": pltpu.VMEM((3, 4, 8, 512), F32),
        "feeds": pltpu.SemaphoreType.DMA((4,)),
        "send": pltpu.SemaphoreType.DMA((COPIES,)),
        "recv": pltpu.SemaphoreType.DMA((COPIES,)),
        "local": pltpu.SemaphoreType.DMA((12,)),
        "spills": pltpu.SemaphoreType.DMA((len(SPILLED),)),
        "cross_send": pltpu.SemaphoreType.DMA((8,)),
        "cross_recv": pltpu.SemaphoreType.DMA((8,)),
    }
    for k in range(3):
        width = FAMILIES[k][1]
        for layer in range(2):
            shapes[f"both{k}_{layer}"] = pltpu.VMEM((2,) + one + (width,), BF)
            for name, shape in landing_shapes(width).items():
                shapes[f"{name}{k}_{layer}"] = shape
    for k in (3, 4):
        for layer in range(2):
            shapes[f"sums{k}_{layer}"] = pltpu.VMEM(one + (512,), BF)
        for name, shape in landing_shapes(512).items():
            shapes[f"{name}{k}"] = shape
    shapes.update(Scratch.shapes)
    return shapes


def prepare_mask(region, maps, mask):
    named = lax.broadcasted_iota(jnp.int32, (128, 400), 0)
    row = jnp.concatenate([region[...], jnp.full((1, 204), -1, jnp.int32)], axis=1)
    hot = (named == row).astype(F32).astype(BF)
    places = mul(maps[0, 0, 0:256, :], hot, NT).astype(BF)
    for w in range(4):
        one = places[w * 64 : w * 64 + 64]
        off = (mul(one, one, NT) - 1.0) * 1e9
        off = jnp.concatenate([off, off], axis=1)
        mask[w] = jnp.concatenate([off] * 4, axis=1)


def place_vectors(ln_gain, ln_shift, lane):
    eight = jnp.concatenate([ln_gain[0], ln_gain[1], ln_shift[0], ln_shift[1]], axis=0)
    at = lax.broadcasted_iota(jnp.int32, (8, 128), 1) - lane
    out = jnp.zeros((8, 128), F32)
    for e in range(4):
        out = jnp.where(at == e, eight[:, e : e + 1], out)
    return out


def core_kernel(x, cot, w_qkv, w_proj, b, c, ln_gain, ln_shift, tables, region, rel_index,
                out, g, o_qkv, o_proj, ob, oc, o_gain, o_shift, o_tables, gb, gc, *rest):
    far, rest = dict(zip(SPILLED, rest[: len(SPILLED)])), rest[len(SPILLED) :]
    r = dict(zip(scratch_list(), rest))
    at = coords()
    core = at["c"]
    s = Scratch({name: r[name] for name in Scratch.shapes}, far, r["spills"])
    ga, wp, gd, tb, local, vec = [r[f"ga{k}"] for k in range(4)], r["wp"], r["gd"], r["tb"], r["local"], r["vec"]
    feed = Feed(core, gb, gc, r["wb"], r["wc"], r["feeds"])
    copy = Copier(at, r["send"], r["recv"])
    own = []

    def place(src, dst):
        put = pltpu.make_async_copy(src, dst, local.at[len(own)])
        put.start()
        own.append(put)

    wholes = [[w.at[layer] for w in ga + [gb, gc]] for layer in range(2)]
    orders = (ORDERS[0], ORDERS[1], ORDERS[2], ORDERS[0], ORDERS[1], ORDERS[2])
    for layer in range(2):
        for order, src, whole in zip(orders[4:], (b, c), wholes[layer][4:]):
            i1, i2, i3 = (at[axis] for axis in order)
            place(src.at[layer], whole.at[core, i3, i2, i1])
        for k in range(4):
            i1, i2, i3 = (at[axis] for axis in orders[k])
            if k < 3:
                tile = w_qkv[layer, k]
            else:
                four = w_proj[layer].astype(F32)
                tile = rows_of([four[n // 4 : n // 4 + 1, n % 4 * 128 : n % 4 * 128 + 128] for n in range(16)])
            ga[k][layer, core, i3, i2, i1] = tile.astype(BF)
    start = pltpu.make_async_copy(cot, g, local.at[8])
    start.start()
    lane = 4 * ((at["x"] * 2 + at["z"] % 2) * 4 + (at["z"] // 2) * 2 + core)
    gd[core, at["z"], at["y"], at["x"]] = place_vectors(ln_gain, ln_shift, lane)
    mine = (at["z"] // 2) * 2 + core
    rel = r["rel"]
    rel[...] = jnp.full(rel.shape, -1, jnp.int32)
    rel[0:49, 0:49] = rel_index[...]
    turned = rel[...].T
    rel[...] = jnp.full(rel.shape, -1, jnp.int32)
    rel[0:64, 0:64] = turned[0:64, 0:64]
    rel[0:64, 64:128] = turned[0:64, 0:64]
    tb[mine] = jnp.zeros((2, 8, 256), F32)
    for layer in range(2):
        for k in range(4):
            tb[mine, k % 2, layer * 2 + k // 2 : layer * 2 + k // 2 + 1, 0:169] = tables[layer, k : k + 1, :]
    enter(at, PEERS)
    for put in own:
        put.wait()
    def some(layer, ks, ring=False):
        return Gather(copy, at, [(orders[k], wholes[layer][k]) for k in ks], ring).stages

    early, mid, late = some(0, (0, 1, 2)), some(0, (3,)), some(0, (4, 5), True)
    next_early, next_late = some(1, (0, 1, 2, 3)), some(1, (4, 5), True)
    small = {}

    def small_start(axis, ref):
        steps = (1,) if axis == "c" else (1, 2, 3)
        small[axis] = [copy(ref, ref, axis, step) for step in steps]

    def small_end(axis):
        for one in small[axis]:
            one.wait_recv()

    early[0]()
    small_start("x", gd.at[core, at["z"], at["y"], at["x"]])
    pair = copy(tb.at[mine], tb.at[mine], "z", 2)
    for one in (mid, late, next_early, next_late):
        one[0]()
    maps, pack = r["maps"], r["pack"]
    window_maps(maps)
    proj_maps(pack)
    prepare_mask(region, maps, r["mask"])
    r["gbias"][...] = jnp.zeros(r["gbias"].shape, F32)
    early[1]()
    late[1]()
    mid[1]()
    small_end("x")
    small_start("y", gd.at[core, at["z"], at["y"]])
    pair.wait_recv()
    other = (mine + 2) % 4
    across = [copy(tb.at[k], tb.at[k], "c", 1) for k in (mine, other)]
    early[2]()
    small_end("y")
    small_start("z", gd.at[core, at["z"]])
    late[2]()
    mid[2]()
    for one in across:
        one.wait_recv()
    build_bias(tb, rel, r["bias"])
    small_end("z")
    small_start("c", gd.at[core])
    early[3]()
    small_end("c")
    vecs = r["vecs"]
    for y in range(4):
        total = gd[0, 0, y, 0]
        for n in range(1, 32):
            total = total + gd[n // 16, n // 4 % 4, y, n % 4]
        vecs[:, y * 128 : y * 128 + 128] = total
    early[4]()
    gain = [[vecs[l * 2 + k : l * 2 + k + 1] for k in range(2)] for l in range(2)]
    shift = [[vecs[4 + l * 2 + k : 5 + l * 2 + k] for k in range(2)] for l in range(2)]
    start.wait()

    def unpack_proj(layer):
        for block in range(8):
            tiles = []
            for n in range(16):
                tiles.append(ga[3][(layer,) + slot_of(0, block * 16 + n)])
            tiles = rows_of(tiles)
            for q in range(4):
                wp[layer, block * 64 : block * 64 + 64, q * 128 : q * 128 + 128] = mul(pack[q], tiles).astype(BF)

    forward_plans = (
        {
            "qkv": [mid[3], next_early[1], next_late[1]],
            "half_scores": [late[3]],
            "scores": [mid[4], lambda: unpack_proj(0), next_early[2]],
            "feed_forward": [late[4], next_late[2], late[5]],
            "chunks": [next_early[3]],
            "end": [next_early[4], lambda: unpack_proj(1)],
        },
        {"qkv": [next_late[3]], "feed_forward": [next_late[4], next_late[5]]},
    )
    x1 = r["x1"]
    for layer, before, after in ((0, x, x1), (1, x1, out)):

        def reached(name, plan=forward_plans[layer]):
            for one in plan.get(name, ()):
                one()

        forward(layer, before, after, gain, shift, ga, feed, wp, maps, r["bias"], r["mask"], s, reached)

    def chunk_part(ref, k, n):
        z = pl.ds(2 * (n % 2), 2)
        return ref.at[:, z] if k == 3 else ref.at[:, :, z]

    def chunk_over(k, n):
        sem = (k - 3) * 4 + n
        return pltpu.make_async_remote_copy(
            src_ref=(s.stage_b if k == 3 else s.stage_c).at[n % 2],
            dst_ref=chunk_part(r[f"landed{k}"], k, n),
            send_sem=r["cross_send"].at[sem],
            recv_sem=r["cross_recv"].at[sem],
            device_id=moved(at, "c", 1),
            device_id_type=MESH,
        )

    def chunk_here(layer, k, n):
        src = (s.stage_b if k == 3 else s.stage_c).at[n % 2]
        return pltpu.make_async_copy(
            src, chunk_part(r[f"sums{k}_{layer}"], k, n), r["cross_send"].at[(k - 3) * 4 + n]
        )

    def grads_of(layer):
        first = 0 if layer else 2

        def away(n):
            return jnp.logical_and(n >= first, n < first + 2)

        def send_grads(n):
            for k in (3, 4):
                pl.when(away(n))(lambda k=k: chunk_over(k, n).start())
                pl.when(jnp.logical_not(away(n)))(lambda k=k: chunk_here(layer, k, n).start())

        def wait_grads(n):
            for k in (3, 4):
                pl.when(away(n))(lambda k=k: chunk_over(k, n).wait_send())
                pl.when(jnp.logical_not(away(n)))(lambda k=k: chunk_here(layer, k, n).wait())

        def arrived(k):
            for n in (first, first + 1):
                chunk_over(k, n).wait_recv()

        return send_grads, wait_grads, arrived

    def out_of(ref, layer, lanes):
        def put(total):
            ref[layer, :, lanes] = total

        return put

    def feed_forward_scatter(layer):
        families = []
        for k, ref in ((3, ob), (4, oc)):
            family = {name: r[f"{name}{k}"] for name in landing_shapes(512)}
            family.update(order=FAMILIES[k][0], sums=r[f"sums{k}_{layer}"], out=out_of(ref, layer, slice(0, 512)))
            families.append(family)
        arrived = grads_of(layer)[2]
        return Scatter(copy, at, families, lambda n: arrived(n + 3))

    def heads_out(layer, k):
        def put(total):
            o_qkv[layer, k] = total[:, 0:128]
            if k == 2:
                for n in range(16):
                    lanes = slice(n % 4 * 128, n % 4 * 128 + 128)
                    o_proj[layer, n // 4 : n // 4 + 1, lanes] = total[n : n + 1, 128:256]

        return put

    def heads_scatter(layer):
        families, crossing = [], []
        for k in range(3):
            family = {name: r[f"{name}{k}_{layer}"] for name in landing_shapes(128)}
            both = r[f"both{k}_{layer}"]
            family.update(order=FAMILIES[k][0], sums=both.at[core], out=heads_out(layer, k))
            families.append(family)

        def cross(k):
            crossing.append(copy(r[f"both{k}_{layer}"].at[1 - core], r[f"landed{k}_{layer}"], "c", 1))

        return Scatter(copy, at, families, lambda n: crossing[n].wait_recv()), cross

    wide = {layer: feed_forward_scatter(layer) for layer in (0, 1)}
    heads = {layer: heads_scatter(layer) for layer in (0, 1)}
    tab, tab_pair, tab_sum, vec_sum = r["tab"], r["tab_pair"], r["tab_sum"], r["vec_sum"]
    vec_land, tab_cross, tab_land = r["vec_land"], r["tab_cross"], r["tab_land"]

    def keep_in(ref):
        def keep(total):
            ref[...] = total

        return keep

    def keep_vectors(total):
        lanes = lax.broadcasted_iota(jnp.int32, (8, 128), 1) - lane
        four = jnp.concatenate(
            [jnp.sum(jnp.where(lanes == e, total, 0.0), axis=1, keepdims=True) for e in range(4)], axis=1
        )
        for layer in range(2):
            o_gain[layer] = four[layer * 2 : layer * 2 + 2]
            o_shift[layer] = four[layer * 2 + 4 : layer * 2 + 6]

    def keep_tables(total):
        for layer in range(2):
            for k in range(4):
                row = layer * 2 + k // 2
                o_tables[layer, k : k + 1, :] = total[row : row + 1, k % 2 * 256 : k % 2 * 256 + 169]

    vec_sums = Sums(
        copy,
        at,
        [
            ("y", 4, lambda j: vec.at[:, pl.ds(pl.multiple_of(j * 128, 128), 128)], vec_land.at[0], keep_in(vec_sum)),
            ("x", 4, vec_sum, vec_land.at[1], keep_in(vec_sum)),
            ("z", 4, vec_sum, vec_land.at[2], keep_in(vec_sum)),
            ("c", 2, vec_sum, vec_land.at[3], keep_vectors),
        ],
    )
    tab_sums = Sums(
        copy,
        at,
        [
            ("c", 2, lambda j: tab.at[j], tab_cross, keep_in(tab_pair)),
            ("z", 4, lambda j: tab_pair.at[j // 2], tab_land.at[0], keep_in(tab_sum)),
            ("x", 4, tab_sum, tab_land.at[1], keep_in(tab_sum)),
            ("y", 4, tab_sum, tab_land.at[2], keep_tables),
        ],
    )

    def tables_done():
        table_sums(r["gbias"], rel, tab)

    def stage(sums, n):
        return lambda: sums.stages[n]()

    high_wide, low_wide, high_heads, low_heads = wide[1], wide[0], heads[1][0], heads[0][0]
    plans = {
        1: {
            "feed_forward": [stage(high_wide, 0)],
            "half_scores": [stage(high_wide, 1)],
            "end": [stage(high_wide, 2)],
        },
        0: {
            "chunks": [stage(high_wide, 3), stage(high_heads, 0)],
            "feed_forward": [stage(high_heads, 1), stage(low_wide, 0), stage(high_wide, 4)],
            "half_scores": [stage(high_heads, 2), stage(low_wide, 1)],
            "scores": [tables_done, stage(tab_sums, 0), stage(high_heads, 3)],
            "qkv": [stage(tab_sums, 1), stage(low_wide, 2), stage(high_heads, 4)],
            "gn1": [stage(low_heads, 0), stage(tab_sums, 2)],
            "end": [
                stage(vec_sums, 0),
                stage(low_heads, 1),
                stage(tab_sums, 3),
                stage(vec_sums, 1),
                stage(low_wide, 3),
                stage(low_heads, 2),
                stage(tab_sums, 4),
                stage(vec_sums, 2),
                stage(low_wide, 4),
                stage(low_heads, 3),
                stage(vec_sums, 3),
                stage(low_heads, 4),
                stage(vec_sums, 4),
            ],
        },
    }
    for layer, before in ((1, x1), (0, x)):

        def poll(name, plan=plans[layer]):
            for one in plan.get(name, ()):
                one()

        send, wait, _ = grads_of(layer)
        backward_mlp(layer, g, gain, feed, s, vec, send, wait, poll)
        backward_heads(
            layer, before, g, gain, ga, wp, maps, pack, r["gbias"], s, vec,
            [r[f"both{k}_{layer}"] for k in range(3)], poll, heads[layer][1],
        )
    copy.finish()


def hand_over_kernel(*refs):
    sems = refs[-1]
    count = len(refs) // 2
    copies = [pltpu.make_async_copy(refs[n], refs[count + n], sems.at[n]) for n in range(count)]
    for one in copies:
        one.start()
    for one in copies:
        one.wait()


def hand_over(arrays):
    far, vmem = pl.BlockSpec(memory_space=pl.ANY), pl.BlockSpec(memory_space=pltpu.VMEM)
    return pl.pallas_call(
        hand_over_kernel,
        out_shape=[jax.ShapeDtypeStruct(one.shape, one.dtype) for one in arrays],
        in_specs=[vmem] * len(arrays),
        out_specs=[far] * len(arrays),
        scratch_shapes=[pltpu.SemaphoreType.DMA((len(arrays),))],
        compiler_params=pltpu.CompilerParams(vmem_limit_bytes=63 * 2**20),
        name="hand_over",
    )(*arrays)


def shards(
    inputs, w_qkv, w_proj, w_up, w_down, ln_gain, ln_shift, tables, region, rel_index, cotangent
):
    w_qkv, tables = w_qkv.transpose(0, 2, 1, 3), tables.transpose(0, 2, 1)
    tiles = jax.ShapeDtypeStruct((2, 2, 4, 4, 4, 16, 512), BF)
    rows = jax.ShapeDtypeStruct((ROWS, WIDTH), F32)
    vmem, far = pl.BlockSpec(memory_space=pltpu.VMEM), pl.BlockSpec(memory_space=pl.ANY)
    spills = [jax.ShapeDtypeStruct(Scratch.shapes[name].shape, Scratch.shapes[name].dtype) for name in SPILLED]
    grads = [
        jax.ShapeDtypeStruct(one.shape, F32) for one in (w_qkv, w_proj, w_up, w_down, ln_gain, ln_shift, tables)
    ]
    outs = pl.pallas_call(
        core_kernel,
        out_shape=[rows, rows] + grads + [tiles, tiles] + spills,
        in_specs=[vmem, far, vmem, vmem, far, far] + [vmem] * 5,
        out_specs=[vmem] * 9 + [far] * (2 + len(spills)),
        scratch_shapes=list(scratch_list().values()),
        compiler_params=pltpu.CompilerParams(
            vmem_limit_bytes=63 * 2**20, collective_id=0, has_side_effects=True
        ),
        name="both_blocks",
    )(
        inputs, cotangent, w_qkv, w_proj, w_up, w_down, ln_gain, ln_shift, tables, region.reshape(1, -1), rel_index
    )
    out, g, o_qkv, o_proj, ob, oc, o_gain, o_shift, o_tables = hand_over(outs[:9])
    return out, g, o_qkv.transpose(0, 2, 1, 3), o_proj, ob, oc, o_gain, o_shift, o_tables.transpose(0, 2, 1)


def solution(mesh):
    return jax.shard_map(
        shards,
        mesh=mesh,
        in_specs=(
            P(("dp", "tensor"), None),
            P(None, "dp", None, "tensor"),
            P(None, ("tensor", "dp"), None),
            P(None, "dp", "tensor"),
            P(None, ("tensor", "dp"), None),
            P(None, None, ("dp", "tensor")),
            P(None, None, ("dp", "tensor")),
            P(None, None, "tensor"),
            P(),
            P(),
            P(("dp", "tensor"), None),
        ),
        out_specs=(
            P(("dp", "tensor"), None),
            P(("dp", "tensor"), None),
            P(None, "dp", None, "tensor"),
            P(None, ("tensor", "dp"), None),
            P(None, "dp", "tensor"),
            P(None, ("tensor", "dp"), None),
            P(None, None, ("dp", "tensor")),
            P(None, None, ("dp", "tensor")),
            P(None, None, "tensor"),
        ),
        check_vma=False,
    )
```

```python
import functools
import jax
import jax.numpy as jnp
from jax import lax
from jax.experimental import pallas as pl
from jax.experimental.pallas import tpu as pltpu
from jax.sharding import PartitionSpec as P

MESH = pl.DeviceIdType.MESH
ORDERS = (("x", "y", "z"), ("y", "z", "x"), ("z", "x", "y"))


def coords():
    dp, tp = lax.axis_index("dp"), lax.axis_index("tensor")
    return {
        "y": dp // 8,
        "x": (dp // 2) % 4,
        "z": (tp // 2) * 2 + dp % 2,
        "c": tp % 2,
    }


def device(at):
    return (at["y"] * 8 + at["x"] * 2 + at["z"] % 2, (at["z"] // 2) * 2 + at["c"])


def moved(at, axis, step):
    size = 2 if axis == "c" else 4
    return device({**at, axis: (at[axis] + step) % size})


NEIGHBOURS = (("x", 1), ("x", 3), ("y", 1), ("y", 3), ("z", 1), ("z", 3), ("c", 1))


def enter(at, peers=NEIGHBOURS):
    barrier = pltpu.get_barrier_semaphore()
    for axis, step in peers:
        pl.semaphore_signal(barrier, inc=1, device_id=moved(at, axis, step), device_id_type=MESH)
    pl.semaphore_wait(barrier, len(peers))


PEERS = NEIGHBOURS + (("x", 2), ("y", 2), ("z", 2))
COPIES = 305


class Copier:
    def __init__(self, at, send, recv):
        self.at, self.send, self.recv, self.made = at, send, recv, []

    def __call__(self, src, dst, axis, step):
        slot = len(self.made)
        assert slot < COPIES
        copy = pltpu.make_async_remote_copy(
            src_ref=src,
            dst_ref=dst,
            send_sem=self.send.at[slot],
            recv_sem=self.recv.at[slot],
            device_id=moved(self.at, axis, step),
            device_id_type=MESH,
        )
        copy.start()
        self.made.append(copy)
        return copy

    def finish(self):
        for copy in self.made:
            copy.wait_send()


def add_into(dst, *terms):
    lead = dst.shape[:-3]
    count = 1
    for size in lead:
        count *= size

    def body(n, carry):
        index = []
        for size in reversed(lead):
            index.append(n % size)
            n = n // size
        index = tuple(reversed(index)) or slice(None)
        total = dst[index].astype(jnp.float32)
        for term in terms:
            total = total + term[index].astype(jnp.float32)
        dst[index] = total.astype(dst.dtype)
        return carry

    if count == 1:
        body(0, 0)
    else:
        lax.fori_loop(0, count, body, 0)


class Scatter:
    def __init__(self, copy, at, families, crossing):
        self.copy, self.at, self.families, self.crossing = copy, at, families, crossing
        self.held = [{} for _ in families]
        self.stages = [self.join, self.along, self.second, self.third, self.finish]

    def places(self, family):
        i1, i2, i3 = (self.at[axis] for axis in family["order"])
        return i1, i2, i3

    def join(self):
        for n, (family, held) in enumerate(zip(self.families, self.held)):
            self.crossing(n)
            _, _, i3 = self.places(family)
            axis, sums, landed = family["order"][2], family["sums"], family["landed"]
            far = (i3 + 2) % 4
            add_into(sums.at[far], landed.at[far])
            held["r"] = self.copy(sums.at[far, 0:2], family["half"].at[0], axis, 1)
            held["l"] = self.copy(sums.at[far, 2:4], family["half"].at[1], axis, 3)
        for family in self.families:
            _, _, i3 = self.places(family)
            for step in (1, 3, 0):
                j = (i3 + step) % 4
                add_into(family["sums"].at[j], family["landed"].at[j])

    def along(self):
        for family, held in zip(self.families, self.held):
            _, _, i3 = self.places(family)
            axis, sums = family["order"][2], family["sums"]
            right, left = (i3 + 1) % 4, (i3 + 3) % 4
            held["r"].wait_recv()
            add_into(sums.at[right, 0:2], family["half"].at[0])
            held["r2"] = self.copy(sums.at[right], family["full"].at[0], axis, 1)
            held["l"].wait_recv()
            add_into(sums.at[left, 2:4], family["half"].at[1])
            held["l2"] = self.copy(sums.at[left], family["full"].at[1], axis, 3)

    def second(self):
        for family, held in zip(self.families, self.held):
            _, i2, i3 = self.places(family)
            axis, sums = family["order"][1], family["sums"]
            held["r2"].wait_recv()
            held["l2"].wait_recv()
            add_into(sums.at[i3], family["full"].at[0], family["full"].at[1])
            held["2"] = [
                self.copy(sums.at[i3, (i2 + step) % 4], family["two"].at[step - 1], axis, step) for step in (2, 1, 3)
            ]

    def third(self):
        for family, held in zip(self.families, self.held):
            i1, i2, i3 = self.places(family)
            axis, sums = family["order"][0], family["sums"]
            for one in held["2"]:
                one.wait_recv()
            add_into(sums.at[i3, i2], *(family["two"].at[k] for k in range(3)))
            held["1"] = [
                self.copy(sums.at[i3, i2, (i1 + step) % 4], family["one"].at[step - 1], axis, step)
                for step in (2, 1, 3)
            ]

    def finish(self):
        for family, held in zip(self.families, self.held):
            i1, i2, i3 = self.places(family)
            for one in held["1"]:
                one.wait_recv()
            total = family["sums"][i3, i2, i1].astype(jnp.float32)
            for k in range(3):
                total = total + family["one"][k].astype(jnp.float32)
            family["out"](total)


def landing_shapes(width):
    bf = jnp.bfloat16
    return {
        "landed": pltpu.VMEM((4, 4, 4, 16, width), bf),
        "half": pltpu.VMEM((2, 2, 4, 16, width), bf),
        "full": pltpu.VMEM((2, 4, 4, 16, width), bf),
        "two": pltpu.VMEM((3, 4, 16, width), bf),
        "one": pltpu.VMEM((3, 16, width), bf),
    }


WINDOW = 7
SIDE = 14
EPS = 1e-05


BF, F32 = jnp.bfloat16, jnp.float32
SCALE = 32.0 ** -0.5
ROWS, PADDED, WIDTH = 784, 1024, 512
NN = (((1,), (0,)), ((), ()))
NT = (((1,), (1,)), ((), ()))
TN = (((0,), (0,)), ((), ()))


def mul(a, b, dims=NN):
    return lax.dot_general(a, b, dims, preferred_element_type=F32)


def window_maps(maps):
    n = lax.broadcasted_iota(jnp.int32, (512, 1), 0)
    place = n % 64
    token = lax.broadcasted_iota(jnp.int32, (512, 400), 1)
    for layer in range(2):
        row = n // 128 % 2 * 7 + place // 7
        col = n // 64 % 2 * 7 + place % 7
        if layer:
            row, col = (row + 3) % 14, (col + 3) % 14
        taken = jnp.where(place < 49, n // 256 * 196 + row * 14 + col, -100)
        for pair in range(2):
            maps[layer, pair] = (token == taken + 8 * pair).astype(F32).astype(BF)


def proj_maps(pack):
    n = lax.broadcasted_iota(jnp.int32, (64, 1), 0)
    packed = lax.broadcasted_iota(jnp.int32, (64, 256), 1)
    for q in range(4):
        pack[q] = (packed == n // 4 * 16 + n % 4 * 4 + q).astype(F32).astype(BF)


PLACES = [(y, x, zl) for y in range(4) for x in range(4) for zl in range(2)]


def rows_of(tiles):
    return jnp.concatenate(tiles, axis=0)


def up_block(wb, slot):
    return rows_of([wb[slot, x, zl, y] for y, x, zl in PLACES])


def down_block(wc, slot):
    return rows_of([wc[slot, y, x, zl] for y, x, zl in PLACES])


def slot_of(k, dev):
    t, (y, x, zl) = dev // 32, PLACES[dev % 32]
    at = {"x": x, "y": y, "z": 2 * (t // 2) + zl}
    return (t % 2,) + tuple(at[axis] for axis in reversed(ORDERS[k]))


def qkv_block(ga, layer, s):
    return jnp.concatenate(
        [rows_of([ga[s][(layer,) + slot_of(s, t * 32 + n)] for n in range(32)]) for t in range(4)], axis=1
    )


def norm_parts(values):
    mean = jnp.mean(values, axis=1, keepdims=True)
    centered = values - mean
    r = lax.rsqrt(jnp.mean(centered * centered, axis=1, keepdims=True) + EPS)
    return centered * r, r


def norm_back(grad, values, gain):
    xhat, r = norm_parts(values)
    e = grad * gain
    through = r * (
        e - jnp.mean(e, axis=1, keepdims=True) - xhat * jnp.mean(e * xhat, axis=1, keepdims=True)
    )
    return (
        through,
        jnp.sum(grad * xhat, axis=0, keepdims=True),
        jnp.sum(grad, axis=0, keepdims=True),
    )


C0, C1 = 0.7978845608028654, 0.044715


def gelu(u):
    return 0.5 * u * (1.0 + jnp.tanh(C0 * u * (1.0 + C1 * (u * u))))


def gelu_both(u):
    square = u * u
    t = jnp.tanh(C0 * u * (1.0 + C1 * square))
    half = 0.5 * (1.0 + t)
    slope = half + (0.5 * C0) * u * (1.0 - t * t) * (1.0 + (3.0 * C1) * square)
    return u * half, slope


def to_windows_of(maps, layer, tokens):
    return [mul(maps[layer, pair], tokens[pair * 384 : pair * 384 + 400, :]) for pair in range(2)]


def from_windows_of(maps, layer, rows):
    first = mul(maps[layer, 0], rows[0:512, :], TN)
    second = mul(maps[layer, 1], rows[512:1024, :], TN)
    return jnp.concatenate(
        [first[:384], first[384:400] + second[:16], second[16:]], axis=0
    )


def head_masks():
    lane = lax.broadcasted_iota(jnp.int32, (1, 128), 1) // 32
    return [lane == h for h in range(4)]


def spread(v, masks):
    return jnp.concatenate([jnp.where(m, v, jnp.zeros((), v.dtype)) for m in masks], axis=0)


def fold(r, masks):
    out = r[0:64]
    for h in range(1, 4):
        out = jnp.where(masks[h], r[h * 64 : h * 64 + 64], out)
    return out


UNROLL = 4


def columns(s, q):
    return slice(s * 512 + q * 128, s * 512 + q * 128 + 128)


def scores_of(ref, layer, q):
    return ref.at[layer, q // 2, :, q % 2 * 256 : q % 2 * 256 + 256]


def window(w):
    return pl.ds(pl.multiple_of(w * 64, 64), 64)


def attend(layer, qkv, bias, mask, kept, out, part):
    masks = head_masks()

    def some(n, carry):
        items = [(n * UNROLL + u, u, q) for u in range(UNROLL) for q in range(4)]
        scores = [
            mul(qkv[window(w), columns(1, q)], spread(qkv[window(w), columns(0, q)], masks), NT) for w, u, q in items
        ]
        probs = []
        for (w, u, q), s in zip(items, scores):
            s = s * SCALE + scores_of(bias, layer, q)[...]
            if layer:
                s = s + mask[u % 4, :, 0:256]
            e = jnp.exp(s - jnp.max(s, axis=0, keepdims=True))
            p = (e * (1.0 / jnp.sum(e, axis=0, keepdims=True))).astype(BF)
            kept[w * 4 + q] = p
            probs.append(p)
        for (w, u, q), p in zip(items, probs):
            out[window(w), columns(0, q)] = fold(mul(p, qkv[window(w), columns(2, q)], TN), masks).astype(BF)
        return carry

    lax.fori_loop(part * 8 // UNROLL, (part + 1) * 8 // UNROLL, some, 0)


def attend_back(layer, qkv, kept, gout, gbias, part):
    masks = head_masks()

    def some(n, carry):
        items = [(n * UNROLL + u, q) for u in range(UNROLL) for q in range(4)]
        gprobs, gvs = [], []
        for w, q in items:
            d = spread(gout[window(w), columns(0, q)], masks)
            gprobs.append(mul(qkv[window(w), columns(2, q)], d, NT))
            gvs.append(mul(kept[w * 4 + q], d))
        for (w, q), gv in zip(items, gvs):
            qkv[window(w), columns(2, q)] = gv.astype(BF)
        gscores = []
        for (w, q), gp in zip(items, gprobs):
            p = kept[w * 4 + q].astype(F32)
            pg = p * gp
            gscores.append(pg - p * jnp.sum(pg, axis=0, keepdims=True))
        for q in range(4):
            place = scores_of(gbias, layer, q)
            total = place[...]
            for (w, h), gs in zip(items, gscores):
                if h == q:
                    total = total + gs
            place[...] = total
        for (w, q), gs in zip(items, gscores):
            ds = gs.astype(BF)
            query, key = qkv[window(w), columns(0, q)], qkv[window(w), columns(1, q)]
            gk = mul(ds, spread(query, masks)) * SCALE
            gq = fold(mul(ds, key, TN), masks) * SCALE
            qkv[window(w), columns(0, q)] = gq.astype(BF)
            qkv[window(w), columns(1, q)] = gk.astype(BF)
        return carry

    lax.fori_loop(part * 8 // UNROLL, (part + 1) * 8 // UNROLL, some, 0)


SPILLED = ("n1w", "qkv", "kept", "att", "mid", "n2", "hid")


def forward(layer, x, result, gain, shift, ga, feed, wp, maps, bias, mask, s, poll):
    def ready(name):
        if layer:
            s.spilled(name)

    def done(name):
        if not layer:
            s.spill(name)

    xhat, _ = norm_parts(x[...])
    s.low[...] = (xhat * gain[layer][0] + shift[layer][0]).astype(BF)
    ready("n1w")
    for pair, part in enumerate(to_windows_of(maps, layer, s.low)):
        s.n1w[pair * 512 : pair * 512 + 512, :] = part.astype(BF)
    done("n1w")
    ready("qkv")
    for k in range(3):
        s.qkv[:, k * 512 : k * 512 + 512] = mul(s.n1w[...], qkv_block(ga, layer, k)).astype(BF)
    done("qkv")
    poll("qkv")
    ready("kept")
    attend(layer, s.qkv, bias, mask, s.kept, s.ow, 0)
    poll("half_scores")
    attend(layer, s.qkv, bias, mask, s.kept, s.ow, 1)
    done("kept")
    poll("scores")
    ready("att")
    s.att[...] = from_windows_of(maps, layer, s.ow).astype(BF)
    done("att")
    ready("mid")
    s.mid[...] = x[...] + mul(s.att[...], wp[layer])
    done("mid")
    poll("feed_forward")
    feed.fetch(layer, 0, 0)
    ready("n2")
    xhat, _ = norm_parts(s.mid[...])
    s.n2[...] = (xhat * gain[layer][1] + shift[layer][1]).astype(BF)
    done("n2")
    result[...] = s.mid[...]
    ready("hid")

    def chunk(t, carry):
        slot = feed.take(t)

        @pl.when(t < 3)
        def _():
            feed.fetch(layer, t + 1, t + 1)

        if layer:
            pl.when(t == 3)(lambda: feed.fetch(1, feed.turn(1, 0), 0))
        hidden = mul(s.n2[...], up_block(feed.wb, slot))
        s.hid[t] = hidden.astype(BF)
        result[...] += mul(gelu(hidden).astype(BF), down_block(feed.wc, slot))
        return carry

    lax.fori_loop(0, 2, chunk, 0)
    poll("chunks")
    lax.fori_loop(2, 4, chunk, 0)
    done("hid")
    poll("end")


def backward_mlp(layer, g, gain, feed, s, vec, send_grads, wait_grads, poll):
    if not layer:
        s.returned("hid")
        s.returned("n2")
    s.low[...] = g[...].astype(BF)
    s.gn[0:ROWS, :] = jnp.zeros((ROWS, WIDTH), F32)

    def chunk(n, carry):
        t = feed.turn(layer, n)
        slot = feed.take(n)

        @pl.when(n < 3)
        def _():
            feed.fetch(layer, feed.turn(layer, n + 1), n + 1)

        if layer:
            pl.when(n == 3)(lambda: feed.fetch(0, feed.turn(0, 0), 0))

        active, slope = gelu_both(s.hid[t])
        gh = (mul(s.low[...], down_block(feed.wc, slot), NT) * slope.astype(F32)).astype(BF)
        pl.when(n >= 2)(lambda: wait_grads(n - 2))
        gdown = mul(active.astype(BF), s.low[...], TN).astype(BF)
        for k, (y, xx, zl) in enumerate(PLACES):
            s.stage_c[slot, y, xx, zl] = gdown[k * 16 : k * 16 + 16]
        gup = mul(s.n2[...], gh, TN).astype(BF)
        for k, (y, xx, zl) in enumerate(PLACES):
            s.stage_b[slot, xx, zl, y] = gup[k * 16 : k * 16 + 16]
        send_grads(n)
        s.gn[0:ROWS, :] += mul(gh, up_block(feed.wb, slot), NT)
        return carry

    lax.fori_loop(0, 2, chunk, 0)
    poll("chunks")
    lax.fori_loop(2, 4, chunk, 0)
    wait_grads(jnp.int32(2))
    wait_grads(jnp.int32(3))
    poll("feed_forward")
    if layer:
        s.bring("hid")
        s.bring("n2")
    else:
        s.returned("mid")
    through, dg, ds = norm_back(s.gn[0:ROWS, :], s.mid[...], gain[layer][1])
    vec[layer * 2 + 1 : layer * 2 + 2] = dg
    vec[layer * 2 + 5 : layer * 2 + 6] = ds
    if layer:
        s.bring("mid")
    g[...] += through


def backward_heads(layer, x, g, gain, ga, wp, maps, pack, gbias, s, vec, both, poll, cross):
    s.low[...] = g[...].astype(BF)
    if not layer:
        s.returned("att")
    gproj = mul(s.att[...], s.low[...], TN).astype(BF)
    if layer:
        s.bring("att")
    for block in range(8):
        part = gproj[block * 64 : block * 64 + 64]
        packed = mul(pack[0], part[:, 0:128], TN)
        for q in range(1, 4):
            packed = packed + mul(pack[q], part[:, q * 128 : q * 128 + 128], TN)
        packed = packed.astype(BF)
        for n in range(16):
            both[2][slot_of(2, block * 16 + n) + (slice(None), slice(128, 256))] = packed[n * 16 : n * 16 + 16]
    poll("proj")
    for pair, part in enumerate(to_windows_of(maps, layer, s.low)):
        s.ow[pair * 512 : pair * 512 + 512, :] = part.astype(BF)
    s.ow[...] = mul(s.ow[...], wp[layer], NT).astype(BF)
    poll("gatt")
    if not layer:
        s.returned("qkv")
        s.returned("kept")
    attend_back(layer, s.qkv, s.kept, s.ow, gbias, 0)
    poll("half_scores")
    attend_back(layer, s.qkv, s.kept, s.ow, gbias, 1)
    if layer:
        s.bring("kept")
    poll("scores")
    if not layer:
        s.returned("n1w")
    for k in range(3):
        gw = mul(s.n1w[...], s.qkv[:, k * 512 : k * 512 + 512], TN).astype(BF)
        for dev in range(128):
            t, n = dev // 32, dev % 32
            both[k][slot_of(k, dev) + (slice(None), slice(0, 128))] = gw[n * 16 : n * 16 + 16, t * 128 : t * 128 + 128]
        cross(k)
    poll("qkv")
    if layer:
        s.bring("n1w")
    total = mul(s.qkv[:, 0:512], qkv_block(ga, layer, 0), NT)
    for k in range(1, 3):
        total = total + mul(s.qkv[:, k * 512 : k * 512 + 512], qkv_block(ga, layer, k), NT)
    s.ow[...] = total.astype(BF)
    if layer:
        s.bring("qkv")
    poll("gn1")
    through, dg, ds = norm_back(from_windows_of(maps, layer, s.ow), x[...], gain[layer][0])
    vec[layer * 2 : layer * 2 + 1] = dg
    vec[layer * 2 + 4 : layer * 2 + 5] = ds
    g[...] += through
    poll("end")


class Feed:
    def __init__(self, core, gb, gc, wb, wc, sems):
        self.core, self.gb, self.gc, self.wb, self.wc, self.sems = core, gb, gc, wb, wc, sems

    def turn(self, layer, n):
        mine = self.core if layer == 0 else 1 - self.core
        first = jnp.where(n < 2, mine, 1 - mine)
        return 2 * (n % 2) + first

    def copies(self, layer, t, n):
        slot, z = n % 2, pl.ds(2 * (t // 2), 2)
        return (
            pltpu.make_async_copy(self.gb.at[layer, t % 2, :, z], self.wb.at[slot], self.sems.at[slot]),
            pltpu.make_async_copy(self.gc.at[layer, t % 2, :, :, z], self.wc.at[slot], self.sems.at[2 + slot]),
        )

    def fetch(self, layer, t, n):
        for one in self.copies(layer, t, n):
            one.start()

    def take(self, n):
        for one in self.copies(0, 0, n):
            one.wait()
        return n % 2


class Scratch:
    shapes = {
        "low": pltpu.VMEM((ROWS, WIDTH), BF),
        "n1w": pltpu.VMEM((PADDED, WIDTH), BF),
        "qkv": pltpu.VMEM((PADDED, 3 * WIDTH), BF),
        "kept": pltpu.VMEM((64, 64, 256), BF),
        "ow": pltpu.VMEM((PADDED, WIDTH), BF),
        "att": pltpu.VMEM((ROWS, WIDTH), BF),
        "mid": pltpu.VMEM((ROWS, WIDTH), F32),
        "n2": pltpu.VMEM((ROWS, WIDTH), BF),
        "hid": pltpu.VMEM((4, ROWS, WIDTH), BF),
        "gn": pltpu.VMEM((ROWS, WIDTH), F32),
        "stage_b": pltpu.VMEM((2, 4, 2, 4, 16, 512), BF),
        "stage_c": pltpu.VMEM((2, 4, 4, 2, 16, 512), BF),
    }

    def __init__(self, refs, far, sems):
        self.__dict__.update(refs)
        self.far, self.sems = far, sems

    def out_copy(self, name):
        return pltpu.make_async_copy(getattr(self, name), self.far[name], self.sems.at[SPILLED.index(name)])

    def in_copy(self, name):
        return pltpu.make_async_copy(self.far[name], getattr(self, name), self.sems.at[SPILLED.index(name)])

    def spill(self, name):
        self.out_copy(name).start()

    def spilled(self, name):
        self.out_copy(name).wait()

    def bring(self, name):
        self.in_copy(name).start()

    def returned(self, name):
        self.in_copy(name).wait()


def axis_slots(whole, i2, i3):
    return (
        lambda j: whole.at[i3, i2, j],
        lambda j: whole.at[i3, j],
        lambda j: whole.at[j],
    )


class Gather:
    def __init__(self, copy, at, families, ring):
        self.copy, self.at, self.across = copy, at, []
        self.plans = []
        for order, whole in families:
            i1, i2, i3 = (at[axis] for axis in order)
            self.plans.append((order, (i1, i2, i3), axis_slots(whole.at[at["c"]], i2, i3), {}))
        if ring == 2:
            self.stages = [self.first, self.around, self.onward, self.third, self.forward, self.end, self.finish]
        elif ring == 1:
            self.stages = [self.first, self.second, self.third, self.forward, self.end, self.finish]
        else:
            self.stages = [self.first, self.second, self.straight, self.landed, self.finish]

    def pass_on(self, ref):
        self.across.append(self.copy(ref, ref, "c", 1))

    def first(self):
        for order, places, slots, held in self.plans:
            ref = slots[0](places[0])
            held["1"] = [self.copy(ref, ref, order[0], step) for step in (2, 1, 3)]

    def second(self):
        for order, places, slots, held in self.plans:
            for one in held["1"]:
                one.wait_recv()
            ref = slots[1](places[1])
            held["2"] = [self.copy(ref, ref, order[1], step) for step in (2, 1, 3)]

    def around(self):
        for order, places, slots, held in self.plans:
            for one in held["1"]:
                one.wait_recv()
            ref = slots[1](places[1])
            held["a"] = [self.copy(ref, ref, order[1], step) for step in (1, 3)]

    def onward(self):
        for order, places, slots, held in self.plans:
            held["2"] = []
            for n, (step, back) in enumerate(((1, 3), (3, 1))):
                held["a"][n].wait_recv()
                half = slots[1]((places[1] + back) % 4).at[2 * n : 2 * n + 2]
                held["2"].append(self.copy(half, half, order[1], step))

    def straight(self):
        for order, places, slots, held in self.plans:
            for one in held["2"]:
                one.wait_recv()
            ref = slots[2](places[2])
            held["3"] = [(step, self.copy(ref, ref, order[2], step)) for step in (1, 3, 2)]
            self.pass_on(ref)

    def landed(self):
        for n in range(3):
            for order, places, slots, held in self.plans:
                step, one = held["3"][n]
                one.wait_recv()
                self.pass_on(slots[2]((places[2] + 4 - step) % 4))

    def third(self):
        for order, places, slots, held in self.plans:
            for one in held["2"]:
                one.wait_recv()
            ref = slots[2](places[2])
            held["s"] = [self.copy(ref, ref, order[2], step) for step in (1, 3)]
            self.pass_on(ref)

    def forward(self):
        for order, places, slots, held in self.plans:
            held["f"] = []
            for n, (step, back) in enumerate(((1, 3), (3, 1))):
                held["s"][n].wait_recv()
                ref = slots[2]((places[2] + back) % 4)
                half = ref.at[2 * n : 2 * n + 2]
                held["f"].append(self.copy(half, half, order[2], step))
                self.pass_on(ref)

    def end(self):
        for order, places, slots, held in self.plans:
            for one in held["f"]:
                one.wait_recv()
            self.pass_on(slots[2]((places[2] + 2) % 4))

    def finish(self):
        for one in self.across:
            one.wait_recv()


def split3(v):
    high = v.astype(BF)
    rest = v - high.astype(F32)
    mid = rest.astype(BF)
    low = (rest - mid.astype(F32)).astype(BF)
    return jnp.concatenate([high, mid, low], axis=0)


def unsplit3(v):
    rows = v.shape[0] // 3
    return v[:rows] + v[rows : 2 * rows] + v[2 * rows :]


def build_bias(tb, rel, bias):
    sides = [split3(jnp.concatenate([tb[t, p] for t in range(4)], axis=0)) for p in range(2)]
    row = lax.broadcasted_iota(jnp.int32, (256, 64), 0)

    def keys(block, carry):
        eight = pl.ds(pl.multiple_of(block * 8, 8), 8)
        named = rel[eight, 0:64]
        both = []
        for k in range(8):
            hot = (row == named[k : k + 1]).astype(F32).astype(BF)
            both.append(jnp.concatenate([unsplit3(mul(side, hot)) for side in sides], axis=1))
        for t in range(4):
            for layer in range(2):
                for m in range(2):
                    n = t * 8 + layer * 2 + m
                    at = (t % 2) * 256 + m * 128
                    bias[layer, t // 2, eight, at : at + 128] = rows_of([one[n : n + 1] for one in both])
        return carry

    lax.fori_loop(0, 7, keys, 0)
    unused = lax.broadcasted_iota(jnp.int32, (16, 512), 0) >= 1
    for layer in range(2):
        for g in range(2):
            bias[layer, g, 48:64] = jnp.where(unused, F32(-1e30), bias[layer, g, 48:64])


def table_sums(gbias, rel, tab):
    row = lax.broadcasted_iota(jnp.int32, (512, 128), 0)
    lane = lax.broadcasted_iota(jnp.int32, (512, 128), 1)
    side = row // 256 == lane // 64
    named_row = jnp.where(side, row % 256, -2)
    none = jnp.zeros((4, 128), F32)

    def keys(block, total):
        eight = pl.ds(pl.multiple_of(block * 8, 8), 8)
        named = rel[eight, :]
        parts = {}
        for t in range(4):
            for layer in range(2):
                for m in range(2):
                    at = (t % 2) * 256 + m * 128
                    parts[t, layer, m] = gbias[layer, t // 2, eight, at : at + 128]
        for k in range(8):
            hot = (named_row == named[k : k + 1]).astype(F32).astype(BF)
            rows = []
            for t in range(4):
                rows += [parts[t, layer, m][k : k + 1] for layer in range(2) for m in range(2)] + [none]
            total = total + unsplit3(mul(split3(rows_of(rows)), hot, NT))
        return total

    total = lax.fori_loop(0, 7, keys, jnp.zeros((32, 512), F32))
    for t in range(4):
        tab[t % 2, t // 2] = total[t * 8 : t * 8 + 8]


class Sums:
    def __init__(self, copy, at, phases):
        self.stages = []
        sent = []

        def start(axis, size, part, landing):
            mine = at[axis]
            landing[mine] = (part(mine) if callable(part) else part)[...]
            for step in range(1, size):
                src = part((mine + step) % size) if callable(part) else landing.at[mine]
                sent.append(copy(src, landing.at[mine], axis, step))

        def end(size, landing, keep):
            while sent:
                sent.pop().wait_recv()
            total = landing[0]
            for k in range(1, size):
                total = total + landing[k]
            keep(total)

        for n, (axis, size, part, landing, keep) in enumerate(phases):
            before = phases[n - 1] if n else None

            def stage(axis=axis, size=size, part=part, landing=landing, before=before):
                if before:
                    end(before[1], before[3], before[4])
                start(axis, size, part, landing)

            self.stages.append(stage)
        last = phases[-1]
        self.stages.append(lambda: end(last[1], last[3], last[4]))


FAMILIES = ((ORDERS[0], 128), (ORDERS[1], 128), (ORDERS[2], 256), (ORDERS[1], 512), (ORDERS[2], 512))


def scratch_list():
    one = (4, 4, 4, 16)
    shapes = {
        **{f"ga{k}": pltpu.VMEM((2, 2, 4, 4, 4, 16, 128), BF) for k in range(4)},
        "wb": pltpu.VMEM((2, 4, 2, 4, 16, 512), BF),
        "wc": pltpu.VMEM((2, 4, 4, 2, 16, 512), BF),
        "x1": pltpu.VMEM((ROWS, WIDTH), F32),
        "wp": pltpu.VMEM((2, WIDTH, WIDTH), BF),
        "bias": pltpu.VMEM((2, 2, 64, 512), F32),
        "mask": pltpu.VMEM((4, 64, 512), F32),
        "rel": pltpu.VMEM((128, 128), jnp.int32),
        "maps": pltpu.VMEM((2, 2, 512, 400), BF),
        "pack": pltpu.VMEM((4, 64, 256), BF),
        "gbias": pltpu.VMEM((2, 2, 64, 512), F32),
        "vecs": pltpu.VMEM((8, WIDTH), F32),
        "vec": pltpu.VMEM((8, WIDTH), F32),
        "gd": pltpu.VMEM((2, 4, 4, 4, 8, 128), F32),
        "tb": pltpu.VMEM((4, 2, 8, 256), F32),
        "tab": pltpu.VMEM((2, 2, 8, 512), F32),
        "vec_sum": pltpu.VMEM((8, 128), F32),
        "vec_land": pltpu.VMEM((4, 4, 8, 128), F32),
        "tab_pair": pltpu.VMEM((2, 8, 512), F32),
        "tab_sum": pltpu.VMEM((8, 512), F32),
        "tab_cross": pltpu.VMEM((2, 2, 8, 512), F32),
        "tab_land": pltpu.VMEM((3, 4, 8, 512), F32),
        "feeds": pltpu.SemaphoreType.DMA((4,)),
        "send": pltpu.SemaphoreType.DMA((COPIES,)),
        "recv": pltpu.SemaphoreType.DMA((COPIES,)),
        "local": pltpu.SemaphoreType.DMA((12,)),
        "spills": pltpu.SemaphoreType.DMA((len(SPILLED),)),
        "cross_send": pltpu.SemaphoreType.DMA((8,)),
        "cross_recv": pltpu.SemaphoreType.DMA((8,)),
    }
    for k in range(3):
        width = FAMILIES[k][1]
        for layer in range(2):
            shapes[f"both{k}_{layer}"] = pltpu.VMEM((2,) + one + (width,), BF)
            for name, shape in landing_shapes(width).items():
                shapes[f"{name}{k}_{layer}"] = shape
    for k in (3, 4):
        for layer in range(2):
            shapes[f"sums{k}_{layer}"] = pltpu.VMEM(one + (512,), BF)
        for name, shape in landing_shapes(512).items():
            shapes[f"{name}{k}"] = shape
    shapes.update(Scratch.shapes)
    return shapes


def prepare_mask(region, maps, mask):
    named = lax.broadcasted_iota(jnp.int32, (128, 400), 0)
    row = jnp.concatenate([region[...], jnp.full((1, 204), -1, jnp.int32)], axis=1)
    hot = (named == row).astype(F32).astype(BF)
    places = mul(maps[0, 0, 0:256, :], hot, NT).astype(BF)
    for w in range(4):
        one = places[w * 64 : w * 64 + 64]
        off = (mul(one, one, NT) - 1.0) * 1e9
        off = jnp.concatenate([off, off], axis=1)
        mask[w] = jnp.concatenate([off] * 4, axis=1)


def place_vectors(ln_gain, ln_shift, lane):
    eight = jnp.concatenate([ln_gain[0], ln_gain[1], ln_shift[0], ln_shift[1]], axis=0)
    at = lax.broadcasted_iota(jnp.int32, (8, 128), 1) - lane
    out = jnp.zeros((8, 128), F32)
    for e in range(4):
        out = jnp.where(at == e, eight[:, e : e + 1], out)
    return out


def core_kernel(x, cot, w_qkv, w_proj, b, c, ln_gain, ln_shift, tables, region, rel_index,
                out, g, o_qkv, o_proj, ob, oc, o_gain, o_shift, o_tables, gb, gc, *rest):
    far, rest = dict(zip(SPILLED, rest[: len(SPILLED)])), rest[len(SPILLED) :]
    r = dict(zip(scratch_list(), rest))
    at = coords()
    core = at["c"]
    s = Scratch({name: r[name] for name in Scratch.shapes}, far, r["spills"])
    ga, wp, gd, tb, local, vec = [r[f"ga{k}"] for k in range(4)], r["wp"], r["gd"], r["tb"], r["local"], r["vec"]
    feed = Feed(core, gb, gc, r["wb"], r["wc"], r["feeds"])
    copy = Copier(at, r["send"], r["recv"])
    own = []

    def place(src, dst):
        put = pltpu.make_async_copy(src, dst, local.at[len(own)])
        put.start()
        own.append(put)

    wholes = [[w.at[layer] for w in ga + [gb, gc]] for layer in range(2)]
    orders = (ORDERS[0], ORDERS[1], ORDERS[2], ORDERS[0], ORDERS[1], ORDERS[2])
    for layer in range(2):
        for order, src, whole in zip(orders[4:], (b, c), wholes[layer][4:]):
            i1, i2, i3 = (at[axis] for axis in order)
            place(src.at[layer], whole.at[core, i3, i2, i1])
        for k in range(4):
            i1, i2, i3 = (at[axis] for axis in orders[k])
            if k < 3:
                tile = w_qkv[layer, k]
            else:
                four = w_proj[layer].astype(F32)
                tile = rows_of([four[n // 4 : n // 4 + 1, n % 4 * 128 : n % 4 * 128 + 128] for n in range(16)])
            ga[k][layer, core, i3, i2, i1] = tile.astype(BF)
    start = pltpu.make_async_copy(cot, g, local.at[8])
    start.start()
    lane = 4 * ((at["x"] * 2 + at["z"] % 2) * 4 + (at["z"] // 2) * 2 + core)
    gd[core, at["z"], at["y"], at["x"]] = place_vectors(ln_gain, ln_shift, lane)
    mine = (at["z"] // 2) * 2 + core
    rel = r["rel"]
    rel[...] = jnp.full(rel.shape, -1, jnp.int32)
    rel[0:49, 0:49] = rel_index[...]
    turned = rel[...].T
    rel[...] = jnp.full(rel.shape, -1, jnp.int32)
    rel[0:64, 0:64] = turned[0:64, 0:64]
    rel[0:64, 64:128] = turned[0:64, 0:64]
    tb[mine] = jnp.zeros((2, 8, 256), F32)
    for layer in range(2):
        for k in range(4):
            tb[mine, k % 2, layer * 2 + k // 2 : layer * 2 + k // 2 + 1, 0:169] = tables[layer, k : k + 1, :]
    enter(at, PEERS)
    for put in own:
        put.wait()
    def some(layer, ks, ring=0):
        return Gather(copy, at, [(orders[k], wholes[layer][k]) for k in ks], ring).stages

    early, mid, late = some(0, (0, 1, 2)), some(0, (3,)), some(0, (4, 5), 1)
    next_early, next_late = some(1, (0, 1, 2, 3), 1), some(1, (4, 5), 2)
    small = {}

    def small_start(axis, ref):
        steps = (1,) if axis == "c" else (1, 2, 3)
        small[axis] = [copy(ref, ref, axis, step) for step in steps]

    def small_end(axis):
        for one in small[axis]:
            one.wait_recv()

    early[0]()
    small_start("x", gd.at[core, at["z"], at["y"], at["x"]])
    pair = copy(tb.at[mine], tb.at[mine], "z", 2)
    for one in (mid, late, next_early, next_late):
        one[0]()
    maps, pack = r["maps"], r["pack"]
    window_maps(maps)
    proj_maps(pack)
    prepare_mask(region, maps, r["mask"])
    r["gbias"][...] = jnp.zeros(r["gbias"].shape, F32)
    early[1]()
    late[1]()
    mid[1]()
    small_end("x")
    small_start("y", gd.at[core, at["z"], at["y"]])
    pair.wait_recv()
    other = (mine + 2) % 4
    across = [copy(tb.at[k], tb.at[k], "c", 1) for k in (mine, other)]
    early[2]()
    small_end("y")
    small_start("z", gd.at[core, at["z"]])
    late[2]()
    mid[2]()
    next_early[1]()
    next_late[1]()
    for one in across:
        one.wait_recv()
    build_bias(tb, rel, r["bias"])
    small_end("z")
    small_start("c", gd.at[core])
    early[3]()
    next_late[2]()
    small_end("c")
    vecs = r["vecs"]
    for y in range(4):
        total = gd[0, 0, y, 0]
        for n in range(1, 32):
            total = total + gd[n // 16, n // 4 % 4, y, n % 4]
        vecs[:, y * 128 : y * 128 + 128] = total
    early[4]()
    next_early[2]()
    gain = [[vecs[l * 2 + k : l * 2 + k + 1] for k in range(2)] for l in range(2)]
    shift = [[vecs[4 + l * 2 + k : 5 + l * 2 + k] for k in range(2)] for l in range(2)]
    start.wait()

    def unpack_proj(layer):
        for block in range(8):
            tiles = []
            for n in range(16):
                tiles.append(ga[3][(layer,) + slot_of(0, block * 16 + n)])
            tiles = rows_of(tiles)
            for q in range(4):
                wp[layer, block * 64 : block * 64 + 64, q * 128 : q * 128 + 128] = mul(pack[q], tiles).astype(BF)

    forward_plans = (
        {
            "qkv": [mid[3], late[3], next_late[3]],
            "half_scores": [next_early[3]],
            "scores": [mid[4], lambda: unpack_proj(0)],
            "feed_forward": [late[4], late[5]],
            "chunks": [next_early[4], next_late[4]],
            "end": [next_early[5], lambda: unpack_proj(1)],
        },
        {"feed_forward": [next_late[5], next_late[6]]},
    )
    x1 = r["x1"]
    for layer, before, after in ((0, x, x1), (1, x1, out)):

        def reached(name, plan=forward_plans[layer]):
            for one in plan.get(name, ()):
                one()

        forward(layer, before, after, gain, shift, ga, feed, wp, maps, r["bias"], r["mask"], s, reached)

    def chunk_part(ref, k, n):
        z = pl.ds(2 * (n % 2), 2)
        return ref.at[:, z] if k == 3 else ref.at[:, :, z]

    def chunk_over(k, n):
        sem = (k - 3) * 4 + n
        return pltpu.make_async_remote_copy(
            src_ref=(s.stage_b if k == 3 else s.stage_c).at[n % 2],
            dst_ref=chunk_part(r[f"landed{k}"], k, n),
            send_sem=r["cross_send"].at[sem],
            recv_sem=r["cross_recv"].at[sem],
            device_id=moved(at, "c", 1),
            device_id_type=MESH,
        )

    def chunk_here(layer, k, n):
        src = (s.stage_b if k == 3 else s.stage_c).at[n % 2]
        return pltpu.make_async_copy(
            src, chunk_part(r[f"sums{k}_{layer}"], k, n), r["cross_send"].at[(k - 3) * 4 + n]
        )

    def grads_of(layer):
        first = 0 if layer else 2

        def away(n):
            return jnp.logical_and(n >= first, n < first + 2)

        def send_grads(n):
            for k in (3, 4):
                pl.when(away(n))(lambda k=k: chunk_over(k, n).start())
                pl.when(jnp.logical_not(away(n)))(lambda k=k: chunk_here(layer, k, n).start())

        def wait_grads(n):
            for k in (3, 4):
                pl.when(away(n))(lambda k=k: chunk_over(k, n).wait_send())
                pl.when(jnp.logical_not(away(n)))(lambda k=k: chunk_here(layer, k, n).wait())

        def arrived(k):
            for n in (first, first + 1):
                chunk_over(k, n).wait_recv()

        return send_grads, wait_grads, arrived

    def out_of(ref, layer, lanes):
        def put(total):
            ref[layer, :, lanes] = total

        return put

    def feed_forward_scatter(layer):
        families = []
        for k, ref in ((3, ob), (4, oc)):
            family = {name: r[f"{name}{k}"] for name in landing_shapes(512)}
            family.update(order=FAMILIES[k][0], sums=r[f"sums{k}_{layer}"], out=out_of(ref, layer, slice(0, 512)))
            families.append(family)
        arrived = grads_of(layer)[2]
        return Scatter(copy, at, families, lambda n: arrived(n + 3))

    def heads_out(layer, k):
        def put(total):
            o_qkv[layer, k] = total[:, 0:128]
            if k == 2:
                for n in range(16):
                    lanes = slice(n % 4 * 128, n % 4 * 128 + 128)
                    o_proj[layer, n // 4 : n // 4 + 1, lanes] = total[n : n + 1, 128:256]

        return put

    def heads_scatter(layer):
        families, crossing = [], []
        for k in range(3):
            family = {name: r[f"{name}{k}_{layer}"] for name in landing_shapes(128)}
            both = r[f"both{k}_{layer}"]
            family.update(order=FAMILIES[k][0], sums=both.at[core], out=heads_out(layer, k))
            families.append(family)

        def cross(k):
            crossing.append(copy(r[f"both{k}_{layer}"].at[1 - core], r[f"landed{k}_{layer}"], "c", 1))

        return Scatter(copy, at, families, lambda n: crossing[n].wait_recv()), cross

    wide = {layer: feed_forward_scatter(layer) for layer in (0, 1)}
    heads = {layer: heads_scatter(layer) for layer in (0, 1)}
    tab, tab_pair, tab_sum, vec_sum = r["tab"], r["tab_pair"], r["tab_sum"], r["vec_sum"]
    vec_land, tab_cross, tab_land = r["vec_land"], r["tab_cross"], r["tab_land"]

    def keep_in(ref):
        def keep(total):
            ref[...] = total

        return keep

    def keep_vectors(total):
        lanes = lax.broadcasted_iota(jnp.int32, (8, 128), 1) - lane
        four = jnp.concatenate(
            [jnp.sum(jnp.where(lanes == e, total, 0.0), axis=1, keepdims=True) for e in range(4)], axis=1
        )
        for layer in range(2):
            o_gain[layer] = four[layer * 2 : layer * 2 + 2]
            o_shift[layer] = four[layer * 2 + 4 : layer * 2 + 6]

    def keep_tables(total):
        for layer in range(2):
            for k in range(4):
                row = layer * 2 + k // 2
                o_tables[layer, k : k + 1, :] = total[row : row + 1, k % 2 * 256 : k % 2 * 256 + 169]

    vec_sums = Sums(
        copy,
        at,
        [
            ("y", 4, lambda j: vec.at[:, pl.ds(pl.multiple_of(j * 128, 128), 128)], vec_land.at[0], keep_in(vec_sum)),
            ("x", 4, vec_sum, vec_land.at[1], keep_in(vec_sum)),
            ("z", 4, vec_sum, vec_land.at[2], keep_in(vec_sum)),
            ("c", 2, vec_sum, vec_land.at[3], keep_vectors),
        ],
    )
    tab_sums = Sums(
        copy,
        at,
        [
            ("c", 2, lambda j: tab.at[j], tab_cross, keep_in(tab_pair)),
            ("z", 4, lambda j: tab_pair.at[j // 2], tab_land.at[0], keep_in(tab_sum)),
            ("x", 4, tab_sum, tab_land.at[1], keep_in(tab_sum)),
            ("y", 4, tab_sum, tab_land.at[2], keep_tables),
        ],
    )

    def tables_done():
        table_sums(r["gbias"], rel, tab)

    def stage(sums, n):
        return lambda: sums.stages[n]()

    high_wide, low_wide, high_heads, low_heads = wide[1], wide[0], heads[1][0], heads[0][0]
    plans = {
        1: {
            "feed_forward": [stage(high_wide, 0)],
            "half_scores": [stage(high_wide, 1)],
            "end": [stage(high_wide, 2)],
        },
        0: {
            "chunks": [stage(high_wide, 3), stage(high_heads, 0)],
            "feed_forward": [stage(high_heads, 1), stage(low_wide, 0), stage(high_wide, 4)],
            "half_scores": [stage(high_heads, 2), stage(low_wide, 1)],
            "scores": [stage(high_heads, 3)],
            "qkv": [stage(low_wide, 2), stage(high_heads, 4)],
            "gn1": [stage(low_heads, 0)],
            "end": [
                stage(vec_sums, 0),
                tables_done,
                stage(tab_sums, 0),
                stage(low_heads, 1),
                stage(tab_sums, 1),
                stage(vec_sums, 1),
                stage(low_wide, 3),
                stage(low_heads, 2),
                stage(tab_sums, 2),
                stage(vec_sums, 2),
                stage(low_wide, 4),
                stage(low_heads, 3),
                stage(tab_sums, 3),
                stage(vec_sums, 3),
                stage(low_heads, 4),
                stage(tab_sums, 4),
                stage(vec_sums, 4),
            ],
        },
    }
    for layer, before in ((1, x1), (0, x)):

        def poll(name, plan=plans[layer]):
            for one in plan.get(name, ()):
                one()

        send, wait, _ = grads_of(layer)
        backward_mlp(layer, g, gain, feed, s, vec, send, wait, poll)
        backward_heads(
            layer, before, g, gain, ga, wp, maps, pack, r["gbias"], s, vec,
            [r[f"both{k}_{layer}"] for k in range(3)], poll, heads[layer][1],
        )
    copy.finish()


def hand_over_kernel(*refs):
    sems = refs[-1]
    count = len(refs) // 2
    copies = [pltpu.make_async_copy(refs[n], refs[count + n], sems.at[n]) for n in range(count)]
    for one in copies:
        one.start()
    for one in copies:
        one.wait()


def hand_over(arrays):
    far, vmem = pl.BlockSpec(memory_space=pl.ANY), pl.BlockSpec(memory_space=pltpu.VMEM)
    return pl.pallas_call(
        hand_over_kernel,
        out_shape=[jax.ShapeDtypeStruct(one.shape, one.dtype) for one in arrays],
        in_specs=[vmem] * len(arrays),
        out_specs=[far] * len(arrays),
        scratch_shapes=[pltpu.SemaphoreType.DMA((len(arrays),))],
        compiler_params=pltpu.CompilerParams(vmem_limit_bytes=63 * 2**20),
        name="hand_over",
    )(*arrays)


def shards(
    inputs, w_qkv, w_proj, w_up, w_down, ln_gain, ln_shift, tables, region, rel_index, cotangent
):
    w_qkv, tables = w_qkv.transpose(0, 2, 1, 3), tables.transpose(0, 2, 1)
    tiles = jax.ShapeDtypeStruct((2, 2, 4, 4, 4, 16, 512), BF)
    rows = jax.ShapeDtypeStruct((ROWS, WIDTH), F32)
    vmem, far = pl.BlockSpec(memory_space=pltpu.VMEM), pl.BlockSpec(memory_space=pl.ANY)
    spills = [jax.ShapeDtypeStruct(Scratch.shapes[name].shape, Scratch.shapes[name].dtype) for name in SPILLED]
    grads = [
        jax.ShapeDtypeStruct(one.shape, F32) for one in (w_qkv, w_proj, w_up, w_down, ln_gain, ln_shift, tables)
    ]
    outs = pl.pallas_call(
        core_kernel,
        out_shape=[rows, rows] + grads + [tiles, tiles] + spills,
        in_specs=[vmem, far, vmem, vmem, far, far] + [vmem] * 5,
        out_specs=[vmem] * 9 + [far] * (2 + len(spills)),
        scratch_shapes=list(scratch_list().values()),
        compiler_params=pltpu.CompilerParams(
            vmem_limit_bytes=63 * 2**20, collective_id=0, has_side_effects=True
        ),
        name="both_blocks",
    )(
        inputs, cotangent, w_qkv, w_proj, w_up, w_down, ln_gain, ln_shift, tables, region.reshape(1, -1), rel_index
    )
    out, g, o_qkv, o_proj, ob, oc, o_gain, o_shift, o_tables = hand_over(outs[:9])
    return out, g, o_qkv.transpose(0, 2, 1, 3), o_proj, ob, oc, o_gain, o_shift, o_tables.transpose(0, 2, 1)


def solution(mesh):
    return jax.shard_map(
        shards,
        mesh=mesh,
        in_specs=(
            P(("dp", "tensor"), None),
            P(None, "dp", None, "tensor"),
            P(None, ("tensor", "dp"), None),
            P(None, "dp", "tensor"),
            P(None, ("tensor", "dp"), None),
            P(None, None, ("dp", "tensor")),
            P(None, None, ("dp", "tensor")),
            P(None, None, "tensor"),
            P(),
            P(),
            P(("dp", "tensor"), None),
        ),
        out_specs=(
            P(("dp", "tensor"), None),
            P(("dp", "tensor"), None),
            P(None, "dp", None, "tensor"),
            P(None, ("tensor", "dp"), None),
            P(None, "dp", "tensor"),
            P(None, ("tensor", "dp"), None),
            P(None, None, ("dp", "tensor")),
            P(None, None, ("dp", "tensor")),
            P(None, None, "tensor"),
        ),
        check_vma=False,
    )
```

```python
import functools
import jax
import jax.numpy as jnp
from jax import lax
from jax.experimental import pallas as pl
from jax.experimental.pallas import tpu as pltpu
from jax.sharding import PartitionSpec as P

MESH = pl.DeviceIdType.MESH
ORDERS = (("x", "y", "z"), ("y", "z", "x"), ("z", "x", "y"))


def coords():
    dp, tp = lax.axis_index("dp"), lax.axis_index("tensor")
    return {
        "y": dp // 8,
        "x": (dp // 2) % 4,
        "z": (tp // 2) * 2 + dp % 2,
        "c": tp % 2,
    }


def device(at):
    return (at["y"] * 8 + at["x"] * 2 + at["z"] % 2, (at["z"] // 2) * 2 + at["c"])


def moved(at, axis, step):
    size = 2 if axis == "c" else 4
    return device({**at, axis: (at[axis] + step) % size})


NEIGHBOURS = (("x", 1), ("x", 3), ("y", 1), ("y", 3), ("z", 1), ("z", 3), ("c", 1))


def enter(at, peers=NEIGHBOURS):
    barrier = pltpu.get_barrier_semaphore()
    for axis, step in peers:
        pl.semaphore_signal(barrier, inc=1, device_id=moved(at, axis, step), device_id_type=MESH)
    pl.semaphore_wait(barrier, len(peers))


PEERS = NEIGHBOURS + (("x", 2), ("y", 2), ("z", 2))
COPIES = 305


class Copier:
    def __init__(self, at, send, recv):
        self.at, self.send, self.recv, self.made = at, send, recv, []

    def __call__(self, src, dst, axis, step):
        slot = len(self.made)
        assert slot < COPIES
        copy = pltpu.make_async_remote_copy(
            src_ref=src,
            dst_ref=dst,
            send_sem=self.send.at[slot],
            recv_sem=self.recv.at[slot],
            device_id=moved(self.at, axis, step),
            device_id_type=MESH,
        )
        copy.start()
        self.made.append(copy)
        return copy

    def finish(self):
        for copy in self.made:
            copy.wait_send()


def add_into(dst, *terms):
    lead = dst.shape[:-3]
    count = 1
    for size in lead:
        count *= size

    def body(n, carry):
        index = []
        for size in reversed(lead):
            index.append(n % size)
            n = n // size
        index = tuple(reversed(index)) or slice(None)
        total = dst[index].astype(jnp.float32)
        for term in terms:
            total = total + term[index].astype(jnp.float32)
        dst[index] = total.astype(dst.dtype)
        return carry

    if count == 1:
        body(0, 0)
    else:
        lax.fori_loop(0, count, body, 0)


class Scatter:
    def __init__(self, copy, at, families, crossing):
        self.copy, self.at, self.families, self.crossing = copy, at, families, crossing
        self.held = [{} for _ in families]
        self.stages = [self.join, self.along, self.second, self.third, self.finish]

    def places(self, family):
        i1, i2, i3 = (self.at[axis] for axis in family["order"])
        return i1, i2, i3

    def join(self):
        for n, (family, held) in enumerate(zip(self.families, self.held)):
            self.crossing(n)
            _, _, i3 = self.places(family)
            axis, sums, landed = family["order"][2], family["sums"], family["landed"]
            far = (i3 + 2) % 4
            add_into(sums.at[far], landed.at[far])
            held["r"] = self.copy(sums.at[far, 0:2], family["half"].at[0], axis, 1)
            held["l"] = self.copy(sums.at[far, 2:4], family["half"].at[1], axis, 3)
        for family in self.families:
            _, _, i3 = self.places(family)
            for step in (1, 3, 0):
                j = (i3 + step) % 4
                add_into(family["sums"].at[j], family["landed"].at[j])

    def along(self):
        for family, held in zip(self.families, self.held):
            _, _, i3 = self.places(family)
            axis, sums = family["order"][2], family["sums"]
            right, left = (i3 + 1) % 4, (i3 + 3) % 4
            held["r"].wait_recv()
            add_into(sums.at[right, 0:2], family["half"].at[0])
            held["r2"] = self.copy(sums.at[right], family["full"].at[0], axis, 1)
            held["l"].wait_recv()
            add_into(sums.at[left, 2:4], family["half"].at[1])
            held["l2"] = self.copy(sums.at[left], family["full"].at[1], axis, 3)

    def second(self):
        for family, held in zip(self.families, self.held):
            _, i2, i3 = self.places(family)
            axis, sums = family["order"][1], family["sums"]
            held["r2"].wait_recv()
            held["l2"].wait_recv()
            add_into(sums.at[i3], family["full"].at[0], family["full"].at[1])
            held["2"] = [
                self.copy(sums.at[i3, (i2 + step) % 4], family["two"].at[step - 1], axis, step) for step in (2, 1, 3)
            ]

    def third(self):
        for family, held in zip(self.families, self.held):
            i1, i2, i3 = self.places(family)
            axis, sums = family["order"][0], family["sums"]
            for one in held["2"]:
                one.wait_recv()
            add_into(sums.at[i3, i2], *(family["two"].at[k] for k in range(3)))
            held["1"] = [
                self.copy(sums.at[i3, i2, (i1 + step) % 4], family["one"].at[step - 1], axis, step)
                for step in (2, 1, 3)
            ]

    def finish(self):
        for family, held in zip(self.families, self.held):
            i1, i2, i3 = self.places(family)
            for one in held["1"]:
                one.wait_recv()
            total = family["sums"][i3, i2, i1].astype(jnp.float32)
            for k in range(3):
                total = total + family["one"][k].astype(jnp.float32)
            family["out"](total)


def landing_shapes(width):
    bf = jnp.bfloat16
    return {
        "landed": pltpu.VMEM((4, 4, 4, 16, width), bf),
        "half": pltpu.VMEM((2, 2, 4, 16, width), bf),
        "full": pltpu.VMEM((2, 4, 4, 16, width), bf),
        "two": pltpu.VMEM((3, 4, 16, width), bf),
        "one": pltpu.VMEM((3, 16, width), bf),
    }


WINDOW = 7
SIDE = 14
EPS = 1e-05


BF, F32 = jnp.bfloat16, jnp.float32
SCALE = 32.0 ** -0.5
ROWS, PADDED, WIDTH = 784, 1024, 512
NN = (((1,), (0,)), ((), ()))
NT = (((1,), (1,)), ((), ()))
TN = (((0,), (0,)), ((), ()))


def mul(a, b, dims=NN):
    return lax.dot_general(a, b, dims, preferred_element_type=F32)


def window_maps(maps):
    n = lax.broadcasted_iota(jnp.int32, (512, 1), 0)
    place = n % 64
    token = lax.broadcasted_iota(jnp.int32, (512, 400), 1)
    for layer in range(2):
        row = n // 128 % 2 * 7 + place // 7
        col = n // 64 % 2 * 7 + place % 7
        if layer:
            row, col = (row + 3) % 14, (col + 3) % 14
        taken = jnp.where(place < 49, n // 256 * 196 + row * 14 + col, -100)
        for pair in range(2):
            maps[layer, pair] = (token == taken + 8 * pair).astype(F32).astype(BF)


def proj_maps(pack):
    n = lax.broadcasted_iota(jnp.int32, (64, 1), 0)
    packed = lax.broadcasted_iota(jnp.int32, (64, 256), 1)
    for q in range(4):
        pack[q] = (packed == n // 4 * 16 + n % 4 * 4 + q).astype(F32).astype(BF)


PLACES = [(y, x, zl) for y in range(4) for x in range(4) for zl in range(2)]


def rows_of(tiles):
    return jnp.concatenate(tiles, axis=0)


def up_block(wb, slot):
    return rows_of([wb[slot, x, zl, y] for y, x, zl in PLACES])


def down_block(wc, slot):
    return rows_of([wc[slot, y, x, zl] for y, x, zl in PLACES])


def slot_of(k, dev):
    t, (y, x, zl) = dev // 32, PLACES[dev % 32]
    at = {"x": x, "y": y, "z": 2 * (t // 2) + zl}
    return (t % 2,) + tuple(at[axis] for axis in reversed(ORDERS[k]))


def qkv_block(ga, layer, s):
    return jnp.concatenate(
        [rows_of([ga[s][(layer,) + slot_of(s, t * 32 + n)] for n in range(32)]) for t in range(4)], axis=1
    )


def norm_parts(values):
    mean = jnp.mean(values, axis=1, keepdims=True)
    centered = values - mean
    r = lax.rsqrt(jnp.mean(centered * centered, axis=1, keepdims=True) + EPS)
    return centered * r, r


def norm_back(grad, values, gain):
    xhat, r = norm_parts(values)
    e = grad * gain
    through = r * (
        e - jnp.mean(e, axis=1, keepdims=True) - xhat * jnp.mean(e * xhat, axis=1, keepdims=True)
    )
    return (
        through,
        jnp.sum(grad * xhat, axis=0, keepdims=True),
        jnp.sum(grad, axis=0, keepdims=True),
    )


C0, C1 = 0.7978845608028654, 0.044715


def gelu(u):
    return 0.5 * u * (1.0 + jnp.tanh(C0 * u * (1.0 + C1 * (u * u))))


def gelu_both(u):
    square = u * u
    t = jnp.tanh(C0 * u * (1.0 + C1 * square))
    half = 0.5 * (1.0 + t)
    slope = half + (0.5 * C0) * u * (1.0 - t * t) * (1.0 + (3.0 * C1) * square)
    return u * half, slope


def to_windows_of(maps, layer, tokens):
    return [mul(maps[layer, pair], tokens[pair * 384 : pair * 384 + 400, :]) for pair in range(2)]


def from_windows_of(maps, layer, rows):
    first = mul(maps[layer, 0], rows[0:512, :], TN)
    second = mul(maps[layer, 1], rows[512:1024, :], TN)
    return jnp.concatenate(
        [first[:384], first[384:400] + second[:16], second[16:]], axis=0
    )


def head_masks():
    lane = lax.broadcasted_iota(jnp.int32, (1, 128), 1) // 32
    return [lane == h for h in range(4)]


def spread(v, masks):
    return jnp.concatenate([jnp.where(m, v, jnp.zeros((), v.dtype)) for m in masks], axis=0)


def fold(r, masks):
    out = r[0:64]
    for h in range(1, 4):
        out = jnp.where(masks[h], r[h * 64 : h * 64 + 64], out)
    return out


UNROLL = 4


def columns(s, q):
    return slice(s * 512 + q * 128, s * 512 + q * 128 + 128)


def scores_of(ref, layer, q):
    return ref.at[layer, q // 2, :, q % 2 * 256 : q % 2 * 256 + 256]


def window(w):
    return pl.ds(pl.multiple_of(w * 64, 64), 64)


def attend(layer, qkv, bias, mask, kept, out, part):
    masks = head_masks()

    def some(n, carry):
        items = [(n * UNROLL + u, u, q) for u in range(UNROLL) for q in range(4)]
        scores = [
            mul(qkv[window(w), columns(1, q)], spread(qkv[window(w), columns(0, q)], masks), NT) for w, u, q in items
        ]
        probs = []
        for (w, u, q), s in zip(items, scores):
            s = s * SCALE + scores_of(bias, layer, q)[...]
            if layer:
                s = s + mask[u % 4, :, 0:256]
            e = jnp.exp(s - jnp.max(s, axis=0, keepdims=True))
            p = (e * (1.0 / jnp.sum(e, axis=0, keepdims=True))).astype(BF)
            kept[w * 4 + q] = p
            probs.append(p)
        for (w, u, q), p in zip(items, probs):
            out[window(w), columns(0, q)] = fold(mul(p, qkv[window(w), columns(2, q)], TN), masks).astype(BF)
        return carry

    lax.fori_loop(part * 8 // UNROLL, (part + 1) * 8 // UNROLL, some, 0)


def attend_back(layer, qkv, kept, gout, gbias, part):
    masks = head_masks()

    def some(n, carry):
        items = [(n * UNROLL + u, q) for u in range(UNROLL) for q in range(4)]
        gprobs, gvs = [], []
        for w, q in items:
            d = spread(gout[window(w), columns(0, q)], masks)
            gprobs.append(mul(qkv[window(w), columns(2, q)], d, NT))
            gvs.append(mul(kept[w * 4 + q], d))
        for (w, q), gv in zip(items, gvs):
            qkv[window(w), columns(2, q)] = gv.astype(BF)
        gscores = []
        for (w, q), gp in zip(items, gprobs):
            p = kept[w * 4 + q].astype(F32)
            pg = p * gp
            gscores.append(pg - p * jnp.sum(pg, axis=0, keepdims=True))
        for q in range(4):
            place = scores_of(gbias, layer, q)
            total = place[...]
            for (w, h), gs in zip(items, gscores):
                if h == q:
                    total = total + gs
            place[...] = total
        for (w, q), gs in zip(items, gscores):
            ds = gs.astype(BF)
            query, key = qkv[window(w), columns(0, q)], qkv[window(w), columns(1, q)]
            gk = mul(ds, spread(query, masks)) * SCALE
            gq = fold(mul(ds, key, TN), masks) * SCALE
            qkv[window(w), columns(0, q)] = gq.astype(BF)
            qkv[window(w), columns(1, q)] = gk.astype(BF)
        return carry

    lax.fori_loop(part * 8 // UNROLL, (part + 1) * 8 // UNROLL, some, 0)


SPILLED = ("n1w", "qkv", "kept", "att", "mid", "n2", "hid")


def forward(layer, x, result, gain, shift, ga, feed, wp, maps, bias, mask, s, poll):
    def ready(name):
        if layer:
            s.spilled(name)

    def done(name):
        if not layer:
            s.spill(name)

    xhat, _ = norm_parts(x[...])
    s.low[...] = (xhat * gain[layer][0] + shift[layer][0]).astype(BF)
    ready("n1w")
    for pair, part in enumerate(to_windows_of(maps, layer, s.low)):
        s.n1w[pair * 512 : pair * 512 + 512, :] = part.astype(BF)
    done("n1w")
    ready("qkv")
    for k in range(3):
        s.qkv[:, k * 512 : k * 512 + 512] = mul(s.n1w[...], qkv_block(ga, layer, k)).astype(BF)
    done("qkv")
    poll("qkv")
    ready("kept")
    attend(layer, s.qkv, bias, mask, s.kept, s.ow, 0)
    poll("half_scores")
    attend(layer, s.qkv, bias, mask, s.kept, s.ow, 1)
    done("kept")
    poll("scores")
    ready("att")
    s.att[...] = from_windows_of(maps, layer, s.ow).astype(BF)
    done("att")
    ready("mid")
    s.mid[...] = x[...] + mul(s.att[...], wp[layer])
    done("mid")
    poll("feed_forward")
    feed.fetch(layer, 0, 0)
    ready("n2")
    xhat, _ = norm_parts(s.mid[...])
    s.n2[...] = (xhat * gain[layer][1] + shift[layer][1]).astype(BF)
    done("n2")
    result[...] = s.mid[...]
    ready("hid")

    def chunk(t, carry):
        slot = feed.take(t)

        @pl.when(t < 3)
        def _():
            feed.fetch(layer, t + 1, t + 1)

        if layer:
            pl.when(t == 3)(lambda: feed.fetch(1, feed.turn(1, 0), 0))
        hidden = mul(s.n2[...], up_block(feed.wb, slot))
        s.hid[t] = hidden.astype(BF)
        result[...] += mul(gelu(hidden.astype(BF)), down_block(feed.wc, slot))
        return carry

    lax.fori_loop(0, 2, chunk, 0)
    poll("chunks")
    lax.fori_loop(2, 4, chunk, 0)
    done("hid")
    poll("end")


def backward_mlp(layer, g, gain, feed, s, vec, send_grads, wait_grads, poll):
    if not layer:
        s.returned("hid")
        s.returned("n2")
    s.low[...] = g[...].astype(BF)
    s.gn[0:ROWS, :] = jnp.zeros((ROWS, WIDTH), F32)

    def chunk(n, carry):
        t = feed.turn(layer, n)
        slot = feed.take(n)

        @pl.when(n < 3)
        def _():
            feed.fetch(layer, feed.turn(layer, n + 1), n + 1)

        if layer:
            pl.when(n == 3)(lambda: feed.fetch(0, feed.turn(0, 0), 0))

        active, slope = gelu_both(s.hid[t])
        gh = (mul(s.low[...], down_block(feed.wc, slot), NT) * slope.astype(F32)).astype(BF)
        pl.when(n >= 2)(lambda: wait_grads(n - 2))
        gdown = mul(active.astype(BF), s.low[...], TN).astype(BF)
        for k, (y, xx, zl) in enumerate(PLACES):
            s.stage_c[slot, y, xx, zl] = gdown[k * 16 : k * 16 + 16]
        gup = mul(s.n2[...], gh, TN).astype(BF)
        for k, (y, xx, zl) in enumerate(PLACES):
            s.stage_b[slot, xx, zl, y] = gup[k * 16 : k * 16 + 16]
        send_grads(n)
        s.gn[0:ROWS, :] += mul(gh, up_block(feed.wb, slot), NT)
        return carry

    lax.fori_loop(0, 2, chunk, 0)
    poll("chunks")
    lax.fori_loop(2, 4, chunk, 0)
    wait_grads(jnp.int32(2))
    wait_grads(jnp.int32(3))
    poll("feed_forward")
    if layer:
        s.bring("hid")
        s.bring("n2")
    else:
        s.returned("mid")
    through, dg, ds = norm_back(s.gn[0:ROWS, :], s.mid[...], gain[layer][1])
    vec[layer * 2 + 1 : layer * 2 + 2] = dg
    vec[layer * 2 + 5 : layer * 2 + 6] = ds
    if layer:
        s.bring("mid")
    g[...] += through


def backward_heads(layer, x, g, gain, ga, wp, maps, pack, gbias, s, vec, both, poll, cross):
    s.low[...] = g[...].astype(BF)
    if not layer:
        s.returned("att")
    gproj = mul(s.att[...], s.low[...], TN).astype(BF)
    if layer:
        s.bring("att")
    for block in range(8):
        part = gproj[block * 64 : block * 64 + 64]
        packed = mul(pack[0], part[:, 0:128], TN)
        for q in range(1, 4):
            packed = packed + mul(pack[q], part[:, q * 128 : q * 128 + 128], TN)
        packed = packed.astype(BF)
        for n in range(16):
            both[2][slot_of(2, block * 16 + n) + (slice(None), slice(128, 256))] = packed[n * 16 : n * 16 + 16]
    poll("proj")
    for pair, part in enumerate(to_windows_of(maps, layer, s.low)):
        s.ow[pair * 512 : pair * 512 + 512, :] = part.astype(BF)
    s.ow[...] = mul(s.ow[...], wp[layer], NT).astype(BF)
    poll("gatt")
    if not layer:
        s.returned("qkv")
        s.returned("kept")
    attend_back(layer, s.qkv, s.kept, s.ow, gbias, 0)
    poll("half_scores")
    attend_back(layer, s.qkv, s.kept, s.ow, gbias, 1)
    if layer:
        s.bring("kept")
    poll("scores")
    if not layer:
        s.returned("n1w")
    for k in range(3):
        gw = mul(s.n1w[...], s.qkv[:, k * 512 : k * 512 + 512], TN).astype(BF)
        for dev in range(128):
            t, n = dev // 32, dev % 32
            both[k][slot_of(k, dev) + (slice(None), slice(0, 128))] = gw[n * 16 : n * 16 + 16, t * 128 : t * 128 + 128]
        cross(k)
    poll("qkv")
    if layer:
        s.bring("n1w")
    total = mul(s.qkv[:, 0:512], qkv_block(ga, layer, 0), NT)
    for k in range(1, 3):
        total = total + mul(s.qkv[:, k * 512 : k * 512 + 512], qkv_block(ga, layer, k), NT)
    s.ow[...] = total.astype(BF)
    if layer:
        s.bring("qkv")
    poll("gn1")
    through, dg, ds = norm_back(from_windows_of(maps, layer, s.ow), x[...], gain[layer][0])
    vec[layer * 2 : layer * 2 + 1] = dg
    vec[layer * 2 + 4 : layer * 2 + 5] = ds
    g[...] += through
    poll("end")


class Feed:
    def __init__(self, core, gb, gc, wb, wc, sems):
        self.core, self.gb, self.gc, self.wb, self.wc, self.sems = core, gb, gc, wb, wc, sems

    def turn(self, layer, n):
        mine = self.core if layer == 0 else 1 - self.core
        first = jnp.where(n < 2, mine, 1 - mine)
        return 2 * (n % 2) + first

    def copies(self, layer, t, n):
        slot, z = n % 2, pl.ds(2 * (t // 2), 2)
        return (
            pltpu.make_async_copy(self.gb.at[layer, t % 2, :, z], self.wb.at[slot], self.sems.at[slot]),
            pltpu.make_async_copy(self.gc.at[layer, t % 2, :, :, z], self.wc.at[slot], self.sems.at[2 + slot]),
        )

    def fetch(self, layer, t, n):
        for one in self.copies(layer, t, n):
            one.start()

    def take(self, n):
        for one in self.copies(0, 0, n):
            one.wait()
        return n % 2


class Scratch:
    shapes = {
        "low": pltpu.VMEM((ROWS, WIDTH), BF),
        "n1w": pltpu.VMEM((PADDED, WIDTH), BF),
        "qkv": pltpu.VMEM((PADDED, 3 * WIDTH), BF),
        "kept": pltpu.VMEM((64, 64, 256), BF),
        "ow": pltpu.VMEM((PADDED, WIDTH), BF),
        "att": pltpu.VMEM((ROWS, WIDTH), BF),
        "mid": pltpu.VMEM((ROWS, WIDTH), F32),
        "n2": pltpu.VMEM((ROWS, WIDTH), BF),
        "hid": pltpu.VMEM((4, ROWS, WIDTH), BF),
        "gn": pltpu.VMEM((ROWS, WIDTH), F32),
        "stage_b": pltpu.VMEM((2, 4, 2, 4, 16, 512), BF),
        "stage_c": pltpu.VMEM((2, 4, 4, 2, 16, 512), BF),
    }

    def __init__(self, refs, far, sems):
        self.__dict__.update(refs)
        self.far, self.sems = far, sems

    def out_copy(self, name):
        return pltpu.make_async_copy(getattr(self, name), self.far[name], self.sems.at[SPILLED.index(name)])

    def in_copy(self, name):
        return pltpu.make_async_copy(self.far[name], getattr(self, name), self.sems.at[SPILLED.index(name)])

    def spill(self, name):
        self.out_copy(name).start()

    def spilled(self, name):
        self.out_copy(name).wait()

    def bring(self, name):
        self.in_copy(name).start()

    def returned(self, name):
        self.in_copy(name).wait()


def axis_slots(whole, i2, i3):
    return (
        lambda j: whole.at[i3, i2, j],
        lambda j: whole.at[i3, j],
        lambda j: whole.at[j],
    )


class Gather:
    def __init__(self, copy, at, families, ring):
        self.copy, self.at, self.across = copy, at, []
        self.plans = []
        for order, whole in families:
            i1, i2, i3 = (at[axis] for axis in order)
            self.plans.append((order, (i1, i2, i3), axis_slots(whole.at[at["c"]], i2, i3), {}))
        if ring == 2:
            self.stages = [self.first, self.around, self.onward, self.third, self.forward, self.end, self.finish]
        elif ring == 1:
            self.stages = [self.first, self.second, self.third, self.forward, self.end, self.finish]
        else:
            self.stages = [self.first, self.second, self.straight, self.landed, self.finish]

    def pass_on(self, ref):
        self.across.append(self.copy(ref, ref, "c", 1))

    def first(self):
        for order, places, slots, held in self.plans:
            ref = slots[0](places[0])
            held["1"] = [self.copy(ref, ref, order[0], step) for step in (2, 1, 3)]

    def second(self):
        for order, places, slots, held in self.plans:
            for one in held["1"]:
                one.wait_recv()
            ref = slots[1](places[1])
            held["2"] = [self.copy(ref, ref, order[1], step) for step in (2, 1, 3)]

    def around(self):
        for order, places, slots, held in self.plans:
            for one in held["1"]:
                one.wait_recv()
            ref = slots[1](places[1])
            held["a"] = [self.copy(ref, ref, order[1], step) for step in (1, 3)]

    def onward(self):
        for order, places, slots, held in self.plans:
            held["2"] = []
            for n, (step, back) in enumerate(((1, 3), (3, 1))):
                held["a"][n].wait_recv()
                half = slots[1]((places[1] + back) % 4).at[2 * n : 2 * n + 2]
                held["2"].append(self.copy(half, half, order[1], step))

    def straight(self):
        for order, places, slots, held in self.plans:
            for one in held["2"]:
                one.wait_recv()
            ref = slots[2](places[2])
            held["3"] = [(step, self.copy(ref, ref, order[2], step)) for step in (1, 3, 2)]
            self.pass_on(ref)

    def landed(self):
        for n in range(3):
            for order, places, slots, held in self.plans:
                step, one = held["3"][n]
                one.wait_recv()
                self.pass_on(slots[2]((places[2] + 4 - step) % 4))

    def third(self):
        for order, places, slots, held in self.plans:
            for one in held["2"]:
                one.wait_recv()
            ref = slots[2](places[2])
            held["s"] = [self.copy(ref, ref, order[2], step) for step in (1, 3)]
            self.pass_on(ref)

    def forward(self):
        for order, places, slots, held in self.plans:
            held["f"] = []
            for n, (step, back) in enumerate(((1, 3), (3, 1))):
                held["s"][n].wait_recv()
                ref = slots[2]((places[2] + back) % 4)
                half = ref.at[2 * n : 2 * n + 2]
                held["f"].append(self.copy(half, half, order[2], step))
                self.pass_on(ref)

    def end(self):
        for order, places, slots, held in self.plans:
            for one in held["f"]:
                one.wait_recv()
            self.pass_on(slots[2]((places[2] + 2) % 4))

    def finish(self):
        for one in self.across:
            one.wait_recv()


def split3(v):
    high = v.astype(BF)
    rest = v - high.astype(F32)
    mid = rest.astype(BF)
    low = (rest - mid.astype(F32)).astype(BF)
    return jnp.concatenate([high, mid, low], axis=0)


def unsplit3(v):
    rows = v.shape[0] // 3
    return v[:rows] + v[rows : 2 * rows] + v[2 * rows :]


def build_bias(tb, rel, bias):
    sides = [split3(jnp.concatenate([tb[t, p] for t in range(4)], axis=0)) for p in range(2)]
    row = lax.broadcasted_iota(jnp.int32, (256, 64), 0)

    def keys(block, carry):
        eight = pl.ds(pl.multiple_of(block * 8, 8), 8)
        named = rel[eight, 0:64]
        both = []
        for k in range(8):
            hot = (row == named[k : k + 1]).astype(F32).astype(BF)
            both.append(jnp.concatenate([unsplit3(mul(side, hot)) for side in sides], axis=1))
        for t in range(4):
            for layer in range(2):
                for m in range(2):
                    n = t * 8 + layer * 2 + m
                    at = (t % 2) * 256 + m * 128
                    bias[layer, t // 2, eight, at : at + 128] = rows_of([one[n : n + 1] for one in both])
        return carry

    lax.fori_loop(0, 7, keys, 0)
    unused = lax.broadcasted_iota(jnp.int32, (16, 512), 0) >= 1
    for layer in range(2):
        for g in range(2):
            bias[layer, g, 48:64] = jnp.where(unused, F32(-1e30), bias[layer, g, 48:64])


def table_sums(gbias, rel, tab):
    row = lax.broadcasted_iota(jnp.int32, (512, 128), 0)
    lane = lax.broadcasted_iota(jnp.int32, (512, 128), 1)
    side = row // 256 == lane // 64
    named_row = jnp.where(side, row % 256, -2)
    none = jnp.zeros((4, 128), F32)

    def keys(block, total):
        eight = pl.ds(pl.multiple_of(block * 8, 8), 8)
        named = rel[eight, :]
        parts = {}
        for t in range(4):
            for layer in range(2):
                for m in range(2):
                    at = (t % 2) * 256 + m * 128
                    parts[t, layer, m] = gbias[layer, t // 2, eight, at : at + 128]
        for k in range(8):
            hot = (named_row == named[k : k + 1]).astype(F32).astype(BF)
            rows = []
            for t in range(4):
                rows += [parts[t, layer, m][k : k + 1] for layer in range(2) for m in range(2)] + [none]
            total = total + unsplit3(mul(split3(rows_of(rows)), hot, NT))
        return total

    total = lax.fori_loop(0, 7, keys, jnp.zeros((32, 512), F32))
    for t in range(4):
        tab[t % 2, t // 2] = total[t * 8 : t * 8 + 8]


class Sums:
    def __init__(self, copy, at, phases):
        self.stages = []
        sent = []

        def start(axis, size, part, landing):
            mine = at[axis]
            landing[mine] = (part(mine) if callable(part) else part)[...]
            for step in range(1, size):
                src = part((mine + step) % size) if callable(part) else landing.at[mine]
                sent.append(copy(src, landing.at[mine], axis, step))

        def end(size, landing, keep):
            while sent:
                sent.pop().wait_recv()
            total = landing[0]
            for k in range(1, size):
                total = total + landing[k]
            keep(total)

        for n, (axis, size, part, landing, keep) in enumerate(phases):
            before = phases[n - 1] if n else None

            def stage(axis=axis, size=size, part=part, landing=landing, before=before):
                if before:
                    end(before[1], before[3], before[4])
                start(axis, size, part, landing)

            self.stages.append(stage)
        last = phases[-1]
        self.stages.append(lambda: end(last[1], last[3], last[4]))


FAMILIES = ((ORDERS[0], 128), (ORDERS[1], 128), (ORDERS[2], 256), (ORDERS[1], 512), (ORDERS[2], 512))


def scratch_list():
    one = (4, 4, 4, 16)
    shapes = {
        **{f"ga{k}": pltpu.VMEM((2, 2, 4, 4, 4, 16, 128), BF) for k in range(4)},
        "wb": pltpu.VMEM((2, 4, 2, 4, 16, 512), BF),
        "wc": pltpu.VMEM((2, 4, 4, 2, 16, 512), BF),
        "x1": pltpu.VMEM((ROWS, WIDTH), F32),
        "wp": pltpu.VMEM((2, WIDTH, WIDTH), BF),
        "bias": pltpu.VMEM((2, 2, 64, 512), F32),
        "mask": pltpu.VMEM((4, 64, 512), F32),
        "rel": pltpu.VMEM((128, 128), jnp.int32),
        "maps": pltpu.VMEM((2, 2, 512, 400), BF),
        "pack": pltpu.VMEM((4, 64, 256), BF),
        "gbias": pltpu.VMEM((2, 2, 64, 512), F32),
        "vecs": pltpu.VMEM((8, WIDTH), F32),
        "vec": pltpu.VMEM((8, WIDTH), F32),
        "gd": pltpu.VMEM((2, 4, 4, 4, 8, 128), F32),
        "tb": pltpu.VMEM((4, 2, 8, 256), F32),
        "tab": pltpu.VMEM((2, 2, 8, 512), F32),
        "vec_sum": pltpu.VMEM((8, 128), F32),
        "vec_land": pltpu.VMEM((4, 4, 8, 128), F32),
        "tab_pair": pltpu.VMEM((2, 8, 512), F32),
        "tab_sum": pltpu.VMEM((8, 512), F32),
        "tab_cross": pltpu.VMEM((2, 2, 8, 512), F32),
        "tab_land": pltpu.VMEM((3, 4, 8, 512), F32),
        "feeds": pltpu.SemaphoreType.DMA((4,)),
        "send": pltpu.SemaphoreType.DMA((COPIES,)),
        "recv": pltpu.SemaphoreType.DMA((COPIES,)),
        "local": pltpu.SemaphoreType.DMA((12,)),
        "spills": pltpu.SemaphoreType.DMA((len(SPILLED),)),
        "cross_send": pltpu.SemaphoreType.DMA((8,)),
        "cross_recv": pltpu.SemaphoreType.DMA((8,)),
    }
    for k in range(3):
        width = FAMILIES[k][1]
        for layer in range(2):
            shapes[f"both{k}_{layer}"] = pltpu.VMEM((2,) + one + (width,), BF)
            for name, shape in landing_shapes(width).items():
                shapes[f"{name}{k}_{layer}"] = shape
    for k in (3, 4):
        for layer in range(2):
            shapes[f"sums{k}_{layer}"] = pltpu.VMEM(one + (512,), BF)
        for name, shape in landing_shapes(512).items():
            shapes[f"{name}{k}"] = shape
    shapes.update(Scratch.shapes)
    return shapes


def prepare_mask(region, maps, mask):
    named = lax.broadcasted_iota(jnp.int32, (128, 400), 0)
    row = jnp.concatenate([region[...], jnp.full((1, 204), -1, jnp.int32)], axis=1)
    hot = (named == row).astype(F32).astype(BF)
    places = mul(maps[0, 0, 0:256, :], hot, NT).astype(BF)
    for w in range(4):
        one = places[w * 64 : w * 64 + 64]
        off = (mul(one, one, NT) - 1.0) * 1e9
        off = jnp.concatenate([off, off], axis=1)
        mask[w] = jnp.concatenate([off] * 4, axis=1)


def place_vectors(ln_gain, ln_shift, lane):
    eight = jnp.concatenate([ln_gain[0], ln_gain[1], ln_shift[0], ln_shift[1]], axis=0)
    at = lax.broadcasted_iota(jnp.int32, (8, 128), 1) - lane
    out = jnp.zeros((8, 128), F32)
    for e in range(4):
        out = jnp.where(at == e, eight[:, e : e + 1], out)
    return out


def core_kernel(x, cot, w_qkv, w_proj, b, c, ln_gain, ln_shift, tables, region, rel_index,
                out, g, o_qkv, o_proj, ob, oc, o_gain, o_shift, o_tables, gb, gc, *rest):
    far, rest = dict(zip(SPILLED, rest[: len(SPILLED)])), rest[len(SPILLED) :]
    r = dict(zip(scratch_list(), rest))
    at = coords()
    core = at["c"]
    s = Scratch({name: r[name] for name in Scratch.shapes}, far, r["spills"])
    ga, wp, gd, tb, local, vec = [r[f"ga{k}"] for k in range(4)], r["wp"], r["gd"], r["tb"], r["local"], r["vec"]
    feed = Feed(core, gb, gc, r["wb"], r["wc"], r["feeds"])
    copy = Copier(at, r["send"], r["recv"])
    own = []

    def place(src, dst):
        put = pltpu.make_async_copy(src, dst, local.at[len(own)])
        put.start()
        own.append(put)

    wholes = [[w.at[layer] for w in ga + [gb, gc]] for layer in range(2)]
    orders = (ORDERS[0], ORDERS[1], ORDERS[2], ORDERS[0], ORDERS[1], ORDERS[2])
    for layer in range(2):
        for order, src, whole in zip(orders[4:], (b, c), wholes[layer][4:]):
            i1, i2, i3 = (at[axis] for axis in order)
            place(src.at[layer], whole.at[core, i3, i2, i1])
        for k in range(4):
            i1, i2, i3 = (at[axis] for axis in orders[k])
            if k < 3:
                tile = w_qkv[layer, k]
            else:
                four = w_proj[layer].astype(F32)
                tile = rows_of([four[n // 4 : n // 4 + 1, n % 4 * 128 : n % 4 * 128 + 128] for n in range(16)])
            ga[k][layer, core, i3, i2, i1] = tile.astype(BF)
    start = pltpu.make_async_copy(cot, g, local.at[8])
    start.start()
    lane = 4 * ((at["x"] * 2 + at["z"] % 2) * 4 + (at["z"] // 2) * 2 + core)
    gd[core, at["z"], at["y"], at["x"]] = place_vectors(ln_gain, ln_shift, lane)
    mine = (at["z"] // 2) * 2 + core
    rel = r["rel"]
    rel[...] = jnp.full(rel.shape, -1, jnp.int32)
    rel[0:49, 0:49] = rel_index[...]
    turned = rel[...].T
    rel[...] = jnp.full(rel.shape, -1, jnp.int32)
    rel[0:64, 0:64] = turned[0:64, 0:64]
    rel[0:64, 64:128] = turned[0:64, 0:64]
    tb[mine] = jnp.zeros((2, 8, 256), F32)
    for layer in range(2):
        for k in range(4):
            tb[mine, k % 2, layer * 2 + k // 2 : layer * 2 + k // 2 + 1, 0:169] = tables[layer, k : k + 1, :]
    enter(at, PEERS)
    for put in own:
        put.wait()
    def some(layer, ks, ring=0):
        return Gather(copy, at, [(orders[k], wholes[layer][k]) for k in ks], ring).stages

    early, mid, late = some(0, (0, 1, 2)), some(0, (3,)), some(0, (4, 5), 1)
    next_early, next_late = some(1, (0, 1, 2, 3), 1), some(1, (4, 5), 2)
    small = {}

    def small_start(axis, ref):
        steps = (1,) if axis == "c" else (1, 2, 3)
        small[axis] = [copy(ref, ref, axis, step) for step in steps]

    def small_end(axis):
        for one in small[axis]:
            one.wait_recv()

    early[0]()
    small_start("x", gd.at[core, at["z"], at["y"], at["x"]])
    pair = copy(tb.at[mine], tb.at[mine], "z", 2)
    for one in (mid, late, next_early, next_late):
        one[0]()
    maps, pack = r["maps"], r["pack"]
    window_maps(maps)
    proj_maps(pack)
    prepare_mask(region, maps, r["mask"])
    r["gbias"][...] = jnp.zeros(r["gbias"].shape, F32)
    early[1]()
    late[1]()
    mid[1]()
    small_end("x")
    small_start("y", gd.at[core, at["z"], at["y"]])
    pair.wait_recv()
    other = (mine + 2) % 4
    across = [copy(tb.at[k], tb.at[k], "c", 1) for k in (mine, other)]
    early[2]()
    small_end("y")
    small_start("z", gd.at[core, at["z"]])
    late[2]()
    mid[2]()
    next_early[1]()
    next_late[1]()
    for one in across:
        one.wait_recv()
    build_bias(tb, rel, r["bias"])
    small_end("z")
    small_start("c", gd.at[core])
    early[3]()
    next_late[2]()
    small_end("c")
    vecs = r["vecs"]
    for y in range(4):
        total = gd[0, 0, y, 0]
        for n in range(1, 32):
            total = total + gd[n // 16, n // 4 % 4, y, n % 4]
        vecs[:, y * 128 : y * 128 + 128] = total
    early[4]()
    next_early[2]()
    gain = [[vecs[l * 2 + k : l * 2 + k + 1] for k in range(2)] for l in range(2)]
    shift = [[vecs[4 + l * 2 + k : 5 + l * 2 + k] for k in range(2)] for l in range(2)]
    start.wait()

    def unpack_proj(layer):
        for block in range(8):
            tiles = []
            for n in range(16):
                tiles.append(ga[3][(layer,) + slot_of(0, block * 16 + n)])
            tiles = rows_of(tiles)
            for q in range(4):
                wp[layer, block * 64 : block * 64 + 64, q * 128 : q * 128 + 128] = mul(pack[q], tiles).astype(BF)

    forward_plans = (
        {
            "qkv": [mid[3], late[3], next_late[3]],
            "half_scores": [next_early[3]],
            "scores": [mid[4], lambda: unpack_proj(0)],
            "feed_forward": [late[4], late[5]],
            "chunks": [next_early[4], next_late[4]],
            "end": [next_early[5], lambda: unpack_proj(1)],
        },
        {"feed_forward": [next_late[5], next_late[6]]},
    )
    x1 = r["x1"]
    for layer, before, after in ((0, x, x1), (1, x1, out)):

        def reached(name, plan=forward_plans[layer]):
            for one in plan.get(name, ()):
                one()

        forward(layer, before, after, gain, shift, ga, feed, wp, maps, r["bias"], r["mask"], s, reached)

    def chunk_part(ref, k, n):
        z = pl.ds(2 * (n % 2), 2)
        return ref.at[:, z] if k == 3 else ref.at[:, :, z]

    def chunk_over(k, n):
        sem = (k - 3) * 4 + n
        return pltpu.make_async_remote_copy(
            src_ref=(s.stage_b if k == 3 else s.stage_c).at[n % 2],
            dst_ref=chunk_part(r[f"landed{k}"], k, n),
            send_sem=r["cross_send"].at[sem],
            recv_sem=r["cross_recv"].at[sem],
            device_id=moved(at, "c", 1),
            device_id_type=MESH,
        )

    def chunk_here(layer, k, n):
        src = (s.stage_b if k == 3 else s.stage_c).at[n % 2]
        return pltpu.make_async_copy(
            src, chunk_part(r[f"sums{k}_{layer}"], k, n), r["cross_send"].at[(k - 3) * 4 + n]
        )

    def grads_of(layer):
        first = 0 if layer else 2

        def away(n):
            return jnp.logical_and(n >= first, n < first + 2)

        def send_grads(n):
            for k in (3, 4):
                pl.when(away(n))(lambda k=k: chunk_over(k, n).start())
                pl.when(jnp.logical_not(away(n)))(lambda k=k: chunk_here(layer, k, n).start())

        def wait_grads(n):
            for k in (3, 4):
                pl.when(away(n))(lambda k=k: chunk_over(k, n).wait_send())
                pl.when(jnp.logical_not(away(n)))(lambda k=k: chunk_here(layer, k, n).wait())

        def arrived(k):
            for n in (first, first + 1):
                chunk_over(k, n).wait_recv()

        return send_grads, wait_grads, arrived

    def out_of(ref, layer, lanes):
        def put(total):
            ref[layer, :, lanes] = total

        return put

    def feed_forward_scatter(layer):
        families = []
        for k, ref in ((3, ob), (4, oc)):
            family = {name: r[f"{name}{k}"] for name in landing_shapes(512)}
            family.update(order=FAMILIES[k][0], sums=r[f"sums{k}_{layer}"], out=out_of(ref, layer, slice(0, 512)))
            families.append(family)
        arrived = grads_of(layer)[2]
        return Scatter(copy, at, families, lambda n: arrived(n + 3))

    def heads_out(layer, k):
        def put(total):
            o_qkv[layer, k] = total[:, 0:128]
            if k == 2:
                for n in range(16):
                    lanes = slice(n % 4 * 128, n % 4 * 128 + 128)
                    o_proj[layer, n // 4 : n // 4 + 1, lanes] = total[n : n + 1, 128:256]

        return put

    def heads_scatter(layer):
        families, crossing = [], []
        for k in range(3):
            family = {name: r[f"{name}{k}_{layer}"] for name in landing_shapes(128)}
            both = r[f"both{k}_{layer}"]
            family.update(order=FAMILIES[k][0], sums=both.at[core], out=heads_out(layer, k))
            families.append(family)

        def cross(k):
            crossing.append(copy(r[f"both{k}_{layer}"].at[1 - core], r[f"landed{k}_{layer}"], "c", 1))

        return Scatter(copy, at, families, lambda n: crossing[n].wait_recv()), cross

    wide = {layer: feed_forward_scatter(layer) for layer in (0, 1)}
    heads = {layer: heads_scatter(layer) for layer in (0, 1)}
    tab, tab_pair, tab_sum, vec_sum = r["tab"], r["tab_pair"], r["tab_sum"], r["vec_sum"]
    vec_land, tab_cross, tab_land = r["vec_land"], r["tab_cross"], r["tab_land"]

    def keep_in(ref):
        def keep(total):
            ref[...] = total

        return keep

    def keep_vectors(total):
        lanes = lax.broadcasted_iota(jnp.int32, (8, 128), 1) - lane
        four = jnp.concatenate(
            [jnp.sum(jnp.where(lanes == e, total, 0.0), axis=1, keepdims=True) for e in range(4)], axis=1
        )
        for layer in range(2):
            o_gain[layer] = four[layer * 2 : layer * 2 + 2]
            o_shift[layer] = four[layer * 2 + 4 : layer * 2 + 6]

    def keep_tables(total):
        for layer in range(2):
            for k in range(4):
                row = layer * 2 + k // 2
                o_tables[layer, k : k + 1, :] = total[row : row + 1, k % 2 * 256 : k % 2 * 256 + 169]

    vec_sums = Sums(
        copy,
        at,
        [
            ("y", 4, lambda j: vec.at[:, pl.ds(pl.multiple_of(j * 128, 128), 128)], vec_land.at[0], keep_in(vec_sum)),
            ("x", 4, vec_sum, vec_land.at[1], keep_in(vec_sum)),
            ("z", 4, vec_sum, vec_land.at[2], keep_in(vec_sum)),
            ("c", 2, vec_sum, vec_land.at[3], keep_vectors),
        ],
    )
    tab_sums = Sums(
        copy,
        at,
        [
            ("c", 2, lambda j: tab.at[j], tab_cross, keep_in(tab_pair)),
            ("z", 4, lambda j: tab_pair.at[j // 2], tab_land.at[0], keep_in(tab_sum)),
            ("x", 4, tab_sum, tab_land.at[1], keep_in(tab_sum)),
            ("y", 4, tab_sum, tab_land.at[2], keep_tables),
        ],
    )

    def tables_done():
        table_sums(r["gbias"], rel, tab)

    def stage(sums, n):
        return lambda: sums.stages[n]()

    high_wide, low_wide, high_heads, low_heads = wide[1], wide[0], heads[1][0], heads[0][0]
    plans = {
        1: {
            "feed_forward": [stage(high_wide, 0)],
            "half_scores": [stage(high_wide, 1)],
            "end": [stage(high_wide, 2)],
        },
        0: {
            "chunks": [stage(high_wide, 3), stage(high_heads, 0)],
            "feed_forward": [stage(high_heads, 1), stage(low_wide, 0), stage(high_wide, 4)],
            "half_scores": [stage(high_heads, 2), stage(low_wide, 1)],
            "scores": [stage(high_heads, 3)],
            "qkv": [stage(low_wide, 2), stage(high_heads, 4)],
            "gn1": [stage(low_heads, 0)],
            "end": [
                stage(vec_sums, 0),
                tables_done,
                stage(tab_sums, 0),
                stage(low_heads, 1),
                stage(tab_sums, 1),
                stage(vec_sums, 1),
                stage(low_wide, 3),
                stage(low_heads, 2),
                stage(tab_sums, 2),
                stage(vec_sums, 2),
                stage(low_wide, 4),
                stage(low_heads, 3),
                stage(tab_sums, 3),
                stage(vec_sums, 3),
                stage(low_heads, 4),
                stage(tab_sums, 4),
                stage(vec_sums, 4),
            ],
        },
    }
    for layer, before in ((1, x1), (0, x)):

        def poll(name, plan=plans[layer]):
            for one in plan.get(name, ()):
                one()

        send, wait, _ = grads_of(layer)
        backward_mlp(layer, g, gain, feed, s, vec, send, wait, poll)
        backward_heads(
            layer, before, g, gain, ga, wp, maps, pack, r["gbias"], s, vec,
            [r[f"both{k}_{layer}"] for k in range(3)], poll, heads[layer][1],
        )
    copy.finish()


def hand_over_kernel(*refs):
    sems = refs[-1]
    count = len(refs) // 2
    copies = [pltpu.make_async_copy(refs[n], refs[count + n], sems.at[n]) for n in range(count)]
    for one in copies:
        one.start()
    for one in copies:
        one.wait()


def hand_over(arrays):
    far, vmem = pl.BlockSpec(memory_space=pl.ANY), pl.BlockSpec(memory_space=pltpu.VMEM)
    return pl.pallas_call(
        hand_over_kernel,
        out_shape=[jax.ShapeDtypeStruct(one.shape, one.dtype) for one in arrays],
        in_specs=[vmem] * len(arrays),
        out_specs=[far] * len(arrays),
        scratch_shapes=[pltpu.SemaphoreType.DMA((len(arrays),))],
        compiler_params=pltpu.CompilerParams(vmem_limit_bytes=63 * 2**20),
        name="hand_over",
    )(*arrays)


def shards(
    inputs, w_qkv, w_proj, w_up, w_down, ln_gain, ln_shift, tables, region, rel_index, cotangent
):
    w_qkv, tables = w_qkv.transpose(0, 2, 1, 3), tables.transpose(0, 2, 1)
    tiles = jax.ShapeDtypeStruct((2, 2, 4, 4, 4, 16, 512), BF)
    rows = jax.ShapeDtypeStruct((ROWS, WIDTH), F32)
    vmem, far = pl.BlockSpec(memory_space=pltpu.VMEM), pl.BlockSpec(memory_space=pl.ANY)
    spills = [jax.ShapeDtypeStruct(Scratch.shapes[name].shape, Scratch.shapes[name].dtype) for name in SPILLED]
    grads = [
        jax.ShapeDtypeStruct(one.shape, F32) for one in (w_qkv, w_proj, w_up, w_down, ln_gain, ln_shift, tables)
    ]
    outs = pl.pallas_call(
        core_kernel,
        out_shape=[rows, rows] + grads + [tiles, tiles] + spills,
        in_specs=[vmem, far, vmem, vmem, far, far] + [vmem] * 5,
        out_specs=[vmem] * 9 + [far] * (2 + len(spills)),
        scratch_shapes=list(scratch_list().values()),
        compiler_params=pltpu.CompilerParams(
            vmem_limit_bytes=63 * 2**20, collective_id=0, has_side_effects=True
        ),
        name="both_blocks",
    )(
        inputs, cotangent, w_qkv, w_proj, w_up, w_down, ln_gain, ln_shift, tables, region.reshape(1, -1), rel_index
    )
    out, g, o_qkv, o_proj, ob, oc, o_gain, o_shift, o_tables = hand_over(outs[:9])
    return out, g, o_qkv.transpose(0, 2, 1, 3), o_proj, ob, oc, o_gain, o_shift, o_tables.transpose(0, 2, 1)


def solution(mesh):
    return jax.shard_map(
        shards,
        mesh=mesh,
        in_specs=(
            P(("dp", "tensor"), None),
            P(None, "dp", None, "tensor"),
            P(None, ("tensor", "dp"), None),
            P(None, "dp", "tensor"),
            P(None, ("tensor", "dp"), None),
            P(None, None, ("dp", "tensor")),
            P(None, None, ("dp", "tensor")),
            P(None, None, "tensor"),
            P(),
            P(),
            P(("dp", "tensor"), None),
        ),
        out_specs=(
            P(("dp", "tensor"), None),
            P(("dp", "tensor"), None),
            P(None, "dp", None, "tensor"),
            P(None, ("tensor", "dp"), None),
            P(None, "dp", "tensor"),
            P(None, ("tensor", "dp"), None),
            P(None, None, ("dp", "tensor")),
            P(None, None, ("dp", "tensor")),
            P(None, None, "tensor"),
        ),
        check_vma=False,
    )
```
